128 devices in a mesh: gx: 8 (over x, core), gy: 16 (over z, y).
Axes of the slice: x: 4, y: 4, z: 4, core: 2. Of those that a mesh axis runs over, the one named last changes fastest.
Arguments:
- image: float32 [128, 256, 256], P('gx', 'gy'), may hold values from -6 to 6
- conduct: float32 [128, 256, 256], P('gx', 'gy'), may hold values from 4 to 400
Outputs:
- blurred: float32 [128, 256, 256], P('gx', 'gy')
The draws below stay inside these ranges and needn't reach their ends.
All inputs are finite; a program needn't handle non-finite values.
Results may differ from the reference program's by a relative error of at most 0.0003.
Values sent between devices are 32-bit elements; how exact they have to be, the bound alone decides.
A program may use at most 192 MiB of HBM per device.

```python
import math
import jax
import jax.numpy as jnp

NZ = 256
COARSE_SWEEPS = 8
NX = 128
NY = 256


def levels(key, extent, shards, least, top_value):
    gain = 1.0
    for position, blocks in shards:
        heights = jax.random.uniform(jax.random.fold_in(jax.random.fold_in(key, 6), position), (blocks,), jnp.float32, least / len(shards), top_value / len(shards))
        gain = gain * jnp.repeat(jnp.exp(heights), extent[position] // blocks).reshape((-1,) + (1,) * (len(extent) - 1 - position))
    return gain


def gaussian(rng, shape, spread, reach, pieces=(), kind=jnp.bfloat16):
    gain = levels(rng, shape, pieces, -0.22, 0.18) if pieces else 1.0
    drawn = jax.random.normal(rng, shape, jnp.float32) * spread * gain
    return jnp.minimum(jnp.maximum(drawn, -reach), reach).astype(kind)


def setup_inputs(seed: int = 0) -> dict:
    streams_of = jax.random.split(jax.random.key(seed), 3)
    return {
        "image": gaussian(streams_of[0], (NX, NY, NZ), 1.0, 6.0, ((0, 8), (1, 16)), jnp.float32),
        "conduct": jnp.clip(jnp.exp(math.log(400.0) - 4.6051702 * jax.random.uniform(streams_of[1], (NX, NY, NZ), jnp.float32) ** levels(streams_of[1], (NX, NY, NZ), ((0, 8), (1, 16)), -0.2, 0.2)), 4.0, 400.0),
    }


def coarsen(values):
    size_x, size_y, size_z = values.shape
    blocks = values.reshape(size_x // 2, 2, size_y // 2, 2, size_z // 2, 2)
    return blocks.sum(axis=(1, 3, 5)) * 0.125


def refine(values):
    return jnp.repeat(jnp.repeat(jnp.repeat(values, 2, 0), 2, 1), 2, 2)


def shift_up(values):
    return jnp.pad(values[:, :, 1:], ((0, 0), (0, 0), (0, 1)))


def shift_down(values):
    return jnp.pad(values[:, :, :-1], ((0, 0), (0, 0), (1, 0)))


def neighbour_sums(values, conductance, inside, weight_scale):
    cond_mid = conductance[1:-1, 1:-1]
    mid_inside = inside[1:-1, 1:-1]
    weighted = jnp.zeros(cond_mid.shape, jnp.float32)
    total_weight = jnp.zeros(cond_mid.shape, jnp.float32)
    windows = [(slice(2, None), slice(1, -1)), (slice(None, -2), slice(1, -1)),
               (slice(1, -1), slice(2, None)), (slice(1, -1), slice(None, -2))]
    for window in windows:
        coupling = mid_inside * inside[window] * (cond_mid + conductance[window]) * weight_scale
        weighted = weighted + coupling * values[window]
        total_weight = total_weight + coupling
    vals_mid = values[1:-1, 1:-1]
    for mover in (shift_up, shift_down):
        coupling = mid_inside * mover(mid_inside) * (cond_mid + mover(cond_mid)) * weight_scale
        weighted = weighted + coupling * mover(vals_mid)
        total_weight = total_weight + coupling
    return weighted, total_weight


def half_sweep(values, source, conductance, inside, row_ids, col_ids, parity, weight_scale):
    weighted, total_weight = neighbour_sums(values, conductance, inside, weight_scale)
    update = (source + weighted) / (1.0 + total_weight)
    depth_ids = jnp.arange(values.shape[2], dtype=jnp.int32)
    colour = (row_ids[:, None, None] + col_ids[None, :, None] + depth_ids[None, None, :]) % 2
    return jnp.where(colour == parity, update, values[1:-1, 1:-1])


def pad_plane(values):
    return jnp.pad(values, ((1, 1), (1, 1), (0, 0)))


def smooth_whole(estimate, source, conductance, weight_scale, repeats):
    cond_pad = pad_plane(conductance)
    inside = pad_plane(jnp.ones(conductance.shape, jnp.float32))
    row_ids = jnp.arange(conductance.shape[0], dtype=jnp.int32)
    col_ids = jnp.arange(conductance.shape[1], dtype=jnp.int32)
    for repeat in range(repeats):
        estimate = half_sweep(pad_plane(estimate), source, cond_pad, inside, row_ids, col_ids, 0, weight_scale)
        estimate = half_sweep(pad_plane(estimate), source, cond_pad, inside, row_ids, col_ids, 1, weight_scale)
    return estimate


def residual_whole(estimate, source, conductance, weight_scale):
    inside = pad_plane(jnp.ones(conductance.shape, jnp.float32))
    weighted, total_weight = neighbour_sums(pad_plane(estimate), pad_plane(conductance), inside, weight_scale)
    return source - ((1.0 + total_weight) * estimate - weighted)


def reference(image, conduct):
    scales = [0.5 / 4.0 ** grid_level for grid_level in range(4)]
    conductances = [conduct]
    for grid_level in range(3):
        conductances.append(coarsen(conductances[-1]))
    estimate = image
    source = image
    saved = []
    for grid_level in range(3):
        estimate = smooth_whole(estimate, source, conductances[grid_level], scales[grid_level], 2)
        saved.append((estimate, source))
        source = coarsen(residual_whole(estimate, source, conductances[grid_level], scales[grid_level]))
        estimate = jnp.zeros(source.shape, jnp.float32)
    estimate = smooth_whole(estimate, source, conductances[3], scales[3], COARSE_SWEEPS)
    for grid_level in (2, 1, 0):
        kept, source = saved[grid_level]
        estimate = kept + refine(estimate)
        estimate = smooth_whole(estimate, source, conductances[grid_level], scales[grid_level], 2)
    return estimate
```

```python
import jax
import jax.numpy as jnp
from jax import lax
from jax.experimental import pallas as pl
from jax.experimental.pallas import tpu as pltpu
from jax.sharding import PartitionSpec as P

COARSE_SWEEPS = 8
MESH = pl.DeviceIdType.MESH
F32 = jnp.float32
GX, GY = 8, 16
DIRECTIONS = [(-1, 0), (1, 0), (0, -1), (0, 1), (-1, -1), (-1, 1), (1, -1), (1, 1)]
CHIPS = sorted(
    [(x, y, z) for x in range(4) for y in range(4) for z in range(4) if (x, y, z) != (0, 0, 0)],
    key=lambda d: -sum(min(c, 4 - c) for c in d),
)


def iota(shape, dim):
    return lax.broadcasted_iota(jnp.int32, shape, dim)


def roll(values, shift):
    return pltpu.roll(values, shift % 128, values.ndim - 1)


def halo_copies(refs, width, extent, origin, sems, position):
    src, src_origin, dst = refs
    gx, gy = position
    copies = []
    for index, (dx, dy) in enumerate(DIRECTIONS):
        src_at, dst_at = [], []
        for step, size, here, there in zip((dx, dy), extent, src_origin, origin):
            if step == 0:
                src_at.append(slice(here, here + size))
                dst_at.append(slice(there, there + size))
            elif step > 0:
                src_at.append(slice(here + size - width, here + size))
                dst_at.append(slice(there - width, there))
            else:
                src_at.append(slice(here, here + width))
                dst_at.append(slice(there + size, there + size + width))
        lead = (slice(None),) * (len(dst.shape) - 3)
        copies.append(
            pltpu.make_async_remote_copy(
                src_ref=src.at[lead + tuple(src_at)],
                dst_ref=dst.at[lead + tuple(dst_at)],
                send_sem=sems.at[0, index],
                recv_sem=sems.at[1, index],
                device_id=(lax.rem(gx + dx + GX, GX), lax.rem(gy + dy + GY, GY)),
                device_id_type=MESH,
            )
        )
    return copies


def kernel(
    image, conduct, out,
    kx, vx, vs, vk, c0, s0, d0, t0, p0,
    k1, s1x, v1, vk1, c1, s1, i1, d1, t1, p1,
    own2, part2, mix2, kg, sg, v2, c2, s2, i2, d2, t2, p2,
    k3, v3, c3, s3, i3, dummy,
    halo_sems, pair_sems,
):
    gx, gy = lax.axis_index("gx"), lax.axis_index("gy")
    chip_x, core = gx // 2, lax.rem(gx, 2)
    chip_z, chip_y = gy // 4, lax.rem(gy, 4)
    sibling = (chip_x * 2 + 1 - core, gy)
    chips = [
        (lax.rem(chip_x + x, 4) * 2 + core, lax.rem(chip_z + z, 4) * 4 + lax.rem(chip_y + y, 4))
        for x, y, z in CHIPS
    ]
    position = (gx, gy)

    barrier = pltpu.get_barrier_semaphore()
    greeted = chips + [
        (lax.rem(gx + dx + GX, GX), lax.rem(gy + dy + GY, GY)) for dx, dy in DIRECTIONS if dx
    ]
    for peer in greeted:
        pl.semaphore_signal(barrier, inc=1, device_id=peer, device_id_type=MESH)

    lane0 = iota((16, 128), 1)
    odd_row = iota((16, 128), 0) & 1
    low0 = lane0 < 64
    half_lane = (lane0 & 63) * 2

    def split(values, par):
        parity = odd_row ^ par
        first = half_lane + jnp.where(low0, parity, 1 - parity)
        second = half_lane + jnp.where(low0, 1 - parity, parity)
        left = jnp.take_along_axis(values[:, :128], first, axis=1)
        right = jnp.take_along_axis(values[:, 128:], second, axis=1)
        return jnp.where(low0, left, right), roll(jnp.where(low0, right, left), 64)

    def join(red, black, par):
        parity = odd_row ^ par
        turned = roll(black, 64)
        left, right = jnp.where(low0, red, turned), jnp.where(low0, turned, red)
        same = (lane0 & 1) == parity
        half = lane0 >> 1
        first = half + jnp.where(same, 0, 64)
        second = half + jnp.where(same, 64, 0)
        return jnp.take_along_axis(left, first, axis=1), jnp.take_along_axis(right, second, axis=1)

    for i in range(16):
        kx[0, i + 5, 8:24], kx[1, i + 5, 8:24] = split(conduct[i], i & 1)
    for i in range(16):
        red, black = split(image[i], i & 1)
        vx[0, i + 5, 8:24], vx[1, i + 5, 8:24] = red, black
        vs[0, i], vs[1, i] = red, black
    nothing = jnp.zeros((4, 4, 8, 128), F32)
    for ref in (kg, v2):
        ref[:, :, 0:8], ref[:, :, 72:80] = nothing, nothing
    v3[...] = jnp.zeros(v3.shape, F32)
    k3[...] = jnp.zeros(k3.shape, F32)

    pl.semaphore_wait(barrier, len(greeted))

    send_k = halo_copies((kx, (5, 8), kx), 5, (16, 16), (5, 8), halo_sems.at[0], position)
    send_v = halo_copies((vs, (0, 0), vx), 5, (16, 16), (5, 8), halo_sems.at[1], position)
    for copy in send_k + send_v:
        copy.start()

    def block_mean(block):
        for i in range(8):
            t0[i] = block(2 * i) + block(2 * i + 1)
        return [0.125 * (t0[i, pl.ds(0, 8, stride=2)] + t0[i, pl.ds(1, 8, stride=2)]) for i in range(8)]

    even_lane = (iota((8, 128), 1) & 63) * 2

    def block_mean_1(rows):
        for i in range(4):
            pair = rows[2 * i] + rows[2 * i + 1]
            t1[i] = jnp.take_along_axis(pair, even_lane, axis=1) + jnp.take_along_axis(pair, even_lane + 1, axis=1)
        for i in range(4):
            own2[i] = 0.125 * (t1[i, pl.ds(0, 4, stride=2)] + t1[i, pl.ds(1, 4, stride=2)])

    def pair_copy(src, dst, kind, step):
        return pltpu.make_async_remote_copy(
            src_ref=src, dst_ref=dst, send_sem=pair_sems.at[kind, step, 0], recv_sem=pair_sems.at[kind, step, 1],
            device_id=sibling, device_id_type=MESH,
        )

    def gather_copies(kind, whole):
        swap = pair_copy(own2.at[pl.ds(2 - 2 * core, 2)] if kind == 1 else mix2.at[pl.ds(2 - 2 * core, 2)], part2.at[kind], kind, 0)
        rows = (chip_x, pl.ds(2 * core, 2), pl.ds(8 + 4 * gy, 4))
        spread = [
            pltpu.make_async_remote_copy(
                src_ref=mix2.at[pl.ds(4 + 2 * kind, 2)], dst_ref=whole.at[rows], send_sem=pair_sems.at[kind, 1, 0],
                recv_sem=pair_sems.at[kind, 1, 1], device_id=chip, device_id_type=MESH,
            )
            for chip in chips
        ]
        half = whole.at[:, pl.ds(2 * core, 2), 8:72]
        share = pair_copy(half, half, kind, 2)
        return swap, spread, share

    def mix(kind, own_rows, whole):
        mine = iota((2, 4, 128), 2) // 64 == core
        chip_rows = jnp.where(mine, own_rows, part2[kind])
        mix2[4 + 2 * kind:6 + 2 * kind] = chip_rows
        whole[chip_x, pl.ds(2 * core, 2), pl.ds(8 + 4 * gy, 4)] = chip_rows

    def all_arrived(kind):
        pltpu.make_async_copy(dummy, dummy, pair_sems.at[kind, 1, 1]).wait()

    rows = block_mean(lambda i: kx[0, i + 5, 8:24] + kx[1, i + 5, 8:24])
    for i in range(8):
        k1[i + 7, 16:24] = rows[i]
    block_mean_1(rows)
    mix2[0:4] = own2[...]
    send_k1 = halo_copies((k1, (7, 16), k1), 6, (8, 8), (7, 16), halo_sems.at[2], position)
    swap_k, spread_k, share_k = gather_copies(0, kg)
    swap_k.start()
    for copy in send_k1:
        copy.start()

    shape = (2, 24, 128)
    sub, lanes = iota(shape, 1), iota(shape, 2)
    even_row = ((iota(shape, 0) + sub) & 1) == 0
    wy_low = jnp.where((sub == 4) & (gy == 0), 0.0, 0.5).astype(F32)
    wy_high = jnp.where((sub == 19) & (gy == GY - 1), 0.0, 0.5).astype(F32)
    wx_low = jnp.where(gx == 0, 0.0, 0.5).astype(F32)
    wx_high = jnp.where(gx == GX - 1, 0.0, 0.5).astype(F32)
    wz = [
        jnp.where(even_row, jnp.where(lanes == 0, 0.0, 0.5), jnp.where(lanes == 127, 0.0, 0.5)).astype(F32),
        jnp.where(even_row, jnp.where(lanes == 127, 0.0, 0.5), jnp.where(lanes == 0, 0.0, 0.5)).astype(F32),
    ]

    def beside(values, colour, rows_even):
        below, above = roll(values, 1), roll(values, -1)
        return jnp.where(rows_even, below, above) if colour == 0 else jnp.where(rows_even, above, below)

    row_index = iota((2, 1, 1), 0)

    def couplings_0(colour, start, stop):
        for i in range(start, stop, 2):
            e = i + 5
            here, other = kx[colour, e:e + 2, 4:28], kx[1 - colour, e:e + 2, 4:28]
            wx_l = jnp.where(row_index == 0, wx_low, 0.5) if i == 0 else 0.5
            wx_h = jnp.where(row_index == 1, wx_high, 0.5) if i == 14 else 0.5
            parts = [
                (here + kx[1 - colour, e - 1:e + 1, 4:28]) * wx_l,
                (here + kx[1 - colour, e + 1:e + 3, 4:28]) * wx_h,
                (here + kx[1 - colour, e:e + 2, 3:27]) * wy_low,
                (here + kx[1 - colour, e:e + 2, 5:29]) * wy_high,
                (here + other) * 0.5,
                (here + beside(other, colour, even_row)) * wz[colour],
            ]
            total = ((parts[0] + parts[1]) + (parts[2] + parts[3])) + ((parts[4] + parts[5]) + 1.0)
            inverse = 1.0 / total
            d0[colour, i + 4:i + 6] = total
            s0[colour, i + 4:i + 6] = inverse
            for n in range(6):
                c0[colour, n, i + 4:i + 6] = parts[n] * inverse

    def update_0(colour, i, lo, hi, rows_even):
        e, f = i + 5, i + 4
        a, b = lo + 8, hi + 8
        here = slice(lo + 4, hi + 4)
        other = vx[1 - colour, e:e + 2, a:b]
        acc0 = s0[colour, f:f + 2, here] + c0[colour, 0, f:f + 2, here] * vx[1 - colour, e - 1:e + 1, a:b]
        acc1 = c0[colour, 1, f:f + 2, here] * vx[1 - colour, e + 1:e + 3, a:b]
        acc1 += c0[colour, 2, f:f + 2, here] * vx[1 - colour, e:e + 2, a - 1:b - 1]
        acc2 = c0[colour, 3, f:f + 2, here] * vx[1 - colour, e:e + 2, a + 1:b + 1]
        acc2 += c0[colour, 4, f:f + 2, here] * other
        acc3 = c0[colour, 5, f:f + 2, here] * beside(other, colour, rows_even)
        return (acc0 + acc1) + (acc2 + acc3)

    own_even = ((iota((2, 16, 128), 0) + iota((2, 16, 128), 1)) & 1) == 0

    def half_sweep_0(colour, start, stop, lo=-4, hi=20):
        rows_even = even_row if hi - lo == 24 else own_even
        for i in range(start, stop, 2):
            vx[colour, i + 5:i + 7, lo + 8:hi + 8] = update_0(colour, i, lo, hi, rows_even)

    for copy in send_k:
        copy.wait_recv()
    couplings_0(0, -4, 20)
    couplings_0(1, -4, 20)

    swap_k.wait_recv()
    mix(0, mix2[pl.ds(2 * core, 2)], kg)
    for copy in spread_k:
        copy.start()

    for copy in send_v:
        copy.wait_recv()
    for colour in (0, 1):
        for i in range(-4, 20, 2):
            s0[colour, i + 4:i + 6] = s0[colour, i + 4:i + 6] * vx[colour, i + 5:i + 7, 4:28]

    half_sweep_0(0, -4, 20)
    half_sweep_0(1, -4, 20)
    half_sweep_0(0, -2, 18)
    half_sweep_0(1, -2, 18)

    def residual_0(i):
        total = None
        for colour in (0, 1):
            left = update_0(colour, i, 0, 16, own_even) - vx[colour, i + 5:i + 7, 8:24]
            left = d0[colour, i + 4:i + 6, 4:20] * left
            total = left if total is None else total + left
        return total

    for i in range(8):
        both = residual_0(2 * i)
        t0[i] = both[0] + both[1]
    for i in range(8):
        s1x[i + 7, 16:24] = 0.125 * (t0[i, pl.ds(0, 8, stride=2)] + t0[i, pl.ds(1, 8, stride=2)])
    send_s1 = halo_copies((s1x, (7, 16), s1x), 5, (8, 8), (7, 16), halo_sems.at[3], position)
    for copy in send_s1:
        copy.start()
    vk[5:21, 8:24] = vx[1, 5:21, 8:24]
    send_vk = halo_copies((vk, (5, 8), vk), 4, (16, 16), (5, 8), halo_sems.at[4], position)
    for copy in send_vk:
        copy.start()

    shape = (2, 24, 128)
    col, lanes = iota(shape, 1) - 6, iota(shape, 2)
    w1 = 0.5 / 4.0
    wy_low = jnp.where((col == 0) & (gy == 0), 0.0, w1).astype(F32)
    wy_high = jnp.where((col == 7) & (gy == GY - 1), 0.0, w1).astype(F32)
    wx_low = jnp.where(gx == 0, 0.0, w1).astype(F32)
    wx_high = jnp.where(gx == GX - 1, 0.0, w1).astype(F32)
    wz_low = jnp.where(lanes == 0, 0.0, w1).astype(F32)
    wz_high = jnp.where(lanes == 127, 0.0, w1).astype(F32)

    for copy in send_k1:
        copy.wait_recv()
    for i in range(-6, 14, 2):
        e, f = i + 7, i + 6
        here = k1[e:e + 2, 10:34]
        wx_l = jnp.where(row_index == 0, wx_low, w1) if i == 0 else w1
        wx_h = jnp.where(row_index == 1, wx_high, w1) if i == 6 else w1
        parts = [
            (here + k1[e - 1:e + 1, 10:34]) * wx_l,
            (here + k1[e + 1:e + 3, 10:34]) * wx_h,
            (here + k1[e:e + 2, 9:33]) * wy_low,
            (here + k1[e:e + 2, 11:35]) * wy_high,
            (here + roll(here, 1)) * wz_low,
            (here + roll(here, -1)) * wz_high,
        ]
        total = ((parts[0] + parts[1]) + (parts[2] + parts[3])) + ((parts[4] + parts[5]) + 1.0)
        inverse = 1.0 / total
        d1[f:f + 2] = total
        i1[f:f + 2] = inverse
        for n in range(6):
            c1[n, f:f + 2] = parts[n] * inverse

    def update_1(i, lo, hi):
        e, f = i + 7, i + 6
        a, b = lo + 16, hi + 16
        here = slice(lo + 6, hi + 6)
        mid = v1[e:e + 2, a:b]
        acc0 = s1[f:f + 2, here] + c1[0, f:f + 2, here] * v1[e - 1:e + 1, a:b]
        acc1 = c1[1, f:f + 2, here] * v1[e + 1:e + 3, a:b] + c1[2, f:f + 2, here] * v1[e:e + 2, a - 1:b - 1]
        acc2 = c1[3, f:f + 2, here] * v1[e:e + 2, a + 1:b + 1] + c1[4, f:f + 2, here] * roll(mid, 1)
        acc3 = c1[5, f:f + 2, here] * roll(mid, -1)
        return (acc0 + acc1) + (acc2 + acc3), mid

    def colour_1(size):
        box = (2, size, 128)
        return (iota(box, 0) + iota(box, 1) + iota(box, 2)) & 1

    colours_24, colours_16 = colour_1(24), colour_1(16)

    def half_sweep_1(colour, start, stop, lo, hi):
        colours = colours_24 if hi - lo == 24 else colours_16
        for i in range(start, stop, 2):
            new, old = update_1(i, lo, hi)
            v1[i + 7:i + 9, lo + 16:hi + 16] = jnp.where(colours == colour, new, old)

    lane = iota((64, 128), 1)
    place = lane & 63
    j_row = iota((64, 128), 0)
    low = lane < 64
    w2 = 0.5 / 16.0
    wy_low = jnp.where(j_row == 0, 0.0, w2).astype(F32)
    wy_high = jnp.where(j_row == 63, 0.0, w2).astype(F32)
    wz_low = jnp.where(place == 0, 0.0, w2).astype(F32)
    wz_high = jnp.where(place == 63, 0.0, w2).astype(F32)
    first_x = jnp.where(low, 0.0, w2).astype(F32)
    last_x = jnp.where(low, w2, 0.0).astype(F32)

    def row_before(ref, x, i, last, at, first_half):
        if i > 0:
            return ref[x, i - 1, at]
        return roll(jnp.where(first_half, ref[x, last, at], ref[(x + 3) % 4, last, at]), 64)

    def row_after(ref, x, i, last, at, first_half):
        if i < last:
            return ref[x, i + 1, at]
        return roll(jnp.where(first_half, ref[(x + 1) % 4, 0, at], ref[x, 0, at]), 64)

    all_arrived(0)
    share_k.start()
    share_k.wait_recv()
    at = slice(8, 72)
    for x in range(4):
        for i in range(4):
            here = kg[x, i, at]
            parts = [
                (here + row_before(kg, x, i, 3, at, low)) * (first_x if x == 0 and i == 0 else w2),
                (here + row_after(kg, x, i, 3, at, low)) * (last_x if x == 3 and i == 3 else w2),
                (here + kg[x, i, 7:71]) * wy_low,
                (here + kg[x, i, 9:73]) * wy_high,
                (here + roll(here, 1)) * wz_low,
                (here + roll(here, -1)) * wz_high,
            ]
            total = ((parts[0] + parts[1]) + (parts[2] + parts[3])) + ((parts[4] + parts[5]) + 1.0)
            inverse = 1.0 / total
            d2[x, i] = total
            i2[x, i] = inverse
            for n in range(6):
                c2[n, x, i, at] = parts[n] * inverse

    even_place = (lane & 1) == 0

    def pair_lanes(values):
        return values + jnp.where(even_place, roll(values, -1), roll(values, 1))

    def block_mean_2(x, i):
        return 0.125 * (t2[x, i, pl.ds(0, 32, stride=2)] + t2[x, i, pl.ds(1, 32, stride=2)])

    for x in range(4):
        for i in range(2):
            t2[x, i] = pair_lanes(kg[x, 2 * i, at] + kg[x, 2 * i + 1, at])
    for x in range(4):
        for i in range(2):
            k3[x, i, 8:40] = block_mean_2(x, i)
    lane3 = iota((32, 128), 1)
    place3 = (lane3 & 63) >> 1
    row3 = iota((32, 128), 0)
    low3 = lane3 < 64
    w3 = 0.5 / 64.0
    wy_low = jnp.where(row3 == 0, 0.0, w3).astype(F32)
    wy_high = jnp.where(row3 == 31, 0.0, w3).astype(F32)
    wz_low = jnp.where(place3 == 0, 0.0, w3).astype(F32)
    wz_high = jnp.where(place3 == 31, 0.0, w3).astype(F32)
    first_x = jnp.where(low3, 0.0, w3).astype(F32)
    last_x = jnp.where(low3, w3, 0.0).astype(F32)
    at3 = slice(8, 40)
    for x in range(4):
        for i in range(2):
            here = k3[x, i, at3]
            parts = [
                (here + row_before(k3, x, i, 1, at3, low3)) * (first_x if x == 0 and i == 0 else w3),
                (here + row_after(k3, x, i, 1, at3, low3)) * (last_x if x == 3 and i == 1 else w3),
                (here + k3[x, i, 7:39]) * wy_low,
                (here + k3[x, i, 9:41]) * wy_high,
                (here + roll(here, 2)) * wz_low,
                (here + roll(here, -2)) * wz_high,
            ]
            total = ((parts[0] + parts[1]) + (parts[2] + parts[3])) + ((parts[4] + parts[5]) + 1.0)
            inverse = 1.0 / total
            i3[x, i] = inverse
            for n in range(6):
                c3[n, x, i] = parts[n] * inverse

    for copy in send_s1:
        copy.wait_recv()
    for i in range(-6, 14, 2):
        s1[i + 6:i + 8] = i1[i + 6:i + 8] * s1x[i + 7:i + 9, 10:34]
    for i in range(-4, 12, 2):
        v1[i + 7:i + 9, 12:28] = jnp.where(colours_16 == 0, s1[i + 6:i + 8, 2:18], 0.0)
    half_sweep_1(1, -4, 12, -4, 12)
    half_sweep_1(0, -2, 10, -4, 12)
    half_sweep_1(1, -2, 10, -4, 12)
    rows = []
    for i in range(0, 8, 2):
        new, old = update_1(i, 0, 8)
        left = d1[i + 6:i + 8, 6:14] * (new - old)
        rows += [left[0], left[1]]
    block_mean_1(rows)
    swap_s, spread_s, share_s = gather_copies(1, sg)
    swap_s.start()
    vk1[7:15, 16:24] = v1[7:15, 16:24]
    send_vk1 = halo_copies((vk1, (7, 16), vk1), 6, (8, 8), (7, 16), halo_sems.at[5], position)
    swap_s.wait_recv()
    mix(1, own2[pl.ds(2 * core, 2)], sg)
    for copy in spread_s:
        copy.start()
    for copy in send_vk1:
        copy.start()
    all_arrived(1)
    share_s.start()
    share_s.wait_recv()

    colours_2 = [(i + j_row + place) & 1 for i in range(2)]
    for x in range(4):
        for i in range(4):
            source = i2[x, i] * sg[x, i, at]
            s2[x, i, at] = source
            v2[x, i, at] = jnp.where(colours_2[i & 1] == 0, source, 0.0)

    def update_2(x, i, at, before, after, first_half):
        mid = v2[x, i, at]
        acc0 = s2[x, i, at] + c2[0, x, i, at] * row_before(v2, x, i, 3, at, first_half)
        acc1 = c2[1, x, i, at] * row_after(v2, x, i, 3, at, first_half) + c2[2, x, i, at] * v2[x, i, before]
        acc2 = c2[3, x, i, at] * v2[x, i, after] + c2[4, x, i, at] * roll(mid, 1)
        acc3 = c2[5, x, i, at] * roll(mid, -1)
        return (acc0 + acc1) + (acc2 + acc3), mid

    def half_sweep_2(colour):
        for x in range(4):
            for i in range(4):
                new, old = update_2(x, i, at, slice(7, 71), slice(9, 73), low)
                v2[x, i, at] = jnp.where(colours_2[i & 1] == colour, new, old)

    half_sweep_2(1)
    half_sweep_2(0)
    half_sweep_2(1)
    for x in range(4):
        for i in range(2):
            total = None
            for n in (2 * i, 2 * i + 1):
                new, old = update_2(x, n, at, slice(7, 71), slice(9, 73), low)
                left = d2[x, n] * (new - old)
                total = left if total is None else total + left
            t2[x, i] = pair_lanes(total)
    for x in range(4):
        for i in range(2):
            s3[x, i] = i3[x, i] * block_mean_2(x, i)

    colours_3 = [(i + row3 + place3) & 1 for i in range(2)]

    def half_sweep_3(colour):
        for x in range(4):
            for i in range(2):
                mid = v3[x, i, at3]
                acc0 = s3[x, i] + c3[0, x, i] * row_before(v3, x, i, 1, at3, low3)
                acc1 = c3[1, x, i] * row_after(v3, x, i, 1, at3, low3) + c3[2, x, i] * v3[x, i, 7:39]
                acc2 = c3[3, x, i] * v3[x, i, 9:41] + c3[4, x, i] * roll(mid, 2)
                acc3 = c3[5, x, i] * roll(mid, -2)
                new = (acc0 + acc1) + (acc2 + acc3)
                v3[x, i, at3] = jnp.where(colours_3[i] == colour, new, mid)

    def sweep_3(_, carry):
        half_sweep_3(0)
        half_sweep_3(1)
        return carry

    lax.fori_loop(0, COARSE_SWEEPS, sweep_3, 0)

    for x in range(4):
        for i in range(2):
            p2[x, i, pl.ds(8, 32, stride=2)] = v3[x, i, at3]
            p2[x, i, pl.ds(9, 32, stride=2)] = v3[x, i, at3]
    strip = gy // 2
    strip = pl.multiple_of(8 * (strip + 1 - (strip + 7) // 8 - (strip + 1) // 8), 8)
    at, before, after = pl.ds(strip, 24), pl.ds(strip - 1, 24), pl.ds(strip + 1, 24)
    xs = [lax.rem(chip_x + n, 4) for n in (3, 0, 1)]
    low = iota((24, 128), 1) < 64
    place = iota((24, 128), 1) & 63
    colours_2 = [(i + iota((24, 128), 0) + place) & 1 for i in range(2)]
    for x in xs:
        for i in range(4):
            v2[x, i, at] = v2[x, i, at] + p2[x, i // 2, at]
    for colour in (0, 1, 0, 1):
        for x in xs:
            for i in range(4):
                new, old = update_2(x, i, at, before, after, low)
                v2[x, i, at] = jnp.where(colours_2[i & 1] == colour, new, old)

    spot = iota((10, 128), 1) >> 1
    for d in range(-3, 7):
        row = 4 * core + d + 8
        x = lax.rem(chip_x + 3 + row // 8, 4)
        where = spot + 64 * (lax.rem(row, 8) // 4)
        coarse = jnp.take_along_axis(v2[x, d % 4, pl.ds(4 * gy + 5, 10)], where, axis=1)
        p1[d + 3, pl.ds(0, 10, stride=2)] = coarse
        p1[d + 3, pl.ds(1, 10, stride=2)] = coarse
    for copy in send_vk1:
        copy.wait_recv()
    for i in range(-6, 14):
        v1[i + 7, 10:30] = vk1[i + 7, 10:30] + p1[i // 2 + 3]
    half_sweep_1(0, -6, 14, -6, 18)
    half_sweep_1(1, -4, 12, -4, 12)
    half_sweep_1(0, -4, 12, -4, 12)
    half_sweep_1(1, -2, 10, -4, 12)

    for i in range(-2, 10):
        p0[i + 2, pl.ds(0, 12, stride=2)] = v1[i + 7, 14:26]
        p0[i + 2, pl.ds(1, 12, stride=2)] = v1[i + 7, 14:26]
    for copy in send_vk:
        copy.wait_recv()
    for i in range(-4, 20):
        vx[1, i + 5, 4:28] = vk[i + 5, 4:28] + p0[i // 2 + 2]
    half_sweep_0(0, -4, 20)
    half_sweep_0(1, -2, 18)
    half_sweep_0(0, -2, 18)
    half_sweep_0(1, 0, 16, 0, 16)
    for i in range(16):
        out[i, :, :128], out[i, :, 128:] = join(vx[0, i + 5, 8:24], vx[1, i + 5, 8:24], i & 1)

    for copy in send_k + send_v + send_k1 + send_s1 + send_vk + send_vk1 + [swap_k, share_k, swap_s, share_s]:
        copy.wait_send()
    for kind in (0, 1):
        pltpu.make_async_copy(dummy, dummy, pair_sems.at[kind, 1, 0]).wait()


def v_cycle(image, conduct):
    def vmem(*shape):
        return pltpu.VMEM(shape, F32)

    frame0, frame1, frame2 = (26, 32, 128), (22, 40, 128), (4, 4, 80, 128)
    return pl.pallas_call(
        kernel,
        out_shape=jax.ShapeDtypeStruct((16, 16, 256), F32),
        in_specs=[pl.BlockSpec(memory_space=pltpu.VMEM)] * 2,
        out_specs=pl.BlockSpec(memory_space=pltpu.VMEM),
        scratch_shapes=[
            vmem(2, *frame0), vmem(2, *frame0), vmem(2, 16, 16, 128), vmem(*frame0), vmem(2, 6, 24, 24, 128),
            vmem(2, 24, 24, 128), vmem(2, 24, 24, 128), vmem(8, 16, 128), vmem(12, 24, 128),
            vmem(*frame1), vmem(*frame1), vmem(*frame1), vmem(*frame1), vmem(6, 20, 24, 128), vmem(20, 24, 128),
            vmem(20, 24, 128), vmem(20, 24, 128), vmem(4, 8, 128), vmem(10, 20, 128),
            vmem(4, 4, 128), vmem(2, 2, 4, 128), vmem(8, 4, 128), vmem(*frame2), vmem(*frame2), vmem(*frame2),
            vmem(6, *frame2), vmem(*frame2), vmem(4, 4, 64, 128), vmem(4, 4, 64, 128), vmem(4, 2, 64, 128),
            vmem(4, 2, 80, 128),
            vmem(4, 2, 48, 128), vmem(4, 2, 48, 128), vmem(6, 4, 2, 32, 128), vmem(4, 2, 32, 128),
            vmem(4, 2, 32, 128), vmem(63, 2, 4, 128),
            pltpu.SemaphoreType.DMA((6, 2, 8)), pltpu.SemaphoreType.DMA((2, 3, 2)),
        ],
        compiler_params=pltpu.CompilerParams(
            collective_id=0, has_side_effects=True, vmem_limit_bytes=48 * 2**20
        ),
        name="v_cycle",
    )(image, conduct)


def solution(mesh):
    return jax.shard_map(
        v_cycle,
        mesh=mesh,
        in_specs=(P("gx", "gy", None), P("gx", "gy", None)),
        out_specs=P("gx", "gy", None),
        check_vma=False,
    )
```

```python
import jax
import jax.numpy as jnp
from jax import lax
from jax.experimental import pallas as pl
from jax.experimental.pallas import tpu as pltpu
from jax.sharding import PartitionSpec as P

COARSE_SWEEPS = 8
MESH = pl.DeviceIdType.MESH
F32 = jnp.float32
GX, GY = 8, 16
DIRECTIONS = [(-1, 0), (1, 0), (0, -1), (0, 1), (-1, -1), (-1, 1), (1, -1), (1, 1)]
CHIPS = sorted(
    [(x, y, z) for x in range(4) for y in range(4) for z in range(4) if (x, y, z) != (0, 0, 0)],
    key=lambda d: -sum(min(c, 4 - c) for c in d),
)


def iota(shape, dim):
    return lax.broadcasted_iota(jnp.int32, shape, dim)


def roll(values, shift):
    return pltpu.roll(values, shift % 128, values.ndim - 1)


def halo_copies(src, src_origin, dst, origin, extent, widths, sems, position, corners=None):
    gx, gy = position
    lead = (slice(None),) * (len(dst.shape) - 3)

    def piece(step, size, here, there, start, stop):
        if step == 0:
            return slice(here, here + size), slice(there, there + size)
        if step > 0:
            return slice(here + size - stop, here + size - start), slice(there - stop, there - start)
        return slice(here + start, here + stop), slice(there + size + start, there + size + stop)

    copies = []
    for dx, dy in DIRECTIONS:
        boxes = [((0, widths[0]), (0, widths[1]))]
        if dx and dy and corners is not None:
            boxes = [((start, stop), (0, width)) for start, stop, width in corners]
        for box_x, box_y in boxes:
            src_x, dst_x = piece(dx, extent[0], src_origin[0], origin[0], *box_x)
            src_y, dst_y = piece(dy, extent[1], src_origin[1], origin[1], *box_y)
            copies.append(
                pltpu.make_async_remote_copy(
                    src_ref=src.at[lead + (src_x, src_y)],
                    dst_ref=dst.at[lead + (dst_x, dst_y)],
                    send_sem=sems.at[0, len(copies)],
                    recv_sem=sems.at[1, len(copies)],
                    device_id=(lax.rem(gx + dx + GX, GX), lax.rem(gy + dy + GY, GY)),
                    device_id_type=MESH,
                )
            )
    return copies


def couple(here, same, cross, low, high, other, weights, z_step):
    w, w_cross, w_low, w_high, w_below, w_above = weights
    parts = [
        (here + same) * w,
        (here + cross) * w_cross,
        (here + low) * w_low,
        (here + high) * w_high,
        (here + roll(other, z_step)) * w_below,
        (here + roll(other, -z_step)) * w_above,
    ]
    total = ((parts[0] + parts[1]) + (parts[2] + parts[3])) + ((parts[4] + parts[5]) + 1.0)
    inverse = 1.0 / total
    return [part * inverse for part in parts], total, inverse


def relax(source, couplings, same, cross, low, high, z_step):
    acc0 = source + couplings[0] * same
    acc1 = couplings[4] * roll(same, z_step) + couplings[5] * roll(same, -z_step)
    acc2 = couplings[2] * low + couplings[3] * high
    return (acc0 + acc2) + (acc1 + couplings[1] * cross)


def kernel(
    image, conduct, out,
    image_in, conduct_in, kx, vx, vs, vk, c0, s0, d0, t0, p0,
    k1, s1x, v1, vk1, c1, s1, i1, d1, t1, p1,
    own2, part2, mix2, kg, sg, v2, c2, s2, i2, d2, t2, p2,
    k3, v3, c3, s3, i3, dummy,
    halo_sems, pair_sems, in_sems,
):
    gx, gy = lax.axis_index("gx"), lax.axis_index("gy")
    chip_x, core = gx // 2, lax.rem(gx, 2)
    chip_z, chip_y = gy // 4, lax.rem(gy, 4)
    sibling = (chip_x * 2 + 1 - core, gy)
    chips = [
        (lax.rem(chip_x + x, 4) * 2 + core, lax.rem(chip_z + z, 4) * 4 + lax.rem(chip_y + y, 4))
        for x, y, z in CHIPS
    ]
    position = (gx, gy)
    barrier = pltpu.get_barrier_semaphore()
    greeted = chips + [
        (lax.rem(gx + dx + GX, GX), lax.rem(gy + dy + GY, GY)) for dx, dy in DIRECTIONS if dx
    ]
    fetch_k = pltpu.make_async_copy(conduct, conduct_in, in_sems.at[0])
    fetch_v = pltpu.make_async_copy(image, image_in, in_sems.at[1])
    fetch_k.start()
    fetch_v.start()
    for peer in greeted:
        pl.semaphore_signal(barrier, inc=1, device_id=peer, device_id_type=MESH)

    lane0 = iota((16, 128), 1)
    odd_row = iota((16, 128), 0) & 1
    low0 = lane0 < 64
    half_lane = (lane0 & 63) * 2

    def split(values, par):
        parity = odd_row ^ par
        first = half_lane + jnp.where(low0, parity, 1 - parity)
        second = half_lane + jnp.where(low0, 1 - parity, parity)
        left = jnp.take_along_axis(values[:, :128], first, axis=1)
        right = jnp.take_along_axis(values[:, 128:], second, axis=1)
        return jnp.where(low0, left, right), roll(jnp.where(low0, right, left), 64)

    def join(red, black, par):
        parity = odd_row ^ par
        turned = roll(black, 64)
        left, right = jnp.where(low0, red, turned), jnp.where(low0, turned, red)
        same = (lane0 & 1) == parity
        half = lane0 >> 1
        first = half + jnp.where(same, 0, 64)
        second = half + jnp.where(same, 64, 0)
        return jnp.take_along_axis(left, first, axis=1), jnp.take_along_axis(right, second, axis=1)
    nothing = jnp.zeros((2, 4, 2, 8, 128), F32)
    for ref in (kg, v2):
        ref[:, :, :, 0:8], ref[:, :, :, 72:80] = nothing, nothing
    nothing = jnp.zeros((2, 4, 8, 128), F32)
    for ref in (k3, v3):
        ref[:, :, 0:8], ref[:, :, 40:48] = nothing, nothing
    fetch_k.wait()
    for i in range(16):
        kx[0, i + 5, 8:24], kx[1, i + 5, 8:24] = split(conduct_in[i], i & 1)
    pl.semaphore_wait(barrier, len(greeted))
    cone = [(0, 2, 4), (2, 4, 2)]
    send_k = halo_copies(kx, (5, 8), kx, (5, 8), (16, 16), (5, 5), halo_sems.at[0], position, cone)
    send_v = halo_copies(vs, (0, 0), vx, (5, 8), (16, 16), (5, 5), halo_sems.at[1], position, cone)
    for copy in send_k:
        copy.start()
    fetch_v.wait()
    for i in range(16):
        red, black = split(image_in[i], i & 1)
        vx[0, i + 5, 8:24], vx[1, i + 5, 8:24] = red, black
        vs[0, i], vs[1, i] = red, black
    for copy in send_v:
        copy.start()
    def block_mean():
        return [0.125 * (t0[i, pl.ds(0, 8, stride=2)] + t0[i, pl.ds(1, 8, stride=2)]) for i in range(8)]

    odd_8 = ((iota((8, 128), 0) + iota((8, 128), 1)) & 1) == 1
    odd_4 = ((iota((4, 128), 0) + iota((4, 128), 1)) & 1) == 1
    even_lane = (iota((8, 128), 1) & 63) * 2

    def merge(first, second, odd):
        return jnp.where(odd, second, first), jnp.where(odd, first, second)

    def level_2_share(kind, pairs):
        for i in range(4):
            t1[i] = jnp.take_along_axis(pairs[i], even_lane, axis=1) + jnp.take_along_axis(pairs[i], even_lane + 1, axis=1)
        rows = [0.125 * (t1[i, pl.ds(0, 4, stride=2)] + t1[i, pl.ds(1, 4, stride=2)]) for i in range(4)]
        for a in range(2):
            own2[kind, 0, a], own2[kind, 1, a] = merge(rows[2 * a], rows[2 * a + 1], odd_4)

    def pair_copy(src, dst, kind, step):
        return pltpu.make_async_remote_copy(
            src_ref=src, dst_ref=dst, send_sem=pair_sems.at[kind, step, 0], recv_sem=pair_sems.at[kind, step, 1],
            device_id=sibling, device_id_type=MESH,
        )

    def gather_copies(kind, whole):
        swap = pair_copy(own2.at[kind, 1 - core], part2.at[kind], kind, 0)
        place = (core, chip_x, slice(None), pl.ds(8 + 4 * gy, 4))
        spread = [
            pltpu.make_async_remote_copy(
                src_ref=mix2.at[kind], dst_ref=whole.at[place], send_sem=pair_sems.at[kind, 1 + x, 0],
                recv_sem=pair_sems.at[kind, 1 + x, 1], device_id=chip, device_id_type=MESH,
            )
            for chip, (x, _, _) in zip(chips, CHIPS)
        ]
        planes = [whole.at[core, lax.rem(chip_x + 4 - x, 4), :, 8:72] for x in range(4)]
        share = [pair_copy(plane, plane, kind, 5 + x) for x, plane in enumerate(planes)]
        return swap, spread, share

    def mix(kind, whole):
        mine = iota((2, 4, 128), 2) // 64 == core
        cells = jnp.where(mine, own2[kind, core], part2[kind])
        mix2[kind] = cells
        whole[core, chip_x, :, pl.ds(8 + 4 * gy, 4)] = cells

    def landed(kind, x, which):
        some = dummy.at[0:15] if x == 0 else dummy
        pltpu.make_async_copy(some, some, pair_sems.at[kind, 1 + x, which]).wait()

    def pass_on(kind, share):
        for x in (0, 1, 3, 2):
            landed(kind, x, 1)
            share[x].start()
        for copy in share:
            copy.wait_recv()

    for i in range(8):
        e = 2 * i + 5
        t0[i] = (kx[0, e, 8:24] + kx[1, e, 8:24]) + (kx[0, e + 1, 8:24] + kx[1, e + 1, 8:24])
    rows = block_mean()
    for a in range(4):
        k1[0, a + 4, 16:24], k1[1, a + 4, 16:24] = merge(rows[2 * a], rows[2 * a + 1], odd_8)
    level_2_share(0, [rows[2 * a] + rows[2 * a + 1] for a in range(4)])
    send_k1 = halo_copies(k1, (4, 16), k1, (4, 16), (4, 8), (3, 6), halo_sems.at[2], position)
    swap_k, spread_k, share_k = gather_copies(0, kg)
    swap_k.start()
    for copy in send_k1:
        copy.start()

    shape = (2, 24, 128)
    sub, lanes = iota(shape, 1), iota(shape, 2)
    even_row = ((iota(shape, 0) + sub) & 1) == 0
    wy_low = jnp.where((sub == 4) & (gy == 0), 0.0, 0.5).astype(F32)
    wy_high = jnp.where((sub == 19) & (gy == GY - 1), 0.0, 0.5).astype(F32)
    wx_low = jnp.where(gx == 0, 0.0, 0.5).astype(F32)
    wx_high = jnp.where(gx == GX - 1, 0.0, 0.5).astype(F32)
    wz = [
        jnp.where(even_row, jnp.where(lanes == 0, 0.0, 0.5), jnp.where(lanes == 127, 0.0, 0.5)).astype(F32),
        jnp.where(even_row, jnp.where(lanes == 127, 0.0, 0.5), jnp.where(lanes == 0, 0.0, 0.5)).astype(F32),
    ]

    def beside(values, colour, rows_even):
        below, above = roll(values, 1), roll(values, -1)
        return jnp.where(rows_even, below, above) if colour == 0 else jnp.where(rows_even, above, below)

    row_index = iota((2, 1, 1), 0)

    def couplings_0(colour, start, stop):
        for i in range(start, stop, 2):
            e = i + 5
            here, other = kx[colour, e:e + 2, 4:28], kx[1 - colour, e:e + 2, 4:28]
            wx_l = jnp.where(row_index == 0, wx_low, 0.5) if i == 0 else 0.5
            wx_h = jnp.where(row_index == 1, wx_high, 0.5) if i == 14 else 0.5
            parts = [
                (here + kx[1 - colour, e - 1:e + 1, 4:28]) * wx_l,
                (here + kx[1 - colour, e + 1:e + 3, 4:28]) * wx_h,
                (here + kx[1 - colour, e:e + 2, 3:27]) * wy_low,
                (here + kx[1 - colour, e:e + 2, 5:29]) * wy_high,
                (here + other) * 0.5,
                (here + beside(other, colour, even_row)) * wz[colour],
            ]
            total = ((parts[0] + parts[1]) + (parts[2] + parts[3])) + ((parts[4] + parts[5]) + 1.0)
            inverse = 1.0 / total
            d0[colour, i + 4:i + 6] = total
            s0[colour, i + 4:i + 6] = inverse
            for n in range(6):
                c0[colour, n, i + 4:i + 6] = parts[n] * inverse

    def update_0(colour, i, lo, hi, rows_even):
        e, f = i + 5, i + 4
        a, b = lo + 8, hi + 8
        here = slice(lo + 4, hi + 4)
        other = vx[1 - colour, e:e + 2, a:b]
        acc0 = s0[colour, f:f + 2, here] + c0[colour, 0, f:f + 2, here] * vx[1 - colour, e - 1:e + 1, a:b]
        acc1 = c0[colour, 1, f:f + 2, here] * vx[1 - colour, e + 1:e + 3, a:b]
        acc1 += c0[colour, 2, f:f + 2, here] * vx[1 - colour, e:e + 2, a - 1:b - 1]
        acc2 = c0[colour, 3, f:f + 2, here] * vx[1 - colour, e:e + 2, a + 1:b + 1]
        acc2 += c0[colour, 4, f:f + 2, here] * other
        acc3 = c0[colour, 5, f:f + 2, here] * beside(other, colour, rows_even)
        return (acc0 + acc1) + (acc2 + acc3)

    own_even = ((iota((2, 16, 128), 0) + iota((2, 16, 128), 1)) & 1) == 0

    def half_sweep_0(colour, start, stop, lo=-4, hi=20):
        rows_even = even_row if hi - lo == 24 else own_even
        for i in range(start, stop, 2):
            vx[colour, i + 5:i + 7, lo + 8:hi + 8] = update_0(colour, i, lo, hi, rows_even)
    for copy in send_k:
        copy.wait_recv()
    couplings_0(0, -4, 20)
    couplings_0(1, -4, 20)
    for copy in send_v:
        copy.wait_recv()
    for colour in (0, 1):
        for i in range(-4, 20, 2):
            s0[colour, i + 4:i + 6] = s0[colour, i + 4:i + 6] * vx[colour, i + 5:i + 7, 4:28]

    half_sweep_0(0, -4, 20)
    half_sweep_0(1, -4, 20)
    half_sweep_0(0, -2, 18)
    half_sweep_0(1, -2, 18)
    def residual_0(i):
        total = None
        for colour in (0, 1):
            left = update_0(colour, i, 0, 16, own_even) - vx[colour, i + 5:i + 7, 8:24]
            left = d0[colour, i + 4:i + 6, 4:20] * left
            total = left if total is None else total + left
        return total

    for i in range(8):
        both = residual_0(2 * i)
        t0[i] = both[0] + both[1]
    rows = block_mean()
    for a in range(4):
        s1x[0, a + 4, 16:24], s1x[1, a + 4, 16:24] = merge(rows[2 * a], rows[2 * a + 1], odd_8)
    send_s1 = halo_copies(s1x, (4, 16), s1x, (4, 16), (4, 8), (3, 5), halo_sems.at[3], position)
    for copy in send_s1:
        copy.start()

    swap_k.wait_recv()
    mix(0, kg)
    for copy in spread_k:
        copy.start()
    vk[5:21, 8:24] = vx[1, 5:21, 8:24]
    send_vk = halo_copies(vk, (5, 8), vk, (5, 8), (16, 16), (4, 4), halo_sems.at[4], position)
    for copy in send_vk:
        copy.start()

    shape = (24, 128)
    col, lanes = iota(shape, 0) - 6, iota(shape, 1)
    w1 = 0.5 / 4.0
    wy_low = jnp.where((col == 0) & (gy == 0), 0.0, w1).astype(F32)
    wy_high = jnp.where((col == 7) & (gy == GY - 1), 0.0, w1).astype(F32)
    wx_low = jnp.where(gx == 0, 0.0, w1).astype(F32)
    wx_high = jnp.where(gx == GX - 1, 0.0, w1).astype(F32)
    wz_low = jnp.where(lanes == 0, 0.0, w1).astype(F32)
    wz_high = jnp.where(lanes == 127, 0.0, w1).astype(F32)

    def first_of_pair(size, origin):
        odd = (iota((size, 128), 0) + iota((size, 128), 1) + origin) & 1
        return odd == 0, odd == 1

    first_24, first_16, first_8 = first_of_pair(24, 0), first_of_pair(16, 0), first_of_pair(8, 0)
    for copy in send_k1:
        copy.wait_recv()
    for colour in (0, 1):
        for a in range(-3, 7):
            e, f = a + 4, a + 3
            other = k1[1 - colour, e, 10:34]
            first = first_24[colour]
            w_cross = w1
            if a in (0, 3):
                w_cross = jnp.where(first, wx_low if a == 0 else w1, wx_high if a == 3 else w1)
            parts, total, inverse = couple(
                k1[colour, e, 10:34], other, jnp.where(first, k1[1 - colour, e - 1, 10:34], k1[1 - colour, e + 1, 10:34]),
                k1[1 - colour, e, 9:33], k1[1 - colour, e, 11:35], other, (w1, w_cross, wy_low, wy_high, wz_low, wz_high), 1,
            )
            d1[colour, f] = total
            i1[colour, f] = inverse
            for n in range(6):
                c1[colour, n, f] = parts[n]

    def update_1(colour, a, lo, hi):
        e, f = a + 4, a + 3
        here, at = slice(lo + 6, hi + 6), slice(lo + 16, hi + 16)
        first = {24: first_24, 16: first_16, 8: first_8}[hi - lo][colour]
        return relax(
            s1[colour, f, here], [c1[colour, n, f, here] for n in range(6)], v1[1 - colour, e, at],
            jnp.where(first, v1[1 - colour, e - 1, at], v1[1 - colour, e + 1, at]),
            v1[1 - colour, e, lo + 15:hi + 15], v1[1 - colour, e, lo + 17:hi + 17], 1,
        )

    def half_sweep_1(colour, start, stop, lo, hi):
        for a in range(start, stop):
            v1[colour, a + 4, lo + 16:hi + 16] = update_1(colour, a, lo, hi)

    for copy in send_s1:
        copy.wait_recv()
    for colour in (0, 1):
        for a in range(-3, 7):
            s1[colour, a + 3] = i1[colour, a + 3] * s1x[colour, a + 4, 10:34]
    for a in range(-2, 6):
        v1[0, a + 4, 12:28] = s1[0, a + 3, 2:18]
    half_sweep_1(1, -2, 6, -4, 12)
    half_sweep_1(0, -1, 5, -4, 12)
    half_sweep_1(1, -1, 5, -4, 12)
    pairs = []
    for a in range(4):
        left = [d1[n, a + 3, 6:14] * (update_1(n, a, 0, 8) - v1[n, a + 4, 16:24]) for n in (0, 1)]
        pairs.append(left[0] + left[1])
    level_2_share(1, pairs)
    swap_s, spread_s, share_s = gather_copies(1, sg)
    swap_s.start()
    vk1[4:8, 16:24] = v1[1, 4:8, 16:24]
    send_vk1 = halo_copies(vk1, (4, 16), vk1, (4, 16), (4, 8), (3, 6), halo_sems.at[5], position)
    swap_s.wait_recv()
    mix(1, sg)
    for copy in spread_s:
        copy.start()
    for copy in send_vk1:
        copy.start()

    pass_on(0, share_k)
    lane = iota((64, 128), 1)
    place = lane & 63
    j_row = iota((64, 128), 0)
    low_64 = lane < 64
    first_64 = first_of_pair(64, 0)
    w2 = 0.5 / 16.0
    wy_low = jnp.where(j_row == 0, 0.0, w2).astype(F32)
    wy_high = jnp.where(j_row == 63, 0.0, w2).astype(F32)
    wz_low = jnp.where(place == 0, 0.0, w2).astype(F32)
    wz_high = jnp.where(place == 63, 0.0, w2).astype(F32)

    def cross_2(ref, colour, x, a, at, low, first):
        before, after = lax.rem(x + 3, 4), lax.rem(x + 1, 4)
        if a == 0:
            turned = roll(jnp.where(low, ref[colour, x, 1, at], ref[colour, before, 1, at]), 64)
            return jnp.where(first, turned, ref[colour, x, 1, at])
        turned = roll(jnp.where(low, ref[colour, after, 0, at], ref[colour, x, 0, at]), 64)
        return jnp.where(first, ref[colour, x, 0, at], turned)

    at = slice(8, 72)
    for colour in (0, 1):
        for x in range(4):
            for a in range(2):
                other = kg[1 - colour, x, a, at]
                w_cross = w2
                if (x, a) == (0, 0):
                    w_cross = jnp.where(first_64[colour] & low_64, 0.0, w2).astype(F32)
                if (x, a) == (3, 1):
                    w_cross = jnp.where(first_64[colour] | low_64, w2, 0.0).astype(F32)
                parts, total, inverse = couple(
                    kg[colour, x, a, at], other, cross_2(kg, 1 - colour, x, a, at, low_64, first_64[colour]),
                    kg[1 - colour, x, a, 7:71], kg[1 - colour, x, a, 9:73], other,
                    (w2, w_cross, wy_low, wy_high, wz_low, wz_high), 1,
                )
                d2[colour, x, a] = total
                i2[colour, x, a] = inverse
                for n in range(6):
                    c2[colour, n, x, a, at] = parts[n]
    even_place = (lane & 1) == 0
    lane3 = iota((32, 128), 1)
    place3 = (lane3 & 63) >> 1
    row3 = iota((32, 128), 0)
    low3 = lane3 < 64
    odd3 = ((row3 + place3) & 1) == 1
    first3 = (jnp.logical_not(odd3), odd3)

    def level_3_share(x, pairs):
        for a in range(2):
            t2[x, a] = pairs[a] + jnp.where(even_place, roll(pairs[a], -1), roll(pairs[a], 1))
        rows = [0.125 * (t2[x, a, pl.ds(0, 32, stride=2)] + t2[x, a, pl.ds(1, 32, stride=2)]) for a in range(2)]
        return merge(rows[0], rows[1], odd3)

    w3 = 0.5 / 64.0
    wy_low = jnp.where(row3 == 0, 0.0, w3).astype(F32)
    wy_high = jnp.where(row3 == 31, 0.0, w3).astype(F32)
    wz_low = jnp.where(place3 == 0, 0.0, w3).astype(F32)
    wz_high = jnp.where(place3 == 31, 0.0, w3).astype(F32)
    at3 = slice(8, 40)

    def cross_3(ref, colour, x, first):
        here = ref[colour, x, at3]
        before = jnp.where(low3, here, ref[colour, (x + 3) % 4, at3])
        after = jnp.where(low3, ref[colour, (x + 1) % 4, at3], here)
        return roll(jnp.where(first, before, after), 64)

    for x in range(4):
        k3[0, x, at3], k3[1, x, at3] = level_3_share(x, [kg[0, x, a, at] + kg[1, x, a, at] for a in range(2)])
    for colour in (0, 1):
        for x in range(4):
            other = k3[1 - colour, x, at3]
            w_cross = w3
            if x == 0:
                w_cross = jnp.where(first3[colour] & low3, 0.0, w3).astype(F32)
            if x == 3:
                w_cross = jnp.where(first3[colour] | low3, w3, 0.0).astype(F32)
            parts, _, inverse = couple(
                k3[colour, x, at3], other, cross_3(k3, 1 - colour, x, first3[colour]),
                k3[1 - colour, x, 7:39], k3[1 - colour, x, 9:41], other, (w3, w_cross, wy_low, wy_high, wz_low, wz_high), 2,
            )
            i3[colour, x] = inverse
            for n in range(6):
                c3[colour, n, x] = parts[n]
    pass_on(1, share_s)

    for colour in (0, 1):
        for x in range(4):
            for a in range(2):
                source = i2[colour, x, a] * sg[colour, x, a, at]
                s2[colour, x, a, at] = source
                if colour == 0:
                    v2[0, x, a, at] = source

    def update_2(colour, x, a, at, before, after, low, first):
        return relax(
            s2[colour, x, a, at], [c2[colour, n, x, a, at] for n in range(6)], v2[1 - colour, x, a, at],
            cross_2(v2, 1 - colour, x, a, at, low, first[colour]), v2[1 - colour, x, a, before], v2[1 - colour, x, a, after], 1,
        )

    def half_sweep_2(colour):
        for x in range(4):
            for a in range(2):
                v2[colour, x, a, at] = update_2(colour, x, a, at, slice(7, 71), slice(9, 73), low_64, first_64)

    half_sweep_2(1)
    half_sweep_2(0)
    half_sweep_2(1)
    for x in range(4):
        pairs = []
        for a in range(2):
            total = None
            for colour in (0, 1):
                left = update_2(colour, x, a, at, slice(7, 71), slice(9, 73), low_64, first_64) - v2[colour, x, a, at]
                left = d2[colour, x, a] * left
                total = left if total is None else total + left
            pairs.append(total)
        sources = level_3_share(x, pairs)
        for colour in (0, 1):
            s3[colour, x] = i3[colour, x] * sources[colour]

    def half_sweep_3(colour):
        for x in range(4):
            v3[colour, x, at3] = relax(
                s3[colour, x], [c3[colour, n, x] for n in range(6)], v3[1 - colour, x, at3],
                cross_3(v3, 1 - colour, x, first3[colour]), v3[1 - colour, x, 7:39], v3[1 - colour, x, 9:41], 2,
            )

    for x in range(4):
        v3[0, x, at3] = s3[0, x]
    half_sweep_3(1)
    for _ in range(COARSE_SWEEPS - 1):
        half_sweep_3(0)
        half_sweep_3(1)

    for x in range(4):
        red, black = v3[0, x, at3], v3[1, x, at3]
        for a, row in enumerate((jnp.where(odd3, black, red), jnp.where(odd3, red, black))):
            p2[x, a, pl.ds(8, 32, stride=2)] = row
            p2[x, a, pl.ds(9, 32, stride=2)] = row
    strip = gy // 2
    strip = pl.multiple_of(8 * (strip + 1 - (strip + 7) // 8 - (strip + 1) // 8), 8)
    at, before, after = pl.ds(strip, 24), pl.ds(strip - 1, 24), pl.ds(strip + 1, 24)
    xs = [lax.rem(chip_x + n, 4) for n in (3, 0, 1)]
    low_24 = iota((24, 128), 1) < 64
    for x in xs:
        for a in range(2):
            v2[1, x, a, at] = v2[1, x, a, at] + p2[x, a, at]
    for colour in (0, 1, 0, 1):
        news = [update_2(colour, x, a, at, before, after, low_24, first_24) for x in xs for a in range(2)]
        for n, new in enumerate(news):
            v2[colour, xs[n // 2], n % 2, at] = new

    spot = iota((10, 128), 1) >> 1
    odd_10 = (iota((10, 128), 0) + iota((10, 128), 1) + 1) & 1
    for d in range(-3, 7):
        row = 4 * core + d + 8
        x = lax.rem(chip_x + 3 + row // 8, 4)
        where = spot + 64 * (lax.rem(row, 8) // 4)
        cells = (x, d % 4 // 2, pl.ds(4 * gy + 5, 10))
        coarse = jnp.where(odd_10 == d % 2, v2[(0,) + cells], v2[(1,) + cells])
        coarse = jnp.take_along_axis(coarse, where, axis=1)
        p1[d + 3, pl.ds(0, 10, stride=2)] = coarse
        p1[d + 3, pl.ds(1, 10, stride=2)] = coarse
    for copy in send_vk1:
        copy.wait_recv()
    for a in range(-3, 7):
        v1[1, a + 4, 10:30] = vk1[a + 4, 10:30] + p1[a + 3]
    half_sweep_1(0, -3, 7, -6, 18)
    half_sweep_1(1, -2, 6, -4, 12)
    half_sweep_1(0, -2, 6, -4, 12)
    half_sweep_1(1, -1, 5, -4, 12)

    odd_12 = (iota((12, 128), 0) + iota((12, 128), 1)) & 1
    for i in range(-2, 10):
        a = i // 2
        row = jnp.where(odd_12 == i % 2, v1[0, a + 4, 14:26], v1[1, a + 4, 14:26])
        p0[i + 2, pl.ds(0, 12, stride=2)] = row
        p0[i + 2, pl.ds(1, 12, stride=2)] = row
    for copy in send_vk:
        copy.wait_recv()
    for i in range(-4, 20):
        vx[1, i + 5, 4:28] = vk[i + 5, 4:28] + p0[i // 2 + 2]
    half_sweep_0(0, -4, 20)
    half_sweep_0(1, -2, 18)
    half_sweep_0(0, -2, 18)
    half_sweep_0(1, 0, 16, 0, 16)
    for i in range(16):
        out[i, :, :128], out[i, :, 128:] = join(vx[0, i + 5, 8:24], vx[1, i + 5, 8:24], i & 1)
    for copy in send_k + send_v + send_k1 + send_s1 + send_vk + send_vk1 + [swap_k, swap_s] + share_k + share_s:
        copy.wait_send()
    for kind in (0, 1):
        for x in range(4):
            landed(kind, x, 0)


def v_cycle(image, conduct):
    def vmem(*shape):
        return pltpu.VMEM(shape, F32)

    frame0, frame1, frame2, frame3 = (26, 32, 128), (12, 40, 128), (4, 2, 80, 128), (2, 4, 48, 128)
    return pl.pallas_call(
        kernel,
        out_shape=jax.ShapeDtypeStruct((16, 16, 256), F32),
        in_specs=[pl.BlockSpec(memory_space=pltpu.HBM)] * 2,
        out_specs=pl.BlockSpec(memory_space=pltpu.VMEM),
        scratch_shapes=[
            vmem(16, 16, 256), vmem(16, 16, 256),
            vmem(2, *frame0), vmem(2, *frame0), vmem(2, 16, 16, 128), vmem(*frame0), vmem(2, 6, 24, 24, 128),
            vmem(2, 24, 24, 128), vmem(2, 24, 24, 128), vmem(8, 16, 128), vmem(12, 24, 128),
            vmem(2, *frame1), vmem(2, *frame1), vmem(2, *frame1), vmem(*frame1), vmem(2, 6, 10, 24, 128),
            vmem(2, 10, 24, 128), vmem(2, 10, 24, 128), vmem(2, 10, 24, 128), vmem(4, 8, 128), vmem(10, 20, 128),
            vmem(2, 2, 2, 4, 128), vmem(2, 2, 4, 128), vmem(2, 2, 4, 128),
            vmem(2, *frame2), vmem(2, *frame2), vmem(2, *frame2),
            vmem(2, 6, *frame2), vmem(2, *frame2), vmem(2, 4, 2, 64, 128), vmem(2, 4, 2, 64, 128), vmem(4, 2, 64, 128),
            vmem(*frame2),
            vmem(*frame3), vmem(*frame3), vmem(2, 6, 4, 32, 128), vmem(2, 4, 32, 128),
            vmem(2, 4, 32, 128), vmem(16, 2, 4, 128),
            pltpu.SemaphoreType.DMA((6, 2, 12)), pltpu.SemaphoreType.DMA((2, 9, 2)), pltpu.SemaphoreType.DMA((2,)),
        ],
        compiler_params=pltpu.CompilerParams(
            collective_id=0, has_side_effects=True, vmem_limit_bytes=48 * 2**20
        ),
        name="v_cycle",
    )(image, conduct)


def solution(mesh):
    return jax.shard_map(
        v_cycle,
        mesh=mesh,
        in_specs=(P("gx", "gy", None), P("gx", "gy", None)),
        out_specs=P("gx", "gy", None),
        check_vma=False,
    )
```

```python
import jax
import jax.numpy as jnp
from jax import lax
from jax.experimental import pallas as pl
from jax.experimental.pallas import tpu as pltpu
from jax.sharding import PartitionSpec as P

COARSE_SWEEPS = 8
MESH = pl.DeviceIdType.MESH
F32 = jnp.float32
GX, GY = 8, 16
DIRECTIONS = [(-1, -1), (-1, 1), (1, -1), (1, 1), (0, -1), (0, 1), (-1, 0), (1, 0)]
CHIPS = sorted(
    [(x, y, z) for x in range(4) for y in range(4) for z in range(4) if (x, y, z) != (0, 0, 0)],
    key=lambda d: -sum(min(c, 4 - c) for c in d),
)


def iota(shape, dim):
    return lax.broadcasted_iota(jnp.int32, shape, dim)


def roll(values, shift):
    return pltpu.roll(values, shift % 128, values.ndim - 1)


def halo_copies(src, src_origin, dst, origin, extent, widths, sems, position, corners=None):
    gx, gy = position
    lead = (slice(None),) * (len(dst.shape) - 3)

    def piece(step, size, here, there, start, stop):
        if step == 0:
            return slice(here, here + size), slice(there, there + size)
        if step > 0:
            return slice(here + size - stop, here + size - start), slice(there - stop, there - start)
        return slice(here + start, here + stop), slice(there + size + start, there + size + stop)

    copies, index = [], 0
    for dx, dy in DIRECTIONS:
        boxes = [((0, widths[0]), (0, widths[1]))]
        if dx and dy and corners is not None:
            boxes = [((start, stop), (0, width)) for start, stop, width in corners]
        group = []
        for box_x, box_y in boxes:
            src_x, dst_x = piece(dx, extent[0], src_origin[0], origin[0], *box_x)
            src_y, dst_y = piece(dy, extent[1], src_origin[1], origin[1], *box_y)
            group.append(
                pltpu.make_async_remote_copy(
                    src_ref=src.at[lead + (src_x, src_y)],
                    dst_ref=dst.at[lead + (dst_x, dst_y)],
                    send_sem=sems.at[0, index],
                    recv_sem=sems.at[1, index],
                    device_id=(lax.rem(gx + dx + GX, GX), lax.rem(gy + dy + GY, GY)),
                    device_id_type=MESH,
                )
            )
            index += 1
        copies.append((in_grid(gx + dx, gy + dy), in_grid(gx - dx, gy - dy), group))
    return copies


def in_grid(x, y):
    return (x >= 0) & (x < GX) & (y >= 0) & (y < GY)


def halo_start(copies):
    for sends, _, group in copies:

        @pl.when(sends)
        def _():
            for copy in group:
                copy.start()


def halo_wait(copies):
    for _, receives, group in copies:

        @pl.when(receives)
        def _():
            for copy in group:
                copy.wait_recv()


def halo_sent(copies):
    for sends, _, group in copies:

        @pl.when(sends)
        def _():
            for copy in group:
                copy.wait_send()


def couple(here, same, cross, low, high, other, weights, z_step):
    w, w_cross, w_low, w_high, w_below, w_above = weights
    parts = [
        (here + same) * w,
        (here + cross) * w_cross,
        (here + low) * w_low,
        (here + high) * w_high,
        (here + roll(other, z_step)) * w_below,
        (here + roll(other, -z_step)) * w_above,
    ]
    total = ((parts[0] + parts[1]) + (parts[2] + parts[3])) + ((parts[4] + parts[5]) + 1.0)
    inverse = 1.0 / total
    return [part * inverse for part in parts], total, inverse


def relax(source, couplings, same, cross, low, high, z_step):
    acc0 = source + couplings[0] * same
    acc1 = couplings[4] * roll(same, z_step) + couplings[5] * roll(same, -z_step)
    acc2 = couplings[2] * low + couplings[3] * high
    return (acc0 + acc2) + (acc1 + couplings[1] * cross)


def kernel(
    image, conduct, out,
    image_in, conduct_in, kx, vx, vs, vk, c0, s0, d0, t0, p0,
    k1, s1x, v1, vk1, c1, s1, i1, d1, t1, p1,
    q1, own2, kg, sg, v2, c2, s2, i2, d2, t2, p2,
    k3, v3, c3, s3, i3, dummy,
    halo_sems, gather_sems, tree_sems, in_sems,
):
    gx, gy = lax.axis_index("gx"), lax.axis_index("gy")
    chip_x, core = gx // 2, lax.rem(gx, 2)
    chip_z, chip_y = gy // 4, lax.rem(gy, 4)
    sibling = (chip_x * 2 + 1 - core, gy)
    chips = [
        (lax.rem(chip_x + x, 4) * 2 + core, lax.rem(chip_z + z, 4) * 4 + lax.rem(chip_y + y, 4))
        for x, y, z in CHIPS
    ]
    position = (gx, gy)
    barrier = pltpu.get_barrier_semaphore()
    greeted = chips + [
        (lax.rem(gx + dx + GX, GX), lax.rem(gy + dy + GY, GY)) for dx, dy in DIRECTIONS if dx
    ]
    fetch_k = pltpu.make_async_copy(conduct, conduct_in, in_sems.at[0])
    fetch_v = pltpu.make_async_copy(image, image_in, in_sems.at[1])
    fetch_k.start()
    fetch_v.start()
    for peer in greeted:
        pl.semaphore_signal(barrier, inc=1, device_id=peer, device_id_type=MESH)

    lane0 = iota((16, 128), 1)
    odd_row = iota((16, 128), 0) & 1
    low0 = lane0 < 64
    half_lane = (lane0 & 63) * 2

    def split(values, par):
        parity = odd_row ^ par
        first = half_lane + jnp.where(low0, parity, 1 - parity)
        second = half_lane + jnp.where(low0, 1 - parity, parity)
        left = jnp.take_along_axis(values[:, :128], first, axis=1)
        right = jnp.take_along_axis(values[:, 128:], second, axis=1)
        return jnp.where(low0, left, right), roll(jnp.where(low0, right, left), 64)

    def join(red, black, par):
        parity = odd_row ^ par
        turned = roll(black, 64)
        left, right = jnp.where(low0, red, turned), jnp.where(low0, turned, red)
        same = (lane0 & 1) == parity
        half = lane0 >> 1
        first = half + jnp.where(same, 0, 64)
        second = half + jnp.where(same, 64, 0)
        return jnp.take_along_axis(left, first, axis=1), jnp.take_along_axis(right, second, axis=1)
    nothing = jnp.zeros((2, 4, 4, 8, 128), F32)
    kg[:, :, :, 0:8], kg[:, :, :, 40:48] = nothing, nothing
    nothing = jnp.zeros((2, 20, 8, 128), F32)
    v2[:, :, 0:8], v2[:, :, 40:48] = nothing, nothing
    nothing = jnp.zeros((2, 2, 48, 128), F32)
    v2[:, 0:2], v2[:, 18:20] = nothing, nothing
    for ref in (k3, v3):
        nothing = jnp.zeros((2, 10, 8, 128), F32)
        ref[:, :, 0:8], ref[:, :, 24:32] = nothing, nothing
        nothing = jnp.zeros((2, 1, 32, 128), F32)
        ref[:, 0:1], ref[:, 9:10] = nothing, nothing

    def zero(ref, *at):
        at = (slice(None),) * (len(ref.shape) - 3) + at
        ref[at] = jnp.zeros(ref.at[at].shape, F32)

    for edge, rows0, rows1 in ((gx == 0, slice(0, 5), slice(0, 4)), (gx == GX - 1, slice(21, 26), slice(8, 12))):

        @pl.when(edge)
        def _():
            for ref in (kx, vx, vk):
                zero(ref, rows0)
            for ref in (k1, s1x, vk1):
                zero(ref, rows1)

    for edge, cols0, cols1 in ((gy == 0, slice(0, 8), slice(8, 16)), (gy == GY - 1, slice(24, 32), slice(24, 32))):

        @pl.when(edge)
        def _():
            for ref in (kx, vx, vk):
                zero(ref, slice(None), cols0)
            for ref in (k1, s1x, vk1):
                zero(ref, slice(None), cols1)

    fetch_k.wait()
    for i in range(16):
        kx[0, i + 5, 8:24], kx[1, i + 5, 8:24] = split(conduct_in[i], i & 1)
    pl.semaphore_wait(barrier, len(greeted))
    cone = [(0, 2, 4), (2, 4, 2)]
    send_k = halo_copies(kx, (5, 8), kx, (5, 8), (16, 16), (5, 5), halo_sems.at[0], position, cone)
    send_v = halo_copies(vs, (0, 0), vx, (5, 8), (16, 16), (5, 5), halo_sems.at[1], position, cone)
    halo_start(send_k)
    fetch_v.wait()
    for i in range(16):
        red, black = split(image_in[i], i & 1)
        vx[0, i + 5, 8:24], vx[1, i + 5, 8:24] = red, black
        vs[0, i], vs[1, i] = red, black
    halo_start(send_v)
    def block_mean():
        return [0.125 * (t0[i, pl.ds(0, 8, stride=2)] + t0[i, pl.ds(1, 8, stride=2)]) for i in range(8)]

    odd_8 = ((iota((8, 128), 0) + iota((8, 128), 1)) & 1) == 1
    odd_2 = ((iota((2, 128), 0) + iota((2, 128), 1)) & 1) == 1
    low_2 = iota((2, 128), 1) < 64
    even_lane = (iota((8, 128), 1) & 63) * 2

    def merge(first, second, odd):
        return jnp.where(odd, second, first), jnp.where(odd, first, second)

    def level_2_share(kind, pairs, whole):
        rows = []
        for i in range(4):
            t1[i] = jnp.take_along_axis(pairs[i], even_lane, axis=1) + jnp.take_along_axis(pairs[i], even_lane + 1, axis=1)
        for i in range(4):
            first = t1[i, pl.ds(0, 2, stride=2)] + t1[i, pl.ds(1, 2, stride=2)]
            second = t1[i, pl.ds(4, 2, stride=2)] + t1[i, pl.ds(5, 2, stride=2)]
            rows.append(0.125 * jnp.where(low_2, first, second))
        for a in range(2):
            cells = merge(rows[2 * a], rows[2 * a + 1], odd_2)
            for colour in (0, 1):
                own2[kind, colour, a] = cells[colour]
                whole[colour, chip_x, 2 * core + a, pl.ds(8 + 2 * gy, 2)] = cells[colour]

    def remote(src, dst, sems, device):
        return pltpu.make_async_remote_copy(
            src_ref=src, dst_ref=dst, send_sem=sems.at[0], recv_sem=sems.at[1], device_id=device, device_id_type=MESH
        )

    cores_rows = pl.ds(2 * core, 2)
    own_place = (slice(None), chip_x, cores_rows, pl.ds(8 + 2 * gy, 2))

    spread_s = [
        remote(own2.at[1], sg.at[own_place], gather_sems.at[x], chip) for chip, (x, _, _) in zip(chips, CHIPS)
    ]
    planes = [sg.at[:, lax.rem(chip_x + 4 - x, 4), cores_rows, 8:40] for x in range(4)]
    share_s = [remote(plane, plane, gather_sems.at[4 + x], sibling) for x, plane in enumerate(planes)]

    def landed(x, which):
        some = dummy.at[0:15] if x == 0 else dummy
        pltpu.make_async_copy(some, some, gather_sems.at[x, which]).wait()

    def chip_at(x, y, z):
        return (
            lax.rem(chip_x + x, 4) * 2 + core,
            lax.rem(chip_z + z, 4) * 4 + lax.rem(chip_y + y, 4),
        )

    column = kg.at[:, chip_x, cores_rows, pl.ds(8 + 8 * chip_z, 8)]
    sheet = kg.at[:, :, cores_rows, pl.ds(8 + 8 * chip_z, 8)]
    half = kg.at[:, :, cores_rows, 8:40]
    tree_y = [remote(own2.at[0], kg.at[own_place], tree_sems.at[n - 1], chip_at(0, n, 0)) for n in (2, 1, 3)]
    tree_x = [remote(column, column, tree_sems.at[n + 2], chip_at(n, 0, 0)) for n in (2, 1, 3)]
    tree_z = [remote(sheet, sheet, tree_sems.at[n + 5], chip_at(0, 0, n)) for n in (2, 1, 3)]
    tree_core = [remote(half, half, tree_sems.at[9], sibling)]

    for i in range(8):
        e = 2 * i + 5
        t0[i] = (kx[0, e, 8:24] + kx[1, e, 8:24]) + (kx[0, e + 1, 8:24] + kx[1, e + 1, 8:24])
    rows = block_mean()
    for a in range(4):
        k1[0, a + 4, 16:24], k1[1, a + 4, 16:24] = merge(rows[2 * a], rows[2 * a + 1], odd_8)
    level_2_share(0, [rows[2 * a] + rows[2 * a + 1] for a in range(4)], kg)
    send_k1 = halo_copies(k1, (4, 16), k1, (4, 16), (4, 8), (3, 6), halo_sems.at[2], position)
    halo_start(send_k1)
    for copy in tree_y:
        copy.start()

    shape = (2, 24, 128)
    sub, lanes = iota(shape, 1), iota(shape, 2)
    even_row = ((iota(shape, 0) + sub) & 1) == 0
    wy_low = jnp.where((sub == 4) & (gy == 0), 0.0, 0.5).astype(F32)
    wy_high = jnp.where((sub == 19) & (gy == GY - 1), 0.0, 0.5).astype(F32)
    wx_low = jnp.where(gx == 0, 0.0, 0.5).astype(F32)
    wx_high = jnp.where(gx == GX - 1, 0.0, 0.5).astype(F32)
    wz = [
        jnp.where(even_row, jnp.where(lanes == 0, 0.0, 0.5), jnp.where(lanes == 127, 0.0, 0.5)).astype(F32),
        jnp.where(even_row, jnp.where(lanes == 127, 0.0, 0.5), jnp.where(lanes == 0, 0.0, 0.5)).astype(F32),
    ]

    def beside(values, colour, rows_even):
        below, above = roll(values, 1), roll(values, -1)
        return jnp.where(rows_even, below, above) if colour == 0 else jnp.where(rows_even, above, below)

    row_index = iota((2, 1, 1), 0)

    def couplings_0(colour, start, stop):
        for i in range(start, stop, 2):
            e = i + 5
            here, other = kx[colour, e:e + 2, 4:28], kx[1 - colour, e:e + 2, 4:28]
            wx_l = jnp.where(row_index == 0, wx_low, 0.5) if i == 0 else 0.5
            wx_h = jnp.where(row_index == 1, wx_high, 0.5) if i == 14 else 0.5
            parts = [
                (here + kx[1 - colour, e - 1:e + 1, 4:28]) * wx_l,
                (here + kx[1 - colour, e + 1:e + 3, 4:28]) * wx_h,
                (here + kx[1 - colour, e:e + 2, 3:27]) * wy_low,
                (here + kx[1 - colour, e:e + 2, 5:29]) * wy_high,
                (here + other) * 0.5,
                (here + beside(other, colour, even_row)) * wz[colour],
            ]
            total = ((parts[0] + parts[1]) + (parts[2] + parts[3])) + ((parts[4] + parts[5]) + 1.0)
            inverse = 1.0 / total
            d0[colour, i + 4:i + 6] = total
            s0[colour, i + 4:i + 6] = inverse
            for n in range(6):
                c0[colour, n, i + 4:i + 6] = parts[n] * inverse

    def update_0(colour, i, lo, hi, rows_even):
        e, f = i + 5, i + 4
        a, b = lo + 8, hi + 8
        here = slice(lo + 4, hi + 4)
        other = vx[1 - colour, e:e + 2, a:b]
        acc0 = s0[colour, f:f + 2, here] + c0[colour, 0, f:f + 2, here] * vx[1 - colour, e - 1:e + 1, a:b]
        acc1 = c0[colour, 1, f:f + 2, here] * vx[1 - colour, e + 1:e + 3, a:b]
        acc1 += c0[colour, 2, f:f + 2, here] * vx[1 - colour, e:e + 2, a - 1:b - 1]
        acc2 = c0[colour, 3, f:f + 2, here] * vx[1 - colour, e:e + 2, a + 1:b + 1]
        acc2 += c0[colour, 4, f:f + 2, here] * other
        acc3 = c0[colour, 5, f:f + 2, here] * beside(other, colour, rows_even)
        return (acc0 + acc1) + (acc2 + acc3)

    own_even = ((iota((2, 16, 128), 0) + iota((2, 16, 128), 1)) & 1) == 0

    def half_sweep_0(colour, start, stop, lo=-4, hi=20):
        rows_even = even_row if hi - lo == 24 else own_even
        for i in range(start, stop, 2):
            vx[colour, i + 5:i + 7, lo + 8:hi + 8] = update_0(colour, i, lo, hi, rows_even)
    halo_wait(send_k)
    for copy in tree_y:
        copy.wait_recv()
    for copy in tree_x:
        copy.start()
    couplings_0(0, -4, 20)
    couplings_0(1, -4, 20)
    halo_wait(send_v)
    for colour in (0, 1):
        for i in range(-4, 20, 2):
            s0[colour, i + 4:i + 6] = s0[colour, i + 4:i + 6] * vx[colour, i + 5:i + 7, 4:28]

    half_sweep_0(0, -4, 20)
    half_sweep_0(1, -4, 20)
    half_sweep_0(0, -2, 18)
    half_sweep_0(1, -2, 18)
    def residual_0(i):
        total = None
        for colour in (0, 1):
            left = update_0(colour, i, 0, 16, own_even) - vx[colour, i + 5:i + 7, 8:24]
            left = d0[colour, i + 4:i + 6, 4:20] * left
            total = left if total is None else total + left
        return total

    for i in range(8):
        both = residual_0(2 * i)
        t0[i] = both[0] + both[1]
    rows = block_mean()
    for a in range(4):
        s1x[0, a + 4, 16:24], s1x[1, a + 4, 16:24] = merge(rows[2 * a], rows[2 * a + 1], odd_8)
    send_s1 = halo_copies(s1x, (4, 16), s1x, (4, 16), (4, 8), (3, 5), halo_sems.at[3], position)
    halo_start(send_s1)
    for copy in tree_x:
        copy.wait_recv()
    for copy in tree_z:
        copy.start()
    vk[5:21, 8:24] = vx[1, 5:21, 8:24]
    send_vk = halo_copies(vk, (5, 8), vk, (5, 8), (16, 16), (4, 4), halo_sems.at[4], position)
    halo_start(send_vk)

    shape = (24, 128)
    col, lanes = iota(shape, 0) - 6, iota(shape, 1)
    w1 = 0.5 / 4.0
    wy_low = jnp.where((col == 0) & (gy == 0), 0.0, w1).astype(F32)
    wy_high = jnp.where((col == 7) & (gy == GY - 1), 0.0, w1).astype(F32)
    wx_low = jnp.where(gx == 0, 0.0, w1).astype(F32)
    wx_high = jnp.where(gx == GX - 1, 0.0, w1).astype(F32)
    wz_low = jnp.where(lanes == 0, 0.0, w1).astype(F32)
    wz_high = jnp.where(lanes == 127, 0.0, w1).astype(F32)

    def first_of_pair(size, origin):
        odd = (iota((size, 128), 0) + iota((size, 128), 1) + origin) & 1
        return odd == 0, odd == 1

    first_24, first_16, first_8 = first_of_pair(24, 0), first_of_pair(16, 0), first_of_pair(8, 0)
    halo_wait(send_k1)
    for colour in (0, 1):
        for a in range(-3, 7):
            e, f = a + 4, a + 3
            other = k1[1 - colour, e, 10:34]
            first = first_24[colour]
            w_cross = w1
            if a in (0, 3):
                w_cross = jnp.where(first, wx_low if a == 0 else w1, wx_high if a == 3 else w1)
            parts, total, inverse = couple(
                k1[colour, e, 10:34], other, jnp.where(first, k1[1 - colour, e - 1, 10:34], k1[1 - colour, e + 1, 10:34]),
                k1[1 - colour, e, 9:33], k1[1 - colour, e, 11:35], other, (w1, w_cross, wy_low, wy_high, wz_low, wz_high), 1,
            )
            d1[colour, f] = total
            i1[colour, f] = inverse
            for n in range(6):
                c1[colour, n, f] = parts[n]

    def update_1(colour, a, lo, hi):
        e, f = a + 4, a + 3
        here, at = slice(lo + 6, hi + 6), slice(lo + 16, hi + 16)
        first = {24: first_24, 16: first_16, 8: first_8}[hi - lo][colour]
        return relax(
            s1[colour, f, here], [c1[colour, n, f, here] for n in range(6)], v1[1 - colour, e, at],
            jnp.where(first, v1[1 - colour, e - 1, at], v1[1 - colour, e + 1, at]),
            v1[1 - colour, e, lo + 15:hi + 15], v1[1 - colour, e, lo + 17:hi + 17], 1,
        )

    def half_sweep_1(colour, start, stop, lo, hi):
        for a in range(start, stop):
            v1[colour, a + 4, lo + 16:hi + 16] = update_1(colour, a, lo, hi)

    halo_wait(send_s1)
    for colour in (0, 1):
        for a in range(-3, 7):
            s1[colour, a + 3] = i1[colour, a + 3] * s1x[colour, a + 4, 10:34]
    for a in range(-2, 6):
        v1[0, a + 4, 12:28] = s1[0, a + 3, 2:18]
    half_sweep_1(1, -2, 6, -4, 12)
    half_sweep_1(0, -1, 5, -4, 12)
    half_sweep_1(1, -1, 5, -4, 12)
    pairs = []
    for a in range(4):
        left = [d1[n, a + 3, 6:14] * (update_1(n, a, 0, 8) - v1[n, a + 4, 16:24]) for n in (0, 1)]
        pairs.append(left[0] + left[1])
    level_2_share(1, pairs, sg)
    for copy in spread_s:
        copy.start()
    for copy in tree_z:
        copy.wait_recv()
    tree_core[0].start()
    vk1[4:8, 16:24] = v1[1, 4:8, 16:24]
    send_vk1 = halo_copies(vk1, (4, 16), vk1, (4, 16), (4, 8), (3, 6), halo_sems.at[5], position)
    halo_start(send_vk1)

    tree_core[0].wait_recv()
    def two_columns(size):
        return iota((size, 128), 1) < 64, (iota((size, 128), 0) & 1) == 1

    def beside_2(row_low, row_high, low, odd):
        turned = roll(jnp.where(low, row_high, row_low), 64)
        return jnp.where(odd, row_low, turned), jnp.where(odd, turned, row_high)

    lane = iota((32, 128), 1)
    place = lane & 63
    j_row = iota((32, 128), 0)
    low_32, odd_32 = two_columns(32)
    first_32 = first_of_pair(32, 0)
    w2 = 0.5 / 16.0
    wy_low = jnp.where((j_row == 0) & low_32, 0.0, w2).astype(F32)
    wy_high = jnp.where((j_row == 31) & (lane >= 64), 0.0, w2).astype(F32)
    wz_low = jnp.where(place == 0, 0.0, w2).astype(F32)
    wz_high = jnp.where(place == 63, 0.0, w2).astype(F32)

    def kg_rows(colour, a, at):
        return kg[colour, a // 4, a % 4, at]

    at = slice(8, 40)
    for colour in (0, 1):
        for a in range(16):
            other = kg_rows(1 - colour, a, at)
            before = kg_rows(1 - colour, max(a - 1, 0), at)
            after = kg_rows(1 - colour, min(a + 1, 15), at)
            w_cross = w2
            if a == 0:
                w_cross = jnp.where(first_32[colour], 0.0, w2).astype(F32)
            if a == 15:
                w_cross = jnp.where(first_32[colour], w2, 0.0).astype(F32)
            low, high = beside_2(
                kg_rows(1 - colour, a, slice(7, 39)), kg_rows(1 - colour, a, slice(9, 41)), low_32, odd_32
            )
            parts, total, inverse = couple(
                kg_rows(colour, a, at), other, jnp.where(first_32[colour], before, after), low, high, other,
                (w2, w_cross, wy_low, wy_high, wz_low, wz_high), 1,
            )
            d2[colour, a] = total
            i2[colour, a] = inverse
            for n in range(6):
                c2[colour, n, a] = parts[n]
    even_place = (lane & 1) == 0
    lane3 = iota((16, 128), 1)
    place3 = (lane3 & 63) >> 1
    row3 = iota((16, 128), 0)
    low3 = lane3 < 64
    odd3 = (((lane3 >> 6) + place3) & 1) == 1
    first3 = (jnp.logical_not(odd3), odd3)

    def level_3_share(p, pairs):
        for n in range(2):
            t2[2 * p + n] = pairs[n] + jnp.where(even_place, roll(pairs[n], -1), roll(pairs[n], 1))
        rows = [0.125 * (t2[2 * p + n, pl.ds(0, 16, stride=2)] + t2[2 * p + n, pl.ds(1, 16, stride=2)]) for n in range(2)]
        return merge(rows[0], rows[1], odd3)

    w3 = 0.5 / 64.0
    wy_low = jnp.where((row3 == 0) & low3, 0.0, w3).astype(F32)
    wy_high = jnp.where((row3 == 15) & (lane3 >= 64), 0.0, w3).astype(F32)
    wz_low = jnp.where(place3 == 0, 0.0, w3).astype(F32)
    wz_high = jnp.where(place3 == 31, 0.0, w3).astype(F32)
    at3 = slice(8, 24)

    def around_3(ref, colour, p, first):
        here = ref[colour, p + 1, at3]
        cross = jnp.where(first, ref[colour, p, at3], ref[colour, p + 2, at3])
        low = roll(jnp.where(low3, here, ref[colour, p + 1, 7:23]), 64)
        high = roll(jnp.where(low3, ref[colour, p + 1, 9:25], here), 64)
        return here, cross, low, high

    for p in range(8):
        pairs = [kg_rows(0, a, at) + kg_rows(1, a, at) for a in (2 * p, 2 * p + 1)]
        k3[0, p + 1, at3], k3[1, p + 1, at3] = level_3_share(p, pairs)
    for colour in (0, 1):
        for p in range(8):
            here, cross, low, high = around_3(k3, 1 - colour, p, first3[colour])
            w_cross = w3
            if p == 0:
                w_cross = jnp.where(first3[colour], 0.0, w3).astype(F32)
            if p == 7:
                w_cross = jnp.where(first3[colour], w3, 0.0).astype(F32)
            parts, _, inverse = couple(
                k3[colour, p + 1, at3], here, cross, low, high, here, (w3, w_cross, wy_low, wy_high, wz_low, wz_high), 2
            )
            i3[colour, p] = inverse
            for n in range(6):
                c3[colour, n, p] = parts[n]
    for x in (0, 1, 3, 2):
        landed(x, 1)
        share_s[x].start()
    for copy in share_s:
        copy.wait_recv()

    for colour in (0, 1):
        for a in range(16):
            source = i2[colour, a] * sg[colour, a // 4, a % 4, at]
            s2[colour, a] = source
            if colour == 0:
                v2[0, a + 2, at] = source

    def update_2(colour, a, rows, frame_rows, low, odd, first):
        before, here, after = frame_rows
        row_low, row_high = beside_2(v2[1 - colour, a + 2, before], v2[1 - colour, a + 2, after], low, odd)
        cross = jnp.where(first[colour], v2[1 - colour, a + 1, here], v2[1 - colour, a + 3, here])
        return relax(
            s2[colour, a, rows], [c2[colour, n, a, rows] for n in range(6)], v2[1 - colour, a + 2, here],
            cross, row_low, row_high, 1,
        )

    whole_2 = (slice(0, 32), (slice(7, 39), at, slice(9, 41)), low_32, odd_32, first_32)

    def half_sweep_2(colour):
        for a in range(16):
            v2[colour, a + 2, at] = update_2(colour, a, *whole_2)

    half_sweep_2(1)
    half_sweep_2(0)
    half_sweep_2(1)
    for p in range(8):
        pairs = []
        for a in (2 * p, 2 * p + 1):
            left = [d2[n, a] * (update_2(n, a, *whole_2) - v2[n, a + 2, at]) for n in (0, 1)]
            pairs.append(left[0] + left[1])
        sources = level_3_share(p, pairs)
        for colour in (0, 1):
            s3[colour, p] = i3[colour, p] * sources[colour]

    def half_sweep_3(colour):
        for p in range(8):
            here, cross, low, high = around_3(v3, 1 - colour, p, first3[colour])
            v3[colour, p + 1, at3] = relax(
                s3[colour, p], [c3[colour, n, p] for n in range(6)], here, cross, low, high, 2
            )

    for p in range(8):
        v3[0, p + 1, at3] = s3[0, p]
    half_sweep_3(1)
    for _ in range(COARSE_SWEEPS - 1):
        half_sweep_3(0)
        half_sweep_3(1)

    for p in range(8):
        red, black = v3[0, p + 1, at3], v3[1, p + 1, at3]
        for n, row in enumerate((jnp.where(odd3, black, red), jnp.where(odd3, red, black))):
            p2[2 * p + n, pl.ds(0, 16, stride=2)] = row
            p2[2 * p + n, pl.ds(1, 16, stride=2)] = row

    def within(value, top, span):
        value = value * ((value + span) // span)
        value = top - value
        return top - value * ((value + span) // span)

    a0 = 2 * within(gx - 2, 3, 8)
    r0 = 2 * within(gy - 2, 8, 16)
    strip = pl.ds(r0, 16)
    part_2 = (strip, (pl.ds(r0 + 7, 16), pl.ds(r0 + 8, 16), pl.ds(r0 + 9, 16)), *two_columns(16), first_16)
    for n in range(10):
        v2[1, a0 + n + 2, pl.ds(r0 + 8, 16)] = v2[1, a0 + n + 2, pl.ds(r0 + 8, 16)] + p2[a0 + n, strip]
    for colour in (0, 1, 0, 1):
        news = [update_2(colour, a0 + n, *part_2) for n in range(10)]
        for n, new in enumerate(news):
            v2[colour, a0 + n + 2, pl.ds(r0 + 8, 16)] = new

    spot = iota((8, 128), 1) >> 1
    for d in range(-3, 7):
        cells = (2 * gx + d // 2 + 2, pl.ds(2 * gy + 6, 8))
        coarse = jnp.where(odd_8 == (d % 2 == 1), v2[(0,) + cells], v2[(1,) + cells])
        q1[d + 3, 0] = jnp.take_along_axis(coarse, spot, axis=1)
        q1[d + 3, 1] = jnp.take_along_axis(coarse, spot + 64, axis=1)
    for d in range(10):
        for n in range(2):
            for m in range(2):
                column = q1[d, n, pl.ds(m, 4, stride=2)]
                p1[d, pl.ds(4 * n + 2 * m, 4, stride=8)] = column
                p1[d, pl.ds(4 * n + 2 * m + 1, 4, stride=8)] = column
    halo_wait(send_vk1)
    for a in range(-3, 7):
        v1[1, a + 4, 10:30] = vk1[a + 4, 10:30] + p1[a + 3, 2:22]
    half_sweep_1(0, -3, 7, -6, 18)
    half_sweep_1(1, -2, 6, -4, 12)
    half_sweep_1(0, -2, 6, -4, 12)
    half_sweep_1(1, -1, 5, -4, 12)

    odd_12 = (iota((12, 128), 0) + iota((12, 128), 1)) & 1
    for i in range(-2, 10):
        a = i // 2
        row = jnp.where(odd_12 == i % 2, v1[0, a + 4, 14:26], v1[1, a + 4, 14:26])
        p0[i + 2, pl.ds(0, 12, stride=2)] = row
        p0[i + 2, pl.ds(1, 12, stride=2)] = row
    halo_wait(send_vk)
    for i in range(-4, 20):
        vx[1, i + 5, 4:28] = vk[i + 5, 4:28] + p0[i // 2 + 2]
    half_sweep_0(0, -4, 20)
    half_sweep_0(1, -2, 18)
    half_sweep_0(0, -2, 18)
    half_sweep_0(1, 0, 16, 0, 16)
    for i in range(16):
        out[i, :, :128], out[i, :, 128:] = join(vx[0, i + 5, 8:24], vx[1, i + 5, 8:24], i & 1)
    for copies in (send_k, send_v, send_k1, send_s1, send_vk, send_vk1):
        halo_sent(copies)
    for copy in tree_y + tree_x + tree_z + tree_core + share_s:
        copy.wait_send()
    for x in range(4):
        landed(x, 0)


def v_cycle(image, conduct):
    def vmem(*shape):
        return pltpu.VMEM(shape, F32)

    frame0, frame1, gathered = (26, 32, 128), (12, 40, 128), (2, 4, 4, 48, 128)
    return pl.pallas_call(
        kernel,
        out_shape=jax.ShapeDtypeStruct((16, 16, 256), F32),
        in_specs=[pl.BlockSpec(memory_space=pltpu.HBM)] * 2,
        out_specs=pl.BlockSpec(memory_space=pltpu.VMEM),
        scratch_shapes=[
            vmem(16, 16, 256), vmem(16, 16, 256),
            vmem(2, *frame0), vmem(2, *frame0), vmem(2, 16, 16, 128), vmem(*frame0), vmem(2, 6, 24, 24, 128),
            vmem(2, 24, 24, 128), vmem(2, 24, 24, 128), vmem(8, 16, 128), vmem(12, 24, 128),
            vmem(2, *frame1), vmem(2, *frame1), vmem(2, *frame1), vmem(*frame1), vmem(2, 6, 10, 24, 128),
            vmem(2, 10, 24, 128), vmem(2, 10, 24, 128), vmem(2, 10, 24, 128), vmem(4, 8, 128), vmem(10, 32, 128),
            vmem(10, 2, 8, 128), vmem(2, 2, 2, 2, 128), vmem(*gathered), vmem(*gathered), vmem(2, 20, 48, 128),
            vmem(2, 6, 16, 32, 128), vmem(2, 16, 32, 128), vmem(2, 16, 32, 128), vmem(2, 16, 32, 128), vmem(16, 32, 128),
            vmem(16, 32, 128),
            vmem(2, 10, 32, 128), vmem(2, 10, 32, 128), vmem(2, 6, 8, 16, 128), vmem(2, 8, 16, 128),
            vmem(2, 8, 16, 128), vmem(16, 8, 128),
            pltpu.SemaphoreType.DMA((6, 2, 12)), pltpu.SemaphoreType.DMA((8, 2)), pltpu.SemaphoreType.DMA((10, 2)),
            pltpu.SemaphoreType.DMA((2,)),
        ],
        compiler_params=pltpu.CompilerParams(
            collective_id=0, has_side_effects=True, vmem_limit_bytes=48 * 2**20
        ),
        name="v_cycle",
    )(image, conduct)


def solution(mesh):
    return jax.shard_map(
        v_cycle,
        mesh=mesh,
        in_specs=(P("gx", "gy", None), P("gx", "gy", None)),
        out_specs=P("gx", "gy", None),
        check_vma=False,
    )
```

```python
import jax
import jax.numpy as jnp
from jax import lax
from jax.experimental import pallas as pl
from jax.experimental.pallas import tpu as pltpu
from jax.sharding import PartitionSpec as P

COARSE_SWEEPS = 8
MESH = pl.DeviceIdType.MESH
F32 = jnp.float32
GX, GY = 8, 16
DIRECTIONS = [(-1, -1), (-1, 1), (1, -1), (1, 1), (0, -1), (0, 1), (-1, 0), (1, 0)]
CHIPS = sorted(
    [(x, y, z) for x in range(4) for y in range(4) for z in range(4) if (x, y, z) != (0, 0, 0)],
    key=lambda d: -sum(min(c, 4 - c) for c in d),
)


def iota(shape, dim):
    return lax.broadcasted_iota(jnp.int32, shape, dim)


def roll(values, shift):
    return pltpu.roll(values, shift % 128, values.ndim - 1)


def halo_copies(src, src_origin, dst, origin, extent, widths, sems, position, corners=None):
    gx, gy = position
    lead = (slice(None),) * (len(dst.shape) - 3)

    def piece(step, size, here, there, start, stop):
        if step == 0:
            return slice(here, here + size), slice(there, there + size)
        if step > 0:
            return slice(here + size - stop, here + size - start), slice(there - stop, there - start)
        return slice(here + start, here + stop), slice(there + size + start, there + size + stop)

    copies, index = [], 0
    for dx, dy in DIRECTIONS:
        boxes = [((0, widths[0]), (0, widths[1]))]
        if dx and dy and corners is not None:
            boxes = [((start, stop), (0, width)) for start, stop, width in corners]
        group = []
        for box_x, box_y in boxes:
            src_x, dst_x = piece(dx, extent[0], src_origin[0], origin[0], *box_x)
            src_y, dst_y = piece(dy, extent[1], src_origin[1], origin[1], *box_y)
            group.append(
                pltpu.make_async_remote_copy(
                    src_ref=src.at[lead + (src_x, src_y)],
                    dst_ref=dst.at[lead + (dst_x, dst_y)],
                    send_sem=sems.at[0, index],
                    recv_sem=sems.at[1, index],
                    device_id=(lax.rem(gx + dx + GX, GX), lax.rem(gy + dy + GY, GY)),
                    device_id_type=MESH,
                )
            )
            index += 1
        copies.append((in_grid(gx + dx, gy + dy), in_grid(gx - dx, gy - dy), group))
    return copies


def in_grid(x, y):
    return (x >= 0) & (x < GX) & (y >= 0) & (y < GY)


def halo_start(copies):
    for sends, _, group in copies:

        @pl.when(sends)
        def _():
            for copy in group:
                copy.start()


def halo_wait(copies):
    for _, receives, group in copies:

        @pl.when(receives)
        def _():
            for copy in group:
                copy.wait_recv()


def halo_sent(copies):
    for sends, _, group in copies:

        @pl.when(sends)
        def _():
            for copy in group:
                copy.wait_send()


def couple(here, same, cross, low, high, other, weights, z_step):
    w, w_cross, w_low, w_high, w_below, w_above = weights
    parts = [
        (here + same) * w,
        (here + cross) * w_cross,
        (here + low) * w_low,
        (here + high) * w_high,
        (here + roll(other, z_step)) * w_below,
        (here + roll(other, -z_step)) * w_above,
    ]
    total = ((parts[0] + parts[1]) + (parts[2] + parts[3])) + ((parts[4] + parts[5]) + 1.0)
    inverse = 1.0 / total
    return [part * inverse for part in parts], total, inverse


def relax(source, couplings, same, cross, low, high, z_step):
    acc0 = source + couplings[0] * same
    acc1 = couplings[4] * roll(same, z_step) + couplings[5] * roll(same, -z_step)
    acc2 = couplings[2] * low + couplings[3] * high
    return (acc0 + acc2) + (acc1 + couplings[1] * cross)


def kernel(
    image, conduct, out,
    image_in, conduct_in, kx, vx, vs, vk, c0, s0, d0, t0, p0,
    k1, s1x, v1, vk1, c1, s1, i1, d1, t1, p1,
    q1, own2, kg, sg, v2, c2, s2, i2, d2, t2, p2,
    k3, v3, c3, s3, i3, dummy,
    halo_sems, gather_sems, tree_sems, in_sems, known_sems,
):
    gx, gy = lax.axis_index("gx"), lax.axis_index("gy")
    chip_x, core = gx // 2, lax.rem(gx, 2)
    chip_z, chip_y = gy // 4, lax.rem(gy, 4)
    sibling = (chip_x * 2 + 1 - core, gy)
    chips = [
        (lax.rem(chip_x + x, 4) * 2 + core, lax.rem(chip_z + z, 4) * 4 + lax.rem(chip_y + y, 4))
        for x, y, z in CHIPS
    ]
    position = (gx, gy)
    barrier = pltpu.get_barrier_semaphore()

    def ring(step):
        offsets = sorted({((step * x) % GX, (step * y) % GY) for x, y in DIRECTIONS})
        return [(lax.rem(gx + x, GX), lax.rem(gy + y, GY)) for x, y in offsets]

    def tell(n):
        for peer in ring(1 << n):
            pl.semaphore_signal(known_sems.at[n], inc=1, device_id=peer, device_id_type=MESH)

    def hear(n):
        pl.semaphore_wait(known_sems.at[n], len(ring(1 << n)))

    for peer in ring(1):
        pl.semaphore_signal(barrier, inc=1, device_id=peer, device_id_type=MESH)
    fetch_k = pltpu.make_async_copy(conduct, conduct_in, in_sems.at[0])
    fetch_v = pltpu.make_async_copy(image, image_in, in_sems.at[1])
    fetch_k.start()
    fetch_v.start()

    lane0 = iota((16, 128), 1)
    odd_row = iota((16, 128), 0) & 1
    low0 = lane0 < 64
    half_lane = (lane0 & 63) * 2

    def split(values, par):
        parity = odd_row ^ par
        first = half_lane + jnp.where(low0, parity, 1 - parity)
        second = half_lane + jnp.where(low0, 1 - parity, parity)
        left = jnp.take_along_axis(values[:, :128], first, axis=1)
        right = jnp.take_along_axis(values[:, 128:], second, axis=1)
        return jnp.where(low0, left, right), roll(jnp.where(low0, right, left), 64)

    def join(red, black, par):
        parity = odd_row ^ par
        turned = roll(black, 64)
        left, right = jnp.where(low0, red, turned), jnp.where(low0, turned, red)
        same = (lane0 & 1) == parity
        half = lane0 >> 1
        first = half + jnp.where(same, 0, 64)
        second = half + jnp.where(same, 64, 0)
        return jnp.take_along_axis(left, first, axis=1), jnp.take_along_axis(right, second, axis=1)
    nothing = jnp.zeros((2, 4, 4, 8, 128), F32)
    kg[:, :, :, 0:8], kg[:, :, :, 40:48] = nothing, nothing
    nothing = jnp.zeros((2, 20, 8, 128), F32)
    v2[:, :, 0:8], v2[:, :, 40:48] = nothing, nothing
    nothing = jnp.zeros((2, 2, 48, 128), F32)
    v2[:, 0:2], v2[:, 18:20] = nothing, nothing
    for ref in (k3, v3):
        nothing = jnp.zeros((2, 10, 8, 128), F32)
        ref[:, :, 0:8], ref[:, :, 24:32] = nothing, nothing
        nothing = jnp.zeros((2, 1, 32, 128), F32)
        ref[:, 0:1], ref[:, 9:10] = nothing, nothing

    def zero(ref, *at):
        at = (slice(None),) * (len(ref.shape) - 3) + at
        ref[at] = jnp.zeros(ref.at[at].shape, F32)

    for edge, rows0, rows1 in ((gx == 0, slice(0, 5), slice(0, 4)), (gx == GX - 1, slice(21, 26), slice(8, 12))):

        @pl.when(edge)
        def _():
            for ref in (kx, vx, vk):
                zero(ref, rows0)
            for ref in (k1, s1x, vk1):
                zero(ref, rows1)

    for edge, cols0, cols1 in ((gy == 0, slice(0, 8), slice(8, 16)), (gy == GY - 1, slice(24, 32), slice(24, 32))):

        @pl.when(edge)
        def _():
            for ref in (kx, vx, vk):
                zero(ref, slice(None), cols0)
            for ref in (k1, s1x, vk1):
                zero(ref, slice(None), cols1)

    fetch_k.wait()
    for i in range(16):
        kx[0, i + 5, 8:24], kx[1, i + 5, 8:24] = split(conduct_in[i], i & 1)
    pl.semaphore_wait(barrier, len(ring(1)))
    cone = [(0, 2, 4), (2, 4, 2)]
    send_k = halo_copies(kx, (5, 8), kx, (5, 8), (16, 16), (5, 5), halo_sems.at[0], position, cone)
    send_v = halo_copies(vs, (0, 0), vx, (5, 8), (16, 16), (5, 5), halo_sems.at[1], position, cone)
    halo_start(send_k)
    tell(0)
    fetch_v.wait()
    for i in range(16):
        red, black = split(image_in[i], i & 1)
        vx[0, i + 5, 8:24], vx[1, i + 5, 8:24] = red, black
        vs[0, i], vs[1, i] = red, black
    halo_start(send_v)
    def block_mean():
        return [0.125 * (t0[i, pl.ds(0, 8, stride=2)] + t0[i, pl.ds(1, 8, stride=2)]) for i in range(8)]

    odd_8 = ((iota((8, 128), 0) + iota((8, 128), 1)) & 1) == 1
    odd_2 = ((iota((2, 128), 0) + iota((2, 128), 1)) & 1) == 1
    low_2 = iota((2, 128), 1) < 64
    even_lane = (iota((8, 128), 1) & 63) * 2

    def merge(first, second, odd):
        return jnp.where(odd, second, first), jnp.where(odd, first, second)

    def level_2_share(kind, pairs, whole):
        rows = []
        for i in range(4):
            t1[i] = jnp.take_along_axis(pairs[i], even_lane, axis=1) + jnp.take_along_axis(pairs[i], even_lane + 1, axis=1)
        for i in range(4):
            first = t1[i, pl.ds(0, 2, stride=2)] + t1[i, pl.ds(1, 2, stride=2)]
            second = t1[i, pl.ds(4, 2, stride=2)] + t1[i, pl.ds(5, 2, stride=2)]
            rows.append(0.125 * jnp.where(low_2, first, second))
        for a in range(2):
            cells = merge(rows[2 * a], rows[2 * a + 1], odd_2)
            for colour in (0, 1):
                own2[kind, colour, a] = cells[colour]
                whole[colour, chip_x, 2 * core + a, pl.ds(8 + 2 * gy, 2)] = cells[colour]

    def remote(src, dst, sems, device):
        return pltpu.make_async_remote_copy(
            src_ref=src, dst_ref=dst, send_sem=sems.at[0], recv_sem=sems.at[1], device_id=device, device_id_type=MESH
        )

    cores_rows = pl.ds(2 * core, 2)
    own_place = (slice(None), chip_x, cores_rows, pl.ds(8 + 2 * gy, 2))

    spread_s = [
        remote(own2.at[1], sg.at[own_place], gather_sems.at[x], chip) for chip, (x, _, _) in zip(chips, CHIPS)
    ]
    planes = [sg.at[:, lax.rem(chip_x + 4 - x, 4), cores_rows, 8:40] for x in range(4)]
    share_s = [remote(plane, plane, gather_sems.at[4 + x], sibling) for x, plane in enumerate(planes)]

    def landed(x, which):
        some = dummy.at[0:15] if x == 0 else dummy
        pltpu.make_async_copy(some, some, gather_sems.at[x, which]).wait()

    def chip_at(x, y, z):
        return (
            lax.rem(chip_x + x, 4) * 2 + core,
            lax.rem(chip_z + z, 4) * 4 + lax.rem(chip_y + y, 4),
        )

    sheet = kg.at[:, :, cores_rows, pl.ds(8 + 8 * chip_z, 8)]
    half = kg.at[:, :, cores_rows, 8:40]
    tree_xy = [
        remote(own2.at[0], kg.at[own_place], tree_sems.at[n], chip_at(x, y, 0))
        for n, (x, y) in enumerate((x, y) for x in range(4) for y in range(4) if x or y)
    ]
    tree_z = [remote(sheet, sheet, tree_sems.at[n + 14], chip_at(0, 0, n)) for n in (2, 1, 3)]
    tree_core = [remote(half, half, tree_sems.at[18], sibling)]

    for i in range(8):
        e = 2 * i + 5
        t0[i] = (kx[0, e, 8:24] + kx[1, e, 8:24]) + (kx[0, e + 1, 8:24] + kx[1, e + 1, 8:24])
    rows = block_mean()
    for a in range(4):
        k1[0, a + 4, 16:24], k1[1, a + 4, 16:24] = merge(rows[2 * a], rows[2 * a + 1], odd_8)
    level_2_share(0, [rows[2 * a] + rows[2 * a + 1] for a in range(4)], kg)
    send_k1 = halo_copies(k1, (4, 16), k1, (4, 16), (4, 8), (3, 6), halo_sems.at[2], position)
    halo_start(send_k1)

    shape = (2, 24, 128)
    sub, lanes = iota(shape, 1), iota(shape, 2)
    even_row = ((iota(shape, 0) + sub) & 1) == 0
    wy_low = jnp.where((sub == 4) & (gy == 0), 0.0, 0.5).astype(F32)
    wy_high = jnp.where((sub == 19) & (gy == GY - 1), 0.0, 0.5).astype(F32)
    wx_low = jnp.where(gx == 0, 0.0, 0.5).astype(F32)
    wx_high = jnp.where(gx == GX - 1, 0.0, 0.5).astype(F32)
    wz = [
        jnp.where(even_row, jnp.where(lanes == 0, 0.0, 0.5), jnp.where(lanes == 127, 0.0, 0.5)).astype(F32),
        jnp.where(even_row, jnp.where(lanes == 127, 0.0, 0.5), jnp.where(lanes == 0, 0.0, 0.5)).astype(F32),
    ]

    def beside(values, colour, rows_even):
        below, above = roll(values, 1), roll(values, -1)
        return jnp.where(rows_even, below, above) if colour == 0 else jnp.where(rows_even, above, below)

    row_index = iota((2, 1, 1), 0)

    def couplings_0(colour, start, stop):
        for i in range(start, stop, 2):
            e = i + 5
            here, other = kx[colour, e:e + 2, 4:28], kx[1 - colour, e:e + 2, 4:28]
            wx_l = jnp.where(row_index == 0, wx_low, 0.5) if i == 0 else 0.5
            wx_h = jnp.where(row_index == 1, wx_high, 0.5) if i == 14 else 0.5
            parts = [
                (here + kx[1 - colour, e - 1:e + 1, 4:28]) * wx_l,
                (here + kx[1 - colour, e + 1:e + 3, 4:28]) * wx_h,
                (here + kx[1 - colour, e:e + 2, 3:27]) * wy_low,
                (here + kx[1 - colour, e:e + 2, 5:29]) * wy_high,
                (here + other) * 0.5,
                (here + beside(other, colour, even_row)) * wz[colour],
            ]
            total = ((parts[0] + parts[1]) + (parts[2] + parts[3])) + ((parts[4] + parts[5]) + 1.0)
            inverse = 1.0 / total
            d0[colour, i + 4:i + 6] = total
            s0[colour, i + 4:i + 6] = inverse
            for n in range(6):
                c0[colour, n, i + 4:i + 6] = parts[n] * inverse

    def update_0(colour, i, lo, hi, rows_even):
        e, f = i + 5, i + 4
        a, b = lo + 8, hi + 8
        here = slice(lo + 4, hi + 4)
        other = vx[1 - colour, e:e + 2, a:b]
        acc0 = s0[colour, f:f + 2, here] + c0[colour, 0, f:f + 2, here] * vx[1 - colour, e - 1:e + 1, a:b]
        acc1 = c0[colour, 1, f:f + 2, here] * vx[1 - colour, e + 1:e + 3, a:b]
        acc1 += c0[colour, 2, f:f + 2, here] * vx[1 - colour, e:e + 2, a - 1:b - 1]
        acc2 = c0[colour, 3, f:f + 2, here] * vx[1 - colour, e:e + 2, a + 1:b + 1]
        acc2 += c0[colour, 4, f:f + 2, here] * other
        acc3 = c0[colour, 5, f:f + 2, here] * beside(other, colour, rows_even)
        return (acc0 + acc1) + (acc2 + acc3)

    own_even = ((iota((2, 16, 128), 0) + iota((2, 16, 128), 1)) & 1) == 0

    def half_sweep_0(colour, start, stop, lo=-4, hi=20):
        rows_even = even_row if hi - lo == 24 else own_even
        for i in range(start, stop, 2):
            vx[colour, i + 5:i + 7, lo + 8:hi + 8] = update_0(colour, i, lo, hi, rows_even)
    hear(0)
    tell(1)
    halo_wait(send_k)
    couplings_0(0, -4, 20)
    couplings_0(1, -4, 20)
    hear(1)
    tell(2)
    for copy in tree_xy:
        copy.start()
    halo_wait(send_v)
    for colour in (0, 1):
        for i in range(-4, 20, 2):
            s0[colour, i + 4:i + 6] = s0[colour, i + 4:i + 6] * vx[colour, i + 5:i + 7, 4:28]

    half_sweep_0(0, -4, 20)
    half_sweep_0(1, -4, 20)
    half_sweep_0(0, -2, 18)
    half_sweep_0(1, -2, 18)
    def residual_0(i):
        total = None
        for colour in (0, 1):
            left = update_0(colour, i, 0, 16, own_even) - vx[colour, i + 5:i + 7, 8:24]
            left = d0[colour, i + 4:i + 6, 4:20] * left
            total = left if total is None else total + left
        return total

    for i in range(8):
        both = residual_0(2 * i)
        t0[i] = both[0] + both[1]
    rows = block_mean()
    for a in range(4):
        s1x[0, a + 4, 16:24], s1x[1, a + 4, 16:24] = merge(rows[2 * a], rows[2 * a + 1], odd_8)
    send_s1 = halo_copies(s1x, (4, 16), s1x, (4, 16), (4, 8), (3, 5), halo_sems.at[3], position)
    halo_start(send_s1)

    vk[5:21, 8:24] = vx[1, 5:21, 8:24]
    send_vk = halo_copies(vk, (5, 8), vk, (5, 8), (16, 16), (4, 4), halo_sems.at[4], position)
    halo_start(send_vk)

    shape = (24, 128)
    col, lanes = iota(shape, 0) - 6, iota(shape, 1)
    w1 = 0.5 / 4.0
    wy_low = jnp.where((col == 0) & (gy == 0), 0.0, w1).astype(F32)
    wy_high = jnp.where((col == 7) & (gy == GY - 1), 0.0, w1).astype(F32)
    wx_low = jnp.where(gx == 0, 0.0, w1).astype(F32)
    wx_high = jnp.where(gx == GX - 1, 0.0, w1).astype(F32)
    wz_low = jnp.where(lanes == 0, 0.0, w1).astype(F32)
    wz_high = jnp.where(lanes == 127, 0.0, w1).astype(F32)

    def first_of_pair(size, origin):
        odd = (iota((size, 128), 0) + iota((size, 128), 1) + origin) & 1
        return odd == 0, odd == 1

    first_24, first_16, first_8 = first_of_pair(24, 0), first_of_pair(16, 0), first_of_pair(8, 0)
    halo_wait(send_k1)
    for colour in (0, 1):
        for a in range(-3, 7):
            e, f = a + 4, a + 3
            other = k1[1 - colour, e, 10:34]
            first = first_24[colour]
            w_cross = w1
            if a in (0, 3):
                w_cross = jnp.where(first, wx_low if a == 0 else w1, wx_high if a == 3 else w1)
            parts, total, inverse = couple(
                k1[colour, e, 10:34], other, jnp.where(first, k1[1 - colour, e - 1, 10:34], k1[1 - colour, e + 1, 10:34]),
                k1[1 - colour, e, 9:33], k1[1 - colour, e, 11:35], other, (w1, w_cross, wy_low, wy_high, wz_low, wz_high), 1,
            )
            d1[colour, f] = total
            i1[colour, f] = inverse
            for n in range(6):
                c1[colour, n, f] = parts[n]

    def update_1(colour, a, lo, hi):
        e, f = a + 4, a + 3
        here, at = slice(lo + 6, hi + 6), slice(lo + 16, hi + 16)
        first = {24: first_24, 16: first_16, 8: first_8}[hi - lo][colour]
        return relax(
            s1[colour, f, here], [c1[colour, n, f, here] for n in range(6)], v1[1 - colour, e, at],
            jnp.where(first, v1[1 - colour, e - 1, at], v1[1 - colour, e + 1, at]),
            v1[1 - colour, e, lo + 15:hi + 15], v1[1 - colour, e, lo + 17:hi + 17], 1,
        )

    def half_sweep_1(colour, start, stop, lo, hi):
        for a in range(start, stop):
            v1[colour, a + 4, lo + 16:hi + 16] = update_1(colour, a, lo, hi)
    hear(2)
    for copy in tree_xy:
        copy.wait_recv()
    for copy in tree_z:
        copy.start()

    halo_wait(send_s1)
    for colour in (0, 1):
        for a in range(-3, 7):
            s1[colour, a + 3] = i1[colour, a + 3] * s1x[colour, a + 4, 10:34]
    for a in range(-2, 6):
        v1[0, a + 4, 12:28] = s1[0, a + 3, 2:18]
    half_sweep_1(1, -2, 6, -4, 12)
    half_sweep_1(0, -1, 5, -4, 12)
    half_sweep_1(1, -1, 5, -4, 12)
    pairs = []
    for a in range(4):
        left = [d1[n, a + 3, 6:14] * (update_1(n, a, 0, 8) - v1[n, a + 4, 16:24]) for n in (0, 1)]
        pairs.append(left[0] + left[1])
    level_2_share(1, pairs, sg)
    for copy in spread_s:
        copy.start()
    for copy in tree_z:
        copy.wait_recv()
    tree_core[0].start()
    vk1[4:8, 16:24] = v1[1, 4:8, 16:24]
    send_vk1 = halo_copies(vk1, (4, 16), vk1, (4, 16), (4, 8), (3, 6), halo_sems.at[5], position)
    halo_start(send_vk1)

    tree_core[0].wait_recv()
    def two_columns(size):
        return iota((size, 128), 1) < 64, (iota((size, 128), 0) & 1) == 1

    def beside_2(row_low, row_high, low, odd):
        turned = roll(jnp.where(low, row_high, row_low), 64)
        return jnp.where(odd, row_low, turned), jnp.where(odd, turned, row_high)

    lane = iota((32, 128), 1)
    place = lane & 63
    j_row = iota((32, 128), 0)
    low_32, odd_32 = two_columns(32)
    first_32 = first_of_pair(32, 0)
    w2 = 0.5 / 16.0
    wy_low = jnp.where((j_row == 0) & low_32, 0.0, w2).astype(F32)
    wy_high = jnp.where((j_row == 31) & (lane >= 64), 0.0, w2).astype(F32)
    wz_low = jnp.where(place == 0, 0.0, w2).astype(F32)
    wz_high = jnp.where(place == 63, 0.0, w2).astype(F32)

    def kg_rows(colour, a, at):
        return kg[colour, a // 4, a % 4, at]

    at = slice(8, 40)
    for colour in (0, 1):
        for a in range(16):
            other = kg_rows(1 - colour, a, at)
            before = kg_rows(1 - colour, max(a - 1, 0), at)
            after = kg_rows(1 - colour, min(a + 1, 15), at)
            w_cross = w2
            if a == 0:
                w_cross = jnp.where(first_32[colour], 0.0, w2).astype(F32)
            if a == 15:
                w_cross = jnp.where(first_32[colour], w2, 0.0).astype(F32)
            low, high = beside_2(
                kg_rows(1 - colour, a, slice(7, 39)), kg_rows(1 - colour, a, slice(9, 41)), low_32, odd_32
            )
            parts, total, inverse = couple(
                kg_rows(colour, a, at), other, jnp.where(first_32[colour], before, after), low, high, other,
                (w2, w_cross, wy_low, wy_high, wz_low, wz_high), 1,
            )
            d2[colour, a] = total
            i2[colour, a] = inverse
            for n in range(6):
                c2[colour, n, a] = parts[n]
    lane3 = iota((16, 128), 1)
    even_place = (lane3 & 1) == 0
    place3 = (lane3 & 63) >> 1
    row3 = iota((16, 128), 0)
    low3 = lane3 < 64
    odd3 = (((lane3 >> 6) + place3) & 1) == 1
    first3 = (jnp.logical_not(odd3), odd3)

    def level_3_share(p, pairs):
        rows = []
        for n in range(2):
            t2[2 * p + n] = pairs[n]
        for n in range(2):
            row = t2[2 * p + n, pl.ds(0, 16, stride=2)] + t2[2 * p + n, pl.ds(1, 16, stride=2)]
            rows.append(0.125 * (row + jnp.where(even_place, roll(row, -1), roll(row, 1))))
        return merge(rows[0], rows[1], odd3)

    w3 = 0.5 / 64.0
    wy_low = jnp.where((row3 == 0) & low3, 0.0, w3).astype(F32)
    wy_high = jnp.where((row3 == 15) & (lane3 >= 64), 0.0, w3).astype(F32)
    wz_low = jnp.where(place3 == 0, 0.0, w3).astype(F32)
    wz_high = jnp.where(place3 == 31, 0.0, w3).astype(F32)
    at3 = slice(8, 24)

    def around_3(ref, colour, p, first):
        here = ref[colour, p + 1, at3]
        cross = jnp.where(first, ref[colour, p, at3], ref[colour, p + 2, at3])
        low = roll(jnp.where(low3, here, ref[colour, p + 1, 7:23]), 64)
        high = roll(jnp.where(low3, ref[colour, p + 1, 9:25], here), 64)
        return here, cross, low, high

    for p in range(8):
        pairs = [kg_rows(0, a, at) + kg_rows(1, a, at) for a in (2 * p, 2 * p + 1)]
        k3[0, p + 1, at3], k3[1, p + 1, at3] = level_3_share(p, pairs)
    for colour in (0, 1):
        for p in range(8):
            here, cross, low, high = around_3(k3, 1 - colour, p, first3[colour])
            w_cross = w3
            if p == 0:
                w_cross = jnp.where(first3[colour], 0.0, w3).astype(F32)
            if p == 7:
                w_cross = jnp.where(first3[colour], w3, 0.0).astype(F32)
            parts, _, inverse = couple(
                k3[colour, p + 1, at3], here, cross, low, high, here, (w3, w_cross, wy_low, wy_high, wz_low, wz_high), 2
            )
            i3[colour, p] = inverse
            for n in range(6):
                c3[colour, n, p] = parts[n]
    for x in (0, 1, 3, 2):
        landed(x, 1)
        share_s[x].start()
    for copy in share_s:
        copy.wait_recv()

    for colour in (0, 1):
        for a in range(16):
            source = i2[colour, a] * sg[colour, a // 4, a % 4, at]
            s2[colour, a] = source
            if colour == 0:
                v2[0, a + 2, at] = source

    def update_2(colour, a, rows, frame_rows, low, odd, first):
        before, here, after = frame_rows
        row_low, row_high = beside_2(v2[1 - colour, a + 2, before], v2[1 - colour, a + 2, after], low, odd)
        cross = jnp.where(first[colour], v2[1 - colour, a + 1, here], v2[1 - colour, a + 3, here])
        return relax(
            s2[colour, a, rows], [c2[colour, n, a, rows] for n in range(6)], v2[1 - colour, a + 2, here],
            cross, row_low, row_high, 1,
        )

    whole_2 = (slice(0, 32), (slice(7, 39), at, slice(9, 41)), low_32, odd_32, first_32)

    def half_sweep_2(colour):
        for a in range(16):
            v2[colour, a + 2, at] = update_2(colour, a, *whole_2)

    half_sweep_2(1)
    half_sweep_2(0)
    half_sweep_2(1)
    for p in range(8):
        pairs = []
        for a in (2 * p, 2 * p + 1):
            left = [d2[n, a] * (update_2(n, a, *whole_2) - v2[n, a + 2, at]) for n in (0, 1)]
            pairs.append(left[0] + left[1])
        sources = level_3_share(p, pairs)
        for colour in (0, 1):
            s3[colour, p] = i3[colour, p] * sources[colour]

    def half_sweep_3(colour):
        for p in range(8):
            here, cross, low, high = around_3(v3, 1 - colour, p, first3[colour])
            v3[colour, p + 1, at3] = relax(
                s3[colour, p], [c3[colour, n, p] for n in range(6)], here, cross, low, high, 2
            )

    for p in range(8):
        v3[0, p + 1, at3] = s3[0, p]
    half_sweep_3(1)
    for _ in range(COARSE_SWEEPS - 1):
        half_sweep_3(0)
        half_sweep_3(1)

    for p in range(8):
        red, black = v3[0, p + 1, at3], v3[1, p + 1, at3]
        for n, row in enumerate((jnp.where(odd3, black, red), jnp.where(odd3, red, black))):
            p2[2 * p + n, pl.ds(0, 16, stride=2)] = row
            p2[2 * p + n, pl.ds(1, 16, stride=2)] = row

    def within(value, top, span):
        value = value * ((value + span) // span)
        value = top - value
        return top - value * ((value + span) // span)

    a0 = 2 * within(gx - 2, 3, 8)
    r0 = 2 * within(gy - 2, 8, 16)
    strip = pl.ds(r0, 16)
    part_2 = (strip, (pl.ds(r0 + 7, 16), pl.ds(r0 + 8, 16), pl.ds(r0 + 9, 16)), *two_columns(16), first_16)
    for n in range(10):
        v2[1, a0 + n + 2, pl.ds(r0 + 8, 16)] = v2[1, a0 + n + 2, pl.ds(r0 + 8, 16)] + p2[a0 + n, strip]
    for colour in (0, 1, 0, 1):
        news = [update_2(colour, a0 + n, *part_2) for n in range(10)]
        for n, new in enumerate(news):
            v2[colour, a0 + n + 2, pl.ds(r0 + 8, 16)] = new

    spot = iota((8, 128), 1) >> 1
    for d in range(-3, 7):
        cells = (2 * gx + d // 2 + 2, pl.ds(2 * gy + 6, 8))
        coarse = jnp.where(odd_8 == (d % 2 == 1), v2[(0,) + cells], v2[(1,) + cells])
        q1[d + 3, 0] = jnp.take_along_axis(coarse, spot, axis=1)
        q1[d + 3, 1] = jnp.take_along_axis(coarse, spot + 64, axis=1)
    for d in range(10):
        for n in range(2):
            for m in range(2):
                column = q1[d, n, pl.ds(m, 4, stride=2)]
                p1[d, pl.ds(4 * n + 2 * m, 4, stride=8)] = column
                p1[d, pl.ds(4 * n + 2 * m + 1, 4, stride=8)] = column
    halo_wait(send_vk1)
    for a in range(-3, 7):
        v1[1, a + 4, 10:30] = vk1[a + 4, 10:30] + p1[a + 3, 2:22]
    half_sweep_1(0, -3, 7, -6, 18)
    half_sweep_1(1, -2, 6, -4, 12)
    half_sweep_1(0, -2, 6, -4, 12)
    half_sweep_1(1, -1, 5, -4, 12)

    odd_12 = (iota((12, 128), 0) + iota((12, 128), 1)) & 1
    for i in range(-2, 10):
        a = i // 2
        row = jnp.where(odd_12 == i % 2, v1[0, a + 4, 14:26], v1[1, a + 4, 14:26])
        p0[i + 2, pl.ds(0, 12, stride=2)] = row
        p0[i + 2, pl.ds(1, 12, stride=2)] = row
    halo_wait(send_vk)
    for i in range(-4, 20):
        vx[1, i + 5, 4:28] = vk[i + 5, 4:28] + p0[i // 2 + 2]
    half_sweep_0(0, -4, 20)
    half_sweep_0(1, -2, 18)
    half_sweep_0(0, -2, 18)
    half_sweep_0(1, 0, 16, 0, 16)
    for i in range(16):
        out[i, :, :128], out[i, :, 128:] = join(vx[0, i + 5, 8:24], vx[1, i + 5, 8:24], i & 1)
    for copies in (send_k, send_v, send_k1, send_s1, send_vk, send_vk1):
        halo_sent(copies)
    for copy in tree_xy + tree_z + tree_core + share_s:
        copy.wait_send()
    for x in range(4):
        landed(x, 0)


def v_cycle(image, conduct):
    def vmem(*shape):
        return pltpu.VMEM(shape, F32)

    frame0, frame1, gathered = (26, 32, 128), (12, 40, 128), (2, 4, 4, 48, 128)
    return pl.pallas_call(
        kernel,
        out_shape=jax.ShapeDtypeStruct((16, 16, 256), F32),
        in_specs=[pl.BlockSpec(memory_space=pltpu.HBM)] * 2,
        out_specs=pl.BlockSpec(memory_space=pltpu.VMEM),
        scratch_shapes=[
            vmem(16, 16, 256), vmem(16, 16, 256),
            vmem(2, *frame0), vmem(2, *frame0), vmem(2, 16, 16, 128), vmem(*frame0), vmem(2, 6, 24, 24, 128),
            vmem(2, 24, 24, 128), vmem(2, 24, 24, 128), vmem(8, 16, 128), vmem(12, 24, 128),
            vmem(2, *frame1), vmem(2, *frame1), vmem(2, *frame1), vmem(*frame1), vmem(2, 6, 10, 24, 128),
            vmem(2, 10, 24, 128), vmem(2, 10, 24, 128), vmem(2, 10, 24, 128), vmem(4, 8, 128), vmem(10, 32, 128),
            vmem(10, 2, 8, 128), vmem(2, 2, 2, 2, 128), vmem(*gathered), vmem(*gathered), vmem(2, 20, 48, 128),
            vmem(2, 6, 16, 32, 128), vmem(2, 16, 32, 128), vmem(2, 16, 32, 128), vmem(2, 16, 32, 128), vmem(16, 32, 128),
            vmem(16, 32, 128),
            vmem(2, 10, 32, 128), vmem(2, 10, 32, 128), vmem(2, 6, 8, 16, 128), vmem(2, 8, 16, 128),
            vmem(2, 8, 16, 128), vmem(16, 8, 128),
            pltpu.SemaphoreType.DMA((6, 2, 12)), pltpu.SemaphoreType.DMA((8, 2)), pltpu.SemaphoreType.DMA((19, 2)),
            pltpu.SemaphoreType.DMA((2,)), pltpu.SemaphoreType.REGULAR((3,)),
        ],
        compiler_params=pltpu.CompilerParams(
            collective_id=0, has_side_effects=True, vmem_limit_bytes=48 * 2**20
        ),
        name="v_cycle",
    )(image, conduct)


def solution(mesh):
    return jax.shard_map(
        v_cycle,
        mesh=mesh,
        in_specs=(P("gx", "gy", None), P("gx", "gy", None)),
        out_specs=P("gx", "gy", None),
        check_vma=False,
    )
```

```python
import math

import jax
import jax.numpy as jnp
from jax import lax
from jax.experimental import pallas as pl
from jax.experimental.pallas import tpu as pltpu
from jax.sharding import PartitionSpec as P

COARSE_SWEEPS = 8
MESH = pl.DeviceIdType.MESH
F32 = jnp.float32
GX, GY = 8, 16
DIRECTIONS = [(-1, -1), (-1, 1), (1, -1), (1, 1), (0, -1), (0, 1), (-1, 0), (1, 0)]
CHIPS = sorted(
    [(x, y, z) for x in range(4) for y in range(4) for z in range(4) if (x, y, z) != (0, 0, 0)],
    key=lambda d: -sum(min(c, 4 - c) for c in d),
)


def nearness(offset):
    return max(min(offset[0], GX - offset[0]), min(offset[1], GY - offset[1]))


def iota(shape, dim):
    return lax.broadcasted_iota(jnp.int32, shape, dim)


def roll(values, shift):
    return pltpu.roll(values, shift % 128, values.ndim - 1)


def halo_copies(src, src_origin, dst, origin, extent, widths, sems, position, corners=None):
    gx, gy = position
    lead = (slice(None),) * (len(dst.shape) - 3)

    def piece(step, size, here, there, start, stop):
        if step == 0:
            return slice(here, here + size), slice(there, there + size)
        if step > 0:
            return slice(here + size - stop, here + size - start), slice(there - stop, there - start)
        return slice(here + start, here + stop), slice(there + size + start, there + size + stop)

    copies = []
    for dx, dy in DIRECTIONS:
        boxes = [((0, widths[0]), (0, widths[1]))]
        if dx and dy and corners is not None:
            boxes = [((start, stop), (0, width)) for start, stop, width in corners]
        group = []
        for box_x, box_y in boxes:
            src_x, dst_x = piece(dx, extent[0], src_origin[0], origin[0], *box_x)
            src_y, dst_y = piece(dy, extent[1], src_origin[1], origin[1], *box_y)
            group.append(
                pltpu.make_async_remote_copy(
                    src_ref=src.at[lead + (src_x, src_y)],
                    dst_ref=dst.at[lead + (dst_x, dst_y)],
                    send_sem=sems[0],
                    recv_sem=sems[1],
                    device_id=(lax.rem(gx + dx + GX, GX), lax.rem(gy + dy + GY, GY)),
                    device_id_type=MESH,
                )
            )
        copies.append((in_grid(gx + dx, gy + dy), group))
    return copies


def in_grid(x, y):
    return (x >= 0) & (x < GX) & (y >= 0) & (y < GY)


def halo_start(copies):
    for sends, group in copies:

        @pl.when(sends)
        def _():
            for copy in group:
                copy.start()


def rows_of(group):
    return sum(math.prod(copy.src_ref.shape[:-1]) for copy in group)


def wait_rows(rows, sem, room):
    pltpu.make_async_copy(room.at[0:rows], room.at[0:rows], sem).wait()


def halo_wait(exchanges, position, sem, room, more=0):
    edge_x = (position[0] == 0) | (position[0] == GX - 1)
    edge_y = (position[1] == 0) | (position[1] == GY - 1)
    rows = {direction: 0 for direction in DIRECTIONS}
    for copies in exchanges:
        for direction, (_, group) in zip(DIRECTIONS, copies):
            rows[direction] += rows_of(group)
    for at_x in (False, True):
        for at_y in (False, True):
            lost = [(dx, dy) for dx, dy in DIRECTIONS if (at_x and dx == 1) or (at_y and dy == 1)]
            total = more + sum(rows.values()) - sum(rows[direction] for direction in lost)

            @pl.when((edge_x == at_x) & (edge_y == at_y))
            def _():
                wait_rows(total, sem, room)


def couple(here, same, cross, low, high, other, weights, z_step):
    w, w_cross, w_low, w_high, w_below, w_above = weights
    parts = [
        (here + same) * w,
        (here + cross) * w_cross,
        (here + low) * w_low,
        (here + high) * w_high,
        (here + roll(other, z_step)) * w_below,
        (here + roll(other, -z_step)) * w_above,
    ]
    total = ((parts[0] + parts[1]) + (parts[2] + parts[3])) + ((parts[4] + parts[5]) + 1.0)
    inverse = 1.0 / total
    return [part * inverse for part in parts], total, inverse


def relax(source, couplings, same, cross, low, high, z_step):
    acc0 = source + couplings[0] * same
    acc1 = couplings[4] * roll(same, z_step) + couplings[5] * roll(same, -z_step)
    acc2 = couplings[2] * low + couplings[3] * high
    return (acc0 + acc2) + (acc1 + couplings[1] * cross)


def kernel(
    image, conduct, out,
    image_in, conduct_in, kx, vx, vs, vk, c0, s0, d0, t0, p0,
    k1, s1x, v1, vk1, c1, s1, i1, d1, t1, p1,
    q1, own2, kg, sg, v2, c2, s2, i2, d2, t2, p2,
    k3, v3, c3, s3, i3, dummy,
    sent, arrived, in_sems, known_sems,
):
    gx, gy = lax.axis_index("gx"), lax.axis_index("gy")
    chip_x, core = gx // 2, lax.rem(gx, 2)
    chip_z, chip_y = gy // 4, lax.rem(gy, 4)
    sibling = (chip_x * 2 + 1 - core, gy)
    chips = [
        (lax.rem(chip_x + x, 4) * 2 + core, lax.rem(chip_z + z, 4) * 4 + lax.rem(chip_y + y, 4))
        for x, y, z in CHIPS
    ]
    position = (gx, gy)

    barrier = pltpu.get_barrier_semaphore()

    fetch_k = pltpu.make_async_copy(conduct, conduct_in, in_sems.at[0])
    fetch_v = pltpu.make_async_copy(image, image_in, in_sems.at[1])
    fetch_k.start()
    fetch_v.start()

    def near(steps):
        offsets = sorted({(x % GX, y % GY) for x in steps for y in steps} - {(0, 0)}, key=nearness)
        return [(lax.rem(gx + x, GX), lax.rem(gy + y, GY)) for x, y in offsets]

    def tell(n):
        for peer in near((0, 2 << n, -2 << n)):
            pl.semaphore_signal(known_sems.at[n], inc=1, device_id=peer, device_id_type=MESH)

    def hear(n):
        pl.semaphore_wait(known_sems.at[n], len(near((0, 2 << n, -2 << n))))

    greeted = near(range(-2, 3))
    for peer in greeted:
        pl.semaphore_signal(barrier, inc=1, device_id=peer, device_id_type=MESH)

    lane0 = iota((16, 128), 1)
    odd_row = iota((16, 128), 0) & 1
    low0 = lane0 < 64
    half_lane = (lane0 & 63) * 2

    def split(values, par):
        parity = odd_row ^ par
        first = half_lane + jnp.where(low0, parity, 1 - parity)
        second = half_lane + jnp.where(low0, 1 - parity, parity)
        left = jnp.take_along_axis(values[:, :128], first, axis=1)
        right = jnp.take_along_axis(values[:, 128:], second, axis=1)
        return jnp.where(low0, left, right), roll(jnp.where(low0, right, left), 64)

    nothing = jnp.zeros((2, 4, 4, 8, 128), F32)
    kg[:, :, :, 0:8], kg[:, :, :, 40:48] = nothing, nothing
    nothing = jnp.zeros((2, 20, 8, 128), F32)
    v2[:, :, 0:8], v2[:, :, 40:48] = nothing, nothing
    nothing = jnp.zeros((2, 2, 48, 128), F32)
    v2[:, 0:2], v2[:, 18:20] = nothing, nothing
    nothing = jnp.zeros((2, 4, 8, 128), F32)
    for ref in (k3, v3):
        ref[:, :, 0:8], ref[:, :, 24:32] = nothing, nothing

    def zero(ref, *at):
        at = (slice(None),) * (len(ref.shape) - 3) + at
        ref[at] = jnp.zeros(ref.at[at].shape, F32)

    for edge, rows0, rows1 in ((gx == 0, slice(0, 5), slice(0, 4)), (gx == GX - 1, slice(21, 26), slice(8, 12))):

        @pl.when(edge)
        def _():
            for ref in (kx, vx, vk):
                zero(ref, rows0)
            for ref in (k1, s1x, vk1):
                zero(ref, rows1)

    for edge, cols0, cols1 in ((gy == 0, slice(0, 8), slice(8, 16)), (gy == GY - 1, slice(24, 32), slice(24, 32))):

        @pl.when(edge)
        def _():
            for ref in (kx, vx, vk):
                zero(ref, slice(None), cols0)
            for ref in (k1, s1x, vk1):
                zero(ref, slice(None), cols1)

    for i in range(16):
        if i == 0:
            fetch_k.wait()
        kx[0, i + 5, 8:24], kx[1, i + 5, 8:24] = split(conduct_in[i], i & 1)

    pl.semaphore_wait(barrier, len(greeted))
    cone = [(0, 2, 4), (2, 4, 2)]
    send_k = halo_copies(kx, (5, 8), kx, (5, 8), (16, 16), (5, 5), (sent.at[0], arrived.at[0]), position, cone)
    send_v = halo_copies(vs, (0, 0), vx, (5, 8), (16, 16), (5, 5), (sent.at[0], arrived.at[1]), position, cone)
    tell(0)
    halo_start(send_k)
    fetch_v.wait()
    for i in range(16):
        red, black = split(image_in[i], i & 1)
        vx[0, i + 5, 8:24], vx[1, i + 5, 8:24] = red, black
        vs[0, i], vs[1, i] = red, black
    halo_start(send_v)

    def block_mean():
        return [0.125 * (t0[i, pl.ds(0, 8, stride=2)] + t0[i, pl.ds(1, 8, stride=2)]) for i in range(8)]

    odd_8 = ((iota((8, 128), 0) + iota((8, 128), 1)) & 1) == 1
    odd_2 = ((iota((2, 128), 0) + iota((2, 128), 1)) & 1) == 1
    low_2 = iota((2, 128), 1) < 64
    even_lane = (iota((8, 128), 1) & 63) * 2

    def merge(first, second, odd):
        return jnp.where(odd, second, first), jnp.where(odd, first, second)

    def level_2_share(kind, pairs, whole):
        rows = []
        for i in range(4):
            t1[i] = jnp.take_along_axis(pairs[i], even_lane, axis=1) + jnp.take_along_axis(pairs[i], even_lane + 1, axis=1)
        for i in range(4):
            first = t1[i, pl.ds(0, 2, stride=2)] + t1[i, pl.ds(1, 2, stride=2)]
            second = t1[i, pl.ds(4, 2, stride=2)] + t1[i, pl.ds(5, 2, stride=2)]
            rows.append(0.125 * jnp.where(low_2, first, second))
        for a in range(2):
            cells = merge(rows[2 * a], rows[2 * a + 1], odd_2)
            for colour in (0, 1):
                own2[kind, colour, a] = cells[colour]
                whole[colour, chip_x, 2 * core + a, pl.ds(8 + 2 * gy, 2)] = cells[colour]

    def remote(src, dst, which, device):
        return pltpu.make_async_remote_copy(
            src_ref=src, dst_ref=dst, send_sem=sent.at[which // 9], recv_sem=arrived.at[which], device_id=device, device_id_type=MESH
        )

    cores_rows = pl.ds(2 * core, 2)
    own_place = (slice(None), chip_x, cores_rows, pl.ds(8 + 2 * gy, 2))

    spread_s = [
        remote(own2.at[1], sg.at[own_place], 9 + x, chip) for chip, (x, _, _) in zip(chips, CHIPS)
    ]
    planes = [sg.at[:, lax.rem(chip_x + 4 - x, 4), cores_rows, 8:40] for x in range(4)]
    share_s = [remote(plane, plane, 13, sibling) for plane in planes]

    def arrive(copies, which):
        wait_rows(rows_of(copies), arrived.at[which], dummy)

    def chip_at(x, y, z):
        return (
            lax.rem(chip_x + x, 4) * 2 + core,
            lax.rem(chip_z + z, 4) * 4 + lax.rem(chip_y + y, 4),
        )

    sheet = kg.at[:, :, cores_rows, pl.ds(8 + 8 * chip_z, 8)]
    half = kg.at[:, :, cores_rows, 8:40]
    tree_xy = [
        remote(own2.at[0], kg.at[own_place], 6, chip_at(x, y, 0))
        for x in range(4)
        for y in range(4)
        if x or y
    ]
    tree_z = [remote(sheet, sheet, 7, chip_at(0, 0, n)) for n in (2, 1, 3)]
    tree_core = [remote(half, half, 8, sibling)]

    for i in range(8):
        e = 2 * i + 5
        t0[i] = (kx[0, e, 8:24] + kx[1, e, 8:24]) + (kx[0, e + 1, 8:24] + kx[1, e + 1, 8:24])
    rows = block_mean()
    for a in range(4):
        k1[0, a + 4, 16:24], k1[1, a + 4, 16:24] = merge(rows[2 * a], rows[2 * a + 1], odd_8)
    level_2_share(0, [rows[2 * a] + rows[2 * a + 1] for a in range(4)], kg)
    send_k1 = halo_copies(k1, (4, 16), k1, (4, 16), (4, 8), (3, 6), (sent.at[0], arrived.at[2]), position)
    halo_start(send_k1)

    shape = (2, 24, 128)
    sub, lanes = iota(shape, 1), iota(shape, 2)
    even_row = ((iota(shape, 0) + sub) & 1) == 0
    wy_low = jnp.where((sub == 4) & (gy == 0), 0.0, 0.5).astype(F32)
    wy_high = jnp.where((sub == 19) & (gy == GY - 1), 0.0, 0.5).astype(F32)
    wx_low = jnp.where(gx == 0, 0.0, 0.5).astype(F32)
    wx_high = jnp.where(gx == GX - 1, 0.0, 0.5).astype(F32)
    wz = [
        jnp.where(even_row, jnp.where(lanes == 0, 0.0, 0.5), jnp.where(lanes == 127, 0.0, 0.5)).astype(F32),
        jnp.where(even_row, jnp.where(lanes == 127, 0.0, 0.5), jnp.where(lanes == 0, 0.0, 0.5)).astype(F32),
    ]

    def beside(values, colour, even):
        step = 1 if colour == 0 else -1
        first = roll(jnp.where(even, values[0], values[1]), step)
        second = roll(jnp.where(even, values[1], values[0]), -step)
        return jnp.stack([jnp.where(even, first, second), jnp.where(even, second, first)])

    even_24 = (iota((24, 128), 0) & 1) == 0
    even_16 = (iota((16, 128), 0) & 1) == 0

    row_index = iota((2, 1, 1), 0)

    def couplings_0(colour, start, stop):
        for i in range(start, stop, 2):
            e = i + 5
            here, other = kx[colour, e:e + 2, 4:28], kx[1 - colour, e:e + 2, 4:28]
            wx_l = jnp.where(row_index == 0, wx_low, 0.5) if i == 0 else 0.5
            wx_h = jnp.where(row_index == 1, wx_high, 0.5) if i == 14 else 0.5
            parts = [
                (here + kx[1 - colour, e - 1:e + 1, 4:28]) * wx_l,
                (here + kx[1 - colour, e + 1:e + 3, 4:28]) * wx_h,
                (here + kx[1 - colour, e:e + 2, 3:27]) * wy_low,
                (here + kx[1 - colour, e:e + 2, 5:29]) * wy_high,
                (here + other) * 0.5,
                (here + beside(other, colour, even_24)) * wz[colour],
            ]
            total = ((parts[0] + parts[1]) + (parts[2] + parts[3])) + ((parts[4] + parts[5]) + 1.0)
            inverse = 1.0 / total
            d0[colour, i + 4:i + 6] = total
            s0[colour, i + 4:i + 6] = inverse
            for n in range(6):
                c0[colour, n, i + 4:i + 6] = parts[n] * inverse

    def update_0(colour, i, lo, hi, rows_even):
        e, f = i + 5, i + 4
        a, b = lo + 8, hi + 8
        here = slice(lo + 4, hi + 4)
        other = vx[1 - colour, e:e + 2, a:b]
        acc0 = s0[colour, f:f + 2, here] + c0[colour, 0, f:f + 2, here] * vx[1 - colour, e - 1:e + 1, a:b]
        acc1 = c0[colour, 1, f:f + 2, here] * vx[1 - colour, e + 1:e + 3, a:b]
        acc1 += c0[colour, 2, f:f + 2, here] * vx[1 - colour, e:e + 2, a - 1:b - 1]
        acc2 = c0[colour, 3, f:f + 2, here] * vx[1 - colour, e:e + 2, a + 1:b + 1]
        acc2 += c0[colour, 4, f:f + 2, here] * other
        acc3 = c0[colour, 5, f:f + 2, here] * beside(other, colour, rows_even)
        return (acc0 + acc1) + (acc2 + acc3)

    def half_sweep_0(colour, start, stop, lo=-4, hi=20):
        rows_even = even_24 if hi - lo == 24 else even_16
        for i in range(start, stop, 2):
            vx[colour, i + 5:i + 7, lo + 8:hi + 8] = update_0(colour, i, lo, hi, rows_even)

    halo_wait([send_k], position, arrived.at[0], dummy)
    hear(0)
    tell(1)
    couplings_0(0, -4, 20)
    couplings_0(1, -4, 20)
    for copy in tree_xy:
        copy.start()
    halo_wait([send_v], position, arrived.at[1], dummy)
    for colour in (0, 1):
        for i in range(-4, 20, 2):
            s0[colour, i + 4:i + 6] = s0[colour, i + 4:i + 6] * vx[colour, i + 5:i + 7, 4:28]

    half_sweep_0(0, -4, 20)
    half_sweep_0(1, -4, 20)
    half_sweep_0(0, -2, 18)
    half_sweep_0(1, -2, 18)

    def residual_0(i):
        total = None
        for colour in (0, 1):
            left = update_0(colour, i, 0, 16, even_16) - vx[colour, i + 5:i + 7, 8:24]
            left = d0[colour, i + 4:i + 6, 4:20] * left
            total = left if total is None else total + left
        return total

    for i in range(8):
        both = residual_0(2 * i)
        t0[i] = both[0] + both[1]
    rows = block_mean()
    for a in range(4):
        s1x[0, a + 4, 16:24], s1x[1, a + 4, 16:24] = merge(rows[2 * a], rows[2 * a + 1], odd_8)
    send_s1 = halo_copies(s1x, (4, 16), s1x, (4, 16), (4, 8), (3, 5), (sent.at[0], arrived.at[3]), position)
    halo_start(send_s1)

    vk[5:21, 8:24] = vx[1, 5:21, 8:24]
    send_vk = halo_copies(vk, (5, 8), vk, (5, 8), (16, 16), (4, 4), (sent.at[0], arrived.at[4]), position)
    halo_start(send_vk)

    shape = (24, 128)
    col, lanes = iota(shape, 0) - 6, iota(shape, 1)
    w1 = 0.5 / 4.0
    wy_low = jnp.where((col == 0) & (gy == 0), 0.0, w1).astype(F32)
    wy_high = jnp.where((col == 7) & (gy == GY - 1), 0.0, w1).astype(F32)
    wx_low = jnp.where(gx == 0, 0.0, w1).astype(F32)
    wx_high = jnp.where(gx == GX - 1, 0.0, w1).astype(F32)
    wz_low = jnp.where(lanes == 0, 0.0, w1).astype(F32)
    wz_high = jnp.where(lanes == 127, 0.0, w1).astype(F32)

    def first_of_pair(size, origin):
        odd = (iota((size, 128), 0) + iota((size, 128), 1) + origin) & 1
        return odd == 0, odd == 1

    first_24, first_16, first_8 = first_of_pair(24, 0), first_of_pair(16, 0), first_of_pair(8, 0)

    halo_wait([send_k1], position, arrived.at[2], dummy)
    for colour in (0, 1):
        for a in range(-3, 7):
            e, f = a + 4, a + 3
            other = k1[1 - colour, e, 10:34]
            first = first_24[colour]
            w_cross = w1
            if a in (0, 3):
                w_cross = jnp.where(first, wx_low if a == 0 else w1, wx_high if a == 3 else w1)
            parts, total, inverse = couple(
                k1[colour, e, 10:34], other, jnp.where(first, k1[1 - colour, e - 1, 10:34], k1[1 - colour, e + 1, 10:34]),
                k1[1 - colour, e, 9:33], k1[1 - colour, e, 11:35], other, (w1, w_cross, wy_low, wy_high, wz_low, wz_high), 1,
            )
            d1[colour, f] = total
            i1[colour, f] = inverse
            for n in range(6):
                c1[colour, n, f] = parts[n]

    def update_1(colour, a, lo, hi):
        e, f = a + 4, a + 3
        here, at = slice(lo + 6, hi + 6), slice(lo + 16, hi + 16)
        first = {24: first_24, 16: first_16, 8: first_8}[hi - lo][colour]
        return relax(
            s1[colour, f, here], [c1[colour, n, f, here] for n in range(6)], v1[1 - colour, e, at],
            jnp.where(first, v1[1 - colour, e - 1, at], v1[1 - colour, e + 1, at]),
            v1[1 - colour, e, lo + 15:hi + 15], v1[1 - colour, e, lo + 17:hi + 17], 1,
        )

    def half_sweep_1(colour, start, stop, lo, hi):
        for a in range(start, stop):
            v1[colour, a + 4, lo + 16:hi + 16] = update_1(colour, a, lo, hi)

    hear(1)
    arrive(tree_xy, 6)
    for copy in tree_z:
        copy.start()

    halo_wait([send_s1], position, arrived.at[3], dummy)
    for colour in (0, 1):
        for a in range(-3, 7):
            s1[colour, a + 3] = i1[colour, a + 3] * s1x[colour, a + 4, 10:34]
    for a in range(-2, 6):
        v1[0, a + 4, 12:28] = s1[0, a + 3, 2:18]
    half_sweep_1(1, -2, 6, -4, 12)
    half_sweep_1(0, -1, 5, -4, 12)
    half_sweep_1(1, -1, 5, -4, 12)
    pairs = []
    for a in range(4):
        left = [d1[n, a + 3, 6:14] * (update_1(n, a, 0, 8) - v1[n, a + 4, 16:24]) for n in (0, 1)]
        pairs.append(left[0] + left[1])
    level_2_share(1, pairs, sg)
    for copy in spread_s:
        copy.start()
    arrive(tree_z, 7)
    tree_core[0].start()
    vk1[4:8, 16:24] = v1[1, 4:8, 16:24]
    send_vk1 = halo_copies(vk1, (4, 16), vk1, (4, 16), (4, 8), (3, 6), (sent.at[0], arrived.at[5]), position)
    halo_start(send_vk1)

    arrive(tree_core, 8)
    def two_columns(size):
        return iota((size, 128), 1) < 64, (iota((size, 128), 0) & 1) == 1

    def beside_2(row_low, row_high, low, odd):
        turned = roll(jnp.where(low, row_high, row_low), 64)
        return jnp.where(odd, row_low, turned), jnp.where(odd, turned, row_high)

    lane = iota((32, 128), 1)
    place = lane & 63
    j_row = iota((32, 128), 0)
    low_32, odd_32 = two_columns(32)
    first_32 = first_of_pair(32, 0)
    w2 = 0.5 / 16.0
    wy_low = jnp.where((j_row == 0) & low_32, 0.0, w2).astype(F32)
    wy_high = jnp.where((j_row == 31) & (lane >= 64), 0.0, w2).astype(F32)
    wz_low = jnp.where(place == 0, 0.0, w2).astype(F32)
    wz_high = jnp.where(place == 63, 0.0, w2).astype(F32)

    def kg_rows(colour, a, at):
        return kg[colour, a // 4, a % 4, at]

    at = slice(8, 40)
    for colour in (0, 1):
        for a in range(16):
            other = kg_rows(1 - colour, a, at)
            before = kg_rows(1 - colour, max(a - 1, 0), at)
            after = kg_rows(1 - colour, min(a + 1, 15), at)
            w_cross = w2
            if a == 0:
                w_cross = jnp.where(first_32[colour], 0.0, w2).astype(F32)
            if a == 15:
                w_cross = jnp.where(first_32[colour], w2, 0.0).astype(F32)
            low, high = beside_2(
                kg_rows(1 - colour, a, slice(7, 39)), kg_rows(1 - colour, a, slice(9, 41)), low_32, odd_32
            )
            parts, total, inverse = couple(
                kg_rows(colour, a, at), other, jnp.where(first_32[colour], before, after), low, high, other,
                (w2, w_cross, wy_low, wy_high, wz_low, wz_high), 1,
            )
            d2[colour, a] = total
            i2[colour, a] = inverse
            for n in range(6):
                c2[colour, n, a] = parts[n]

    lane3 = iota((16, 128), 1)
    even_place = (lane3 & 1) == 0
    place3 = (lane3 & 63) >> 1
    row3 = iota((16, 128), 0)
    low3 = lane3 < 64
    odd3 = (((lane3 >> 6) + place3) & 1) == 1
    first3 = (jnp.logical_not(odd3), odd3)

    lower = even_place

    def level_3_share(p):
        rows = []
        for n in (2 * p, 2 * p + 1):
            both = []
            for a in (n, n + 8):
                row = t2[a, pl.ds(0, 16, stride=2)] + t2[a, pl.ds(1, 16, stride=2)]
                both.append(row + jnp.where(even_place, roll(row, -1), roll(row, 1)))
            rows.append(0.125 * jnp.where(lower, both[0], both[1]))
        return merge(rows[0], rows[1], odd3)

    w3 = 0.5 / 64.0
    wy_low = jnp.where((row3 == 0) & low3, 0.0, w3).astype(F32)
    wy_high = jnp.where((row3 == 15) & (lane3 >= 64), 0.0, w3).astype(F32)
    wz_low = jnp.where(place3 == 0, 0.0, w3).astype(F32)
    wz_high = jnp.where(place3 == 31, 0.0, w3).astype(F32)
    at3 = slice(8, 24)

    def around_3(ref, colour, p, first):
        here = ref[colour, p, at3]
        before = ref[colour, p - 1, at3] if p else roll(ref[colour, 3, at3], 1)
        after = ref[colour, p + 1, at3] if p < 3 else roll(ref[colour, 0, at3], -1)
        low = roll(jnp.where(low3, here, ref[colour, p, 7:23]), 64)
        high = roll(jnp.where(low3, ref[colour, p, 9:25], here), 64)
        return here, jnp.where(first, before, after), low, high

    for a in range(16):
        t2[a] = kg_rows(0, a, at) + kg_rows(1, a, at)
    for p in range(4):
        k3[0, p, at3], k3[1, p, at3] = level_3_share(p)
    for colour in (0, 1):
        for p in range(4):
            here, cross, low, high = around_3(k3, 1 - colour, p, first3[colour])
            w_cross = w3
            if p == 0:
                w_cross = jnp.where(first3[colour] & lower, 0.0, w3).astype(F32)
            if p == 3:
                w_cross = jnp.where(first3[colour] | lower, w3, 0.0).astype(F32)
            parts, _, inverse = couple(
                k3[colour, p, at3], here, cross, low, high, here, (w3, w_cross, wy_low, wy_high, wz_low, wz_high), 2
            )
            i3[colour, p] = inverse
            for n in range(6):
                c3[colour, n, p] = parts[n]

    halo_wait(
        [send_k, send_v, send_k1, send_s1, send_vk, send_vk1], position, sent.at[0], dummy,
        rows_of(tree_xy + tree_z + tree_core),
    )
    for x in (0, 1, 3, 2):
        arrive([copy for copy, chip in zip(spread_s, CHIPS) if chip[0] == x], 9 + x)
        share_s[x].start()
    arrive(share_s, 13)

    for colour in (0, 1):
        for a in range(16):
            source = i2[colour, a] * sg[colour, a // 4, a % 4, at]
            s2[colour, a] = source
            if colour == 0:
                v2[0, a + 2, at] = source

    def update_2(colour, a, rows, frame_rows, low, odd, first):
        before, here, after = frame_rows
        row_low, row_high = beside_2(v2[1 - colour, a + 2, before], v2[1 - colour, a + 2, after], low, odd)
        cross = jnp.where(first[colour], v2[1 - colour, a + 1, here], v2[1 - colour, a + 3, here])
        return relax(
            s2[colour, a, rows], [c2[colour, n, a, rows] for n in range(6)], v2[1 - colour, a + 2, here],
            cross, row_low, row_high, 1,
        )

    whole_2 = (slice(0, 32), (slice(7, 39), at, slice(9, 41)), low_32, odd_32, first_32)

    def half_sweep_2(colour):
        for a in range(16):
            v2[colour, a + 2, at] = update_2(colour, a, *whole_2)

    half_sweep_2(1)
    half_sweep_2(0)
    half_sweep_2(1)
    for a in range(16):
        left = [d2[n, a] * (update_2(n, a, *whole_2) - v2[n, a + 2, at]) for n in (0, 1)]
        t2[a] = left[0] + left[1]
    for p in range(4):
        sources = level_3_share(p)
        for colour in (0, 1):
            s3[colour, p] = i3[colour, p] * sources[colour]

    def half_sweep_3(colour):
        for p in range(4):
            here, cross, low, high = around_3(v3, 1 - colour, p, first3[colour])
            v3[colour, p, at3] = relax(
                s3[colour, p], [c3[colour, n, p] for n in range(6)], here, cross, low, high, 2
            )

    for p in range(4):
        v3[0, p, at3] = s3[0, p]
    half_sweep_3(1)
    for _ in range(COARSE_SWEEPS - 1):
        half_sweep_3(0)
        half_sweep_3(1)

    for p in range(4):
        cells = [v3[colour, p, at3] for colour in (0, 1)]
        firsts = [jnp.where(lower, c, roll(c, 1)) for c in cells]
        seconds = [jnp.where(lower, roll(c, -1), c) for c in cells]
        for pair, (red, black) in ((p, firsts), (p + 4, seconds)):
            for n, row in enumerate((jnp.where(odd3, black, red), jnp.where(odd3, red, black))):
                p2[2 * pair + n, pl.ds(0, 16, stride=2)] = row
                p2[2 * pair + n, pl.ds(1, 16, stride=2)] = row

    def within(value, top, span):
        value = value * ((value + span) // span)
        value = top - value
        return top - value * ((value + span) // span)

    a0 = 2 * within(gx - 2, 3, 8)
    r0 = 2 * within(gy - 2, 8, 16)
    strip = pl.ds(r0, 16)
    part_2 = (strip, (pl.ds(r0 + 7, 16), pl.ds(r0 + 8, 16), pl.ds(r0 + 9, 16)), *two_columns(16), first_16)
    for n in range(10):
        v2[1, a0 + n + 2, pl.ds(r0 + 8, 16)] = v2[1, a0 + n + 2, pl.ds(r0 + 8, 16)] + p2[a0 + n, strip]
    for colour in (0, 1, 0, 1):
        news = [update_2(colour, a0 + n, *part_2) for n in range(10)]
        for n, new in enumerate(news):
            v2[colour, a0 + n + 2, pl.ds(r0 + 8, 16)] = new

    spot = iota((8, 128), 1) >> 1
    for d in range(-3, 7):
        cells = (2 * gx + d // 2 + 2, pl.ds(2 * gy + 6, 8))
        coarse = jnp.where(odd_8 == (d % 2 == 1), v2[(0,) + cells], v2[(1,) + cells])
        q1[d + 3, 0] = jnp.take_along_axis(coarse, spot, axis=1)
        q1[d + 3, 1] = jnp.take_along_axis(coarse, spot + 64, axis=1)
    for d in range(10):
        for n in range(2):
            for m in range(2):
                column = q1[d, n, pl.ds(m, 4, stride=2)]
                p1[d, pl.ds(4 * n + 2 * m, 4, stride=8)] = column
                p1[d, pl.ds(4 * n + 2 * m + 1, 4, stride=8)] = column
    halo_wait([send_vk1], position, arrived.at[5], dummy)
    for a in range(-3, 7):
        v1[1, a + 4, 10:30] = vk1[a + 4, 10:30] + p1[a + 3, 2:22]
    half_sweep_1(0, -3, 7, -6, 18)
    half_sweep_1(1, -2, 6, -4, 12)
    half_sweep_1(0, -2, 6, -4, 12)
    half_sweep_1(1, -1, 5, -4, 12)

    odd_12 = (iota((12, 128), 0) + iota((12, 128), 1)) & 1
    for i in range(-2, 10):
        a = i // 2
        row = jnp.where(odd_12 == i % 2, v1[0, a + 4, 14:26], v1[1, a + 4, 14:26])
        p0[i + 2, pl.ds(0, 12, stride=2)] = row
        p0[i + 2, pl.ds(1, 12, stride=2)] = row
    halo_wait([send_vk], position, arrived.at[4], dummy)
    for i in range(-4, 20):
        vx[1, i + 5, 4:28] = vk[i + 5, 4:28] + p0[i // 2 + 2]
    half_sweep_0(0, -4, 20)
    half_sweep_0(1, -2, 18)
    half_sweep_0(0, -2, 18)
    for i in range(0, 16, 2):
        out[0, i:i + 2] = vx[0, i + 5:i + 7, 8:24]
        out[1, i:i + 2] = update_0(1, i, 0, 16, even_16)

    wait_rows(rows_of(spread_s + share_s), sent.at[1], dummy)


def join(cells, out, rows, sems):
    lane = iota((16, 128), 1)
    odd_row = iota((16, 128), 0) & 1
    low = lane < 64
    half = lane >> 1
    copies = []
    for i in range(16):
        red, turned = cells[0, i], roll(cells[1, i], 64)
        left, right = jnp.where(low, red, turned), jnp.where(low, turned, red)
        same = (lane & 1) == (odd_row ^ (i & 1))
        rows[i, :, :128] = jnp.take_along_axis(left, half + jnp.where(same, 0, 64), axis=1)
        rows[i, :, 128:] = jnp.take_along_axis(right, half + jnp.where(same, 64, 0), axis=1)
        if i % 4 == 3:
            part = pl.ds(i - 3, 4)
            copies.append(pltpu.make_async_copy(rows.at[part], out.at[part], sems.at[i // 4]))
            copies[-1].start()
    for copy in copies:
        copy.wait()


def v_cycle(image, conduct):
    def vmem(*shape):
        return pltpu.VMEM(shape, F32)

    frame0, frame1, gathered = (26, 32, 128), (12, 40, 128), (2, 4, 4, 48, 128)
    cells = pl.pallas_call(
        kernel,
        out_shape=jax.ShapeDtypeStruct((2, 16, 16, 128), F32),
        in_specs=[pl.BlockSpec(memory_space=pltpu.HBM)] * 2,
        out_specs=pl.BlockSpec(memory_space=pltpu.VMEM),
        scratch_shapes=[
            vmem(16, 16, 256), vmem(16, 16, 256),
            vmem(2, *frame0), vmem(2, *frame0), vmem(2, 16, 16, 128), vmem(*frame0), vmem(2, 6, 24, 24, 128),
            vmem(2, 24, 24, 128), vmem(2, 24, 24, 128), vmem(8, 16, 128), vmem(12, 24, 128),
            vmem(2, *frame1), vmem(2, *frame1), vmem(2, *frame1), vmem(*frame1), vmem(2, 6, 10, 24, 128),
            vmem(2, 10, 24, 128), vmem(2, 10, 24, 128), vmem(2, 10, 24, 128), vmem(4, 8, 128), vmem(10, 32, 128),
            vmem(10, 2, 8, 128), vmem(2, 2, 2, 2, 128), vmem(*gathered), vmem(*gathered), vmem(2, 20, 48, 128),
            vmem(2, 6, 16, 32, 128), vmem(2, 16, 32, 128), vmem(2, 16, 32, 128), vmem(2, 16, 32, 128), vmem(16, 32, 128),
            vmem(16, 32, 128),
            vmem(2, 4, 32, 128), vmem(2, 4, 32, 128), vmem(2, 6, 4, 16, 128), vmem(2, 4, 16, 128),
            vmem(2, 4, 16, 128), vmem(4096, 128),
            pltpu.SemaphoreType.DMA((2,)), pltpu.SemaphoreType.DMA((14,)), pltpu.SemaphoreType.DMA((2,)),
            pltpu.SemaphoreType.REGULAR((2,)),
        ],
        compiler_params=pltpu.CompilerParams(
            collective_id=0, has_side_effects=True, vmem_limit_bytes=48 * 2**20
        ),
        name="v_cycle",
    )(*(pltpu.with_memory_space_constraint(array, pltpu.HBM) for array in (image, conduct)))
    return pl.pallas_call(
        join,
        out_shape=jax.ShapeDtypeStruct((16, 16, 256), F32),
        in_specs=[pl.BlockSpec(memory_space=pltpu.VMEM)],
        out_specs=pl.BlockSpec(memory_space=pltpu.HBM),
        scratch_shapes=[vmem(16, 16, 256), pltpu.SemaphoreType.DMA((4,))],
        compiler_params=pltpu.CompilerParams(vmem_limit_bytes=8 * 2**20),
        name="join",
    )(cells)


def solution(mesh):
    return jax.shard_map(
        v_cycle,
        mesh=mesh,
        in_specs=(P("gx", "gy", None), P("gx", "gy", None)),
        out_specs=P("gx", "gy", None),
        check_vma=False,
    )
```

```python
import math

import jax
import jax.numpy as jnp
from jax import lax
from jax.experimental import pallas as pl
from jax.experimental.pallas import tpu as pltpu
from jax.sharding import PartitionSpec as P

COARSE_SWEEPS = 8
MESH = pl.DeviceIdType.MESH
F32 = jnp.float32
GX, GY = 8, 16
DIRECTIONS = [(-1, -1), (-1, 1), (1, -1), (1, 1), (0, -1), (0, 1), (-1, 0), (1, 0)]
CHIPS = sorted(
    [(x, y, z) for x in range(4) for y in range(4) for z in range(4) if (x, y, z) != (0, 0, 0)],
    key=lambda d: -sum(min(c, 4 - c) for c in d),
)


def nearness(offset):
    return max(min(offset[0], GX - offset[0]), min(offset[1], GY - offset[1]))


def iota(shape, dim):
    return lax.broadcasted_iota(jnp.int32, shape, dim)


def roll(values, shift):
    return pltpu.roll(values, shift % 128, values.ndim - 1)


def halo_copies(src, src_origin, dst, origin, extent, widths, sems, position, corners=None, colour=None):
    gx, gy = position
    lead = (slice(None),) * (len(dst.shape) - 3) if colour is None else (colour,)

    def piece(step, size, here, there, start, stop):
        if step == 0:
            return slice(here, here + size), slice(there, there + size)
        if step > 0:
            return slice(here + size - stop, here + size - start), slice(there - stop, there - start)
        return slice(here + start, here + stop), slice(there + size + start, there + size + stop)

    copies = []
    for dx, dy in DIRECTIONS:
        boxes = [((0, widths[0]), (0, widths[1]))]
        if dx and dy and corners is not None:
            boxes = [((start, stop), (0, width)) for start, stop, width in corners]
        group = []
        for box_x, box_y in boxes:
            src_x, dst_x = piece(dx, extent[0], src_origin[0], origin[0], *box_x)
            src_y, dst_y = piece(dy, extent[1], src_origin[1], origin[1], *box_y)
            group.append(
                pltpu.make_async_remote_copy(
                    src_ref=src.at[lead + (src_x, src_y)],
                    dst_ref=dst.at[lead + (dst_x, dst_y)],
                    send_sem=sems[0],
                    recv_sem=sems[1],
                    device_id=(lax.rem(gx + dx + GX, GX), lax.rem(gy + dy + GY, GY)),
                    device_id_type=MESH,
                )
            )
        copies.append((in_grid(gx + dx, gy + dy), group))
    return copies


def in_grid(x, y):
    return (x >= 0) & (x < GX) & (y >= 0) & (y < GY)


def halo_start(copies):
    for sends, group in copies:

        @pl.when(sends)
        def _():
            for copy in group:
                copy.start()


def rows_of(group):
    return sum(math.prod(copy.src_ref.shape[:-1]) for copy in group)


def wait_rows(rows, sem, room):
    pltpu.make_async_copy(room.at[0:rows], room.at[0:rows], sem).wait()


def halo_wait(exchanges, position, sem, room, more=0):
    edge_x = (position[0] == 0) | (position[0] == GX - 1)
    edge_y = (position[1] == 0) | (position[1] == GY - 1)
    rows = {direction: 0 for direction in DIRECTIONS}
    for copies in exchanges:
        for direction, (_, group) in zip(DIRECTIONS, copies):
            rows[direction] += rows_of(group)
    for at_x in (False, True):
        for at_y in (False, True):
            lost = [(dx, dy) for dx, dy in DIRECTIONS if (at_x and dx == 1) or (at_y and dy == 1)]
            total = more + sum(rows.values()) - sum(rows[direction] for direction in lost)

            @pl.when((edge_x == at_x) & (edge_y == at_y))
            def _():
                wait_rows(total, sem, room)


def couple(here, same, cross, low, high, other, weights, z_step):
    w, w_cross, w_low, w_high, w_below, w_above = weights
    parts = [
        (here + same) * w,
        (here + cross) * w_cross,
        (here + low) * w_low,
        (here + high) * w_high,
        (here + roll(other, z_step)) * w_below,
        (here + roll(other, -z_step)) * w_above,
    ]
    total = ((parts[0] + parts[1]) + (parts[2] + parts[3])) + ((parts[4] + parts[5]) + 1.0)
    inverse = 1.0 / total
    return [part * inverse for part in parts], total, inverse


def relax(source, couplings, same, cross, low, high, z_step):
    acc0 = source + couplings[0] * same
    acc1 = couplings[4] * roll(same, z_step) + couplings[5] * roll(same, -z_step)
    acc2 = couplings[2] * low + couplings[3] * high
    return (acc0 + acc2) + (acc1 + couplings[1] * cross)


def kernel(
    image, conduct, out,
    image_in, conduct_in, kx, vx, vs, vk, c0, s0, d0, t0, p0,
    k1, s1x, v1, vk1, c1, s1, i1, d1, t1, p1,
    q1, own2, kg, sg, v2, c2, s2, i2, d2, t2, p2,
    k3, v3, c3, s3, i3, dummy,
    sent, arrived, in_sems, known_sems,
):
    gx, gy = lax.axis_index("gx"), lax.axis_index("gy")
    chip_x, core = gx // 2, lax.rem(gx, 2)
    chip_z, chip_y = gy // 4, lax.rem(gy, 4)
    sibling = (chip_x * 2 + 1 - core, gy)
    chips = [
        (lax.rem(chip_x + x, 4) * 2 + core, lax.rem(chip_z + z, 4) * 4 + lax.rem(chip_y + y, 4))
        for x, y, z in CHIPS
    ]
    position = (gx, gy)

    barrier = pltpu.get_barrier_semaphore()

    fetch_k = pltpu.make_async_copy(conduct, conduct_in, in_sems.at[0])
    fetch_v = pltpu.make_async_copy(image, image_in, in_sems.at[1])
    fetch_k.start()
    fetch_v.start()

    def near(steps):
        offsets = sorted({(x % GX, y % GY) for x in steps for y in steps} - {(0, 0)}, key=nearness)
        return [(lax.rem(gx + x, GX), lax.rem(gy + y, GY)) for x, y in offsets]

    def tell(n):
        for peer in near((0, 2 << n, -2 << n)):
            pl.semaphore_signal(known_sems.at[n], inc=1, device_id=peer, device_id_type=MESH)

    def hear(n):
        pl.semaphore_wait(known_sems.at[n], len(near((0, 2 << n, -2 << n))))

    greeted = near(range(-2, 3)) + [(lax.rem(gx + 4, GX), gy)]
    for peer in greeted:
        pl.semaphore_signal(barrier, inc=1, device_id=peer, device_id_type=MESH)

    lane0 = iota((16, 128), 1)
    odd_row = iota((16, 128), 0) & 1
    low0 = lane0 < 64
    half_lane = (lane0 & 63) * 2

    def split(values, par):
        parity = odd_row ^ par
        first = half_lane + jnp.where(low0, parity, 1 - parity)
        second = half_lane + jnp.where(low0, 1 - parity, parity)
        left = jnp.take_along_axis(values[:, :128], first, axis=1)
        right = jnp.take_along_axis(values[:, 128:], second, axis=1)
        return jnp.where(low0, left, right), roll(jnp.where(low0, right, left), 64)

    nothing = jnp.zeros((2, 4, 4, 8, 128), F32)
    kg[:, :, :, 0:8], kg[:, :, :, 40:48] = nothing, nothing
    nothing = jnp.zeros((2, 20, 8, 128), F32)
    v2[:, :, 0:8], v2[:, :, 40:48] = nothing, nothing
    nothing = jnp.zeros((2, 2, 48, 128), F32)
    v2[:, 0:2], v2[:, 18:20] = nothing, nothing
    nothing = jnp.zeros((2, 4, 8, 128), F32)
    for ref in (k3, v3):
        ref[:, :, 0:8], ref[:, :, 24:32] = nothing, nothing

    def zero(ref, *at):
        at = (slice(None),) * (len(ref.shape) - 3) + at
        ref[at] = jnp.zeros(ref.at[at].shape, F32)

    for edge, rows0, rows1 in ((gx == 0, slice(0, 5), slice(0, 4)), (gx == GX - 1, slice(21, 26), slice(8, 12))):

        @pl.when(edge)
        def _():
            for ref in (kx, vx, vk):
                zero(ref, rows0)
            for ref in (k1, s1x, vk1):
                zero(ref, rows1)

    for edge, cols0, cols1 in ((gy == 0, slice(0, 8), slice(8, 16)), (gy == GY - 1, slice(24, 32), slice(24, 32))):

        @pl.when(edge)
        def _():
            for ref in (kx, vx, vk):
                zero(ref, slice(None), cols0)
            for ref in (k1, s1x, vk1):
                zero(ref, slice(None), cols1)

    for i in range(16):
        if i == 0:
            fetch_k.wait()
        kx[0, i + 5, 8:24], kx[1, i + 5, 8:24] = split(conduct_in[i], i & 1)

    pl.semaphore_wait(barrier, len(greeted))
    def halos(src, src_origin, dst, origin, extent, which, *cones):
        sems = (sent.at[0], arrived.at[which])
        each = [
            halo_copies(src, src_origin, dst, origin, extent, widths, sems, position, corners, colour)
            for colour, widths, corners in cones
        ]
        return [(ways[0][0], sum((group for _, group in ways), [])) for ways in zip(*each)]

    cones = (1, (5, 5), [(0, 2, 4), (2, 4, 2)]), (0, (4, 4), [(0, 3, 3)])
    send_k = halos(kx, (5, 8), kx, (5, 8), (16, 16), 0, *cones)
    send_v = halos(vs, (0, 0), vx, (5, 8), (16, 16), 1, *cones)
    tell(0)
    halo_start(send_k)
    fetch_v.wait()
    for i in range(16):
        red, black = split(image_in[i], i & 1)
        vx[0, i + 5, 8:24], vx[1, i + 5, 8:24] = red, black
        vs[0, i], vs[1, i] = red, black
    halo_start(send_v)

    def block_mean():
        return [0.125 * (t0[i, pl.ds(0, 8, stride=2)] + t0[i, pl.ds(1, 8, stride=2)]) for i in range(8)]

    odd_8 = ((iota((8, 128), 0) + iota((8, 128), 1)) & 1) == 1
    odd_2 = ((iota((2, 128), 0) + iota((2, 128), 1)) & 1) == 1
    low_2 = iota((2, 128), 1) < 64
    even_lane = (iota((8, 128), 1) & 63) * 2

    def merge(first, second, odd):
        return jnp.where(odd, second, first), jnp.where(odd, first, second)

    def level_2_share(kind, pairs, whole):
        rows = []
        for i in range(4):
            t1[i] = jnp.take_along_axis(pairs[i], even_lane, axis=1) + jnp.take_along_axis(pairs[i], even_lane + 1, axis=1)
        for i in range(4):
            first = t1[i, pl.ds(0, 2, stride=2)] + t1[i, pl.ds(1, 2, stride=2)]
            second = t1[i, pl.ds(4, 2, stride=2)] + t1[i, pl.ds(5, 2, stride=2)]
            rows.append(0.125 * jnp.where(low_2, first, second))
        for a in range(2):
            cells = merge(rows[2 * a], rows[2 * a + 1], odd_2)
            for colour in (0, 1):
                own2[kind, colour, a] = cells[colour]
                whole[colour, chip_x, 2 * core + a, pl.ds(8 + 2 * gy, 2)] = cells[colour]

    def remote(src, dst, which, device):
        return pltpu.make_async_remote_copy(
            src_ref=src, dst_ref=dst, send_sem=sent.at[int(9 <= which <= 13)], recv_sem=arrived.at[which], device_id=device, device_id_type=MESH
        )

    cores_rows = pl.ds(2 * core, 2)
    own_place = (slice(None), chip_x, cores_rows, pl.ds(8 + 2 * gy, 2))

    spread_s = [
        remote(own2.at[1], sg.at[own_place], 9 + x, chip) for chip, (x, _, _) in zip(chips, CHIPS)
    ]
    planes = [sg.at[:, lax.rem(chip_x + 4 - x, 4), cores_rows, 8:40] for x in range(4)]
    share_s = [remote(plane, plane, 13, sibling) for plane in planes]

    def arrive(copies, which):
        wait_rows(rows_of(copies), arrived.at[which], dummy)

    def chip_at(x, y, z):
        return (
            lax.rem(chip_x + x, 4) * 2 + core,
            lax.rem(chip_z + z, 4) * 4 + lax.rem(chip_y + y, 4),
        )

    row = kg.at[:, :, cores_rows, pl.ds(8 + 2 * gy, 2)]
    sheet = kg.at[:, :, cores_rows, pl.ds(8 + 8 * chip_z, 8)]
    half = kg.at[:, :, cores_rows, 8:40]
    tree_x = [remote(own2.at[0], kg.at[own_place], 6, chip_at(n, 0, 0)) for n in (2, 1, 3)]
    tree_y = [remote(row, row, 7, chip_at(0, n, 0)) for n in (2, 1, 3)]
    tree_z = [remote(sheet, sheet, 14, chip_at(0, 0, n)) for n in (2, 1, 3)]
    tree_core = [remote(half, half, 8, sibling)]

    for i in range(8):
        e = 2 * i + 5
        t0[i] = (kx[0, e, 8:24] + kx[1, e, 8:24]) + (kx[0, e + 1, 8:24] + kx[1, e + 1, 8:24])
    rows = block_mean()
    for a in range(4):
        k1[0, a + 4, 16:24], k1[1, a + 4, 16:24] = merge(rows[2 * a], rows[2 * a + 1], odd_8)
    level_2_share(0, [rows[2 * a] + rows[2 * a + 1] for a in range(4)], kg)
    send_k1 = halos(k1, (4, 16), k1, (4, 16), (4, 8), 2, (None, (3, 6), [(0, 1, 6), (1, 3, 4)]))
    halo_start(send_k1)

    shape = (2, 24, 128)
    sub, lanes = iota(shape, 1), iota(shape, 2)
    even_row = ((iota(shape, 0) + sub) & 1) == 0
    wy_low = jnp.where((sub == 4) & (gy == 0), 0.0, 0.5).astype(F32)
    wy_high = jnp.where((sub == 19) & (gy == GY - 1), 0.0, 0.5).astype(F32)
    wx_low = jnp.where(gx == 0, 0.0, 0.5).astype(F32)
    wx_high = jnp.where(gx == GX - 1, 0.0, 0.5).astype(F32)
    wz = [
        jnp.where(even_row, jnp.where(lanes == 0, 0.0, 0.5), jnp.where(lanes == 127, 0.0, 0.5)).astype(F32),
        jnp.where(even_row, jnp.where(lanes == 127, 0.0, 0.5), jnp.where(lanes == 0, 0.0, 0.5)).astype(F32),
    ]

    def beside(values, colour, even):
        step = 1 if colour == 0 else -1
        first = roll(jnp.where(even, values[0], values[1]), step)
        second = roll(jnp.where(even, values[1], values[0]), -step)
        return jnp.stack([jnp.where(even, first, second), jnp.where(even, second, first)])

    even_24 = (iota((24, 128), 0) & 1) == 0
    even_16 = (iota((16, 128), 0) & 1) == 0

    row_index = iota((2, 1, 1), 0)

    def couplings_0(colour, start, stop):
        for i in range(start, stop, 2):
            e = i + 5
            here, other = kx[colour, e:e + 2, 4:28], kx[1 - colour, e:e + 2, 4:28]
            wx_l = jnp.where(row_index == 0, wx_low, 0.5) if i == 0 else 0.5
            wx_h = jnp.where(row_index == 1, wx_high, 0.5) if i == 14 else 0.5
            parts = [
                (here + kx[1 - colour, e - 1:e + 1, 4:28]) * wx_l,
                (here + kx[1 - colour, e + 1:e + 3, 4:28]) * wx_h,
                (here + kx[1 - colour, e:e + 2, 3:27]) * wy_low,
                (here + kx[1 - colour, e:e + 2, 5:29]) * wy_high,
                (here + other) * 0.5,
                (here + beside(other, colour, even_24)) * wz[colour],
            ]
            total = ((parts[0] + parts[1]) + (parts[2] + parts[3])) + ((parts[4] + parts[5]) + 1.0)
            inverse = 1.0 / total
            d0[colour, i + 4:i + 6] = total
            s0[colour, i + 4:i + 6] = inverse
            for n in range(6):
                c0[colour, n, i + 4:i + 6] = parts[n] * inverse

    def update_0(colour, i, lo, hi, rows_even):
        e, f = i + 5, i + 4
        a, b = lo + 8, hi + 8
        here = slice(lo + 4, hi + 4)
        other = vx[1 - colour, e:e + 2, a:b]
        acc0 = s0[colour, f:f + 2, here] + c0[colour, 0, f:f + 2, here] * vx[1 - colour, e - 1:e + 1, a:b]
        acc1 = c0[colour, 1, f:f + 2, here] * vx[1 - colour, e + 1:e + 3, a:b]
        acc1 += c0[colour, 2, f:f + 2, here] * vx[1 - colour, e:e + 2, a - 1:b - 1]
        acc2 = c0[colour, 3, f:f + 2, here] * vx[1 - colour, e:e + 2, a + 1:b + 1]
        acc2 += c0[colour, 4, f:f + 2, here] * other
        acc3 = c0[colour, 5, f:f + 2, here] * beside(other, colour, rows_even)
        return (acc0 + acc1) + (acc2 + acc3)

    def half_sweep_0(colour, start, stop, lo=-4, hi=20):
        rows_even = even_24 if hi - lo == 24 else even_16
        for i in range(start, stop, 2):
            vx[colour, i + 5:i + 7, lo + 8:hi + 8] = update_0(colour, i, lo, hi, rows_even)

    for copy in tree_x:
        copy.start()
    halo_wait([send_k], position, arrived.at[0], dummy)
    couplings_0(0, -4, 20)
    couplings_0(1, -4, 20)
    hear(0)
    tell(1)
    arrive(tree_x, 6)
    for copy in tree_y:
        copy.start()
    halo_wait([send_v], position, arrived.at[1], dummy)
    for colour in (0, 1):
        for i in range(-4, 20, 2):
            s0[colour, i + 4:i + 6] = s0[colour, i + 4:i + 6] * vx[colour, i + 5:i + 7, 4:28]

    half_sweep_0(0, -4, 20)
    half_sweep_0(1, -4, 20)
    half_sweep_0(0, -2, 18)
    half_sweep_0(1, -2, 18)

    def residual_0(i):
        total = None
        for colour in (0, 1):
            left = update_0(colour, i, 0, 16, even_16) - vx[colour, i + 5:i + 7, 8:24]
            left = d0[colour, i + 4:i + 6, 4:20] * left
            total = left if total is None else total + left
        return total

    for i in range(8):
        both = residual_0(2 * i)
        t0[i] = both[0] + both[1]
    rows = block_mean()
    for a in range(4):
        s1x[0, a + 4, 16:24], s1x[1, a + 4, 16:24] = merge(rows[2 * a], rows[2 * a + 1], odd_8)
    send_s1 = halos(s1x, (4, 16), s1x, (4, 16), (4, 8), 3, (None, (3, 5), [(0, 1, 5), (1, 3, 3)]))
    halo_start(send_s1)

    vk[5:21, 8:24] = vx[1, 5:21, 8:24]
    send_vk = halos(vk, (5, 8), vk, (5, 8), (16, 16), 4, (None, (4, 4), None))
    halo_start(send_vk)

    shape = (24, 128)
    col, lanes = iota(shape, 0) - 6, iota(shape, 1)
    w1 = 0.5 / 4.0
    wy_low = jnp.where((col == 0) & (gy == 0), 0.0, w1).astype(F32)
    wy_high = jnp.where((col == 7) & (gy == GY - 1), 0.0, w1).astype(F32)
    wx_low = jnp.where(gx == 0, 0.0, w1).astype(F32)
    wx_high = jnp.where(gx == GX - 1, 0.0, w1).astype(F32)
    wz_low = jnp.where(lanes == 0, 0.0, w1).astype(F32)
    wz_high = jnp.where(lanes == 127, 0.0, w1).astype(F32)

    def first_of_pair(size, origin):
        odd = (iota((size, 128), 0) + iota((size, 128), 1) + origin) & 1
        return odd == 0, odd == 1

    first_24, first_16, first_8 = first_of_pair(24, 0), first_of_pair(16, 0), first_of_pair(8, 0)

    halo_wait([send_k1], position, arrived.at[2], dummy)
    for colour in (0, 1):
        for a in range(-3, 7):
            e, f = a + 4, a + 3
            other = k1[1 - colour, e, 10:34]
            first = first_24[colour]
            w_cross = w1
            if a in (0, 3):
                w_cross = jnp.where(first, wx_low if a == 0 else w1, wx_high if a == 3 else w1)
            parts, total, inverse = couple(
                k1[colour, e, 10:34], other, jnp.where(first, k1[1 - colour, e - 1, 10:34], k1[1 - colour, e + 1, 10:34]),
                k1[1 - colour, e, 9:33], k1[1 - colour, e, 11:35], other, (w1, w_cross, wy_low, wy_high, wz_low, wz_high), 1,
            )
            d1[colour, f] = total
            i1[colour, f] = inverse
            for n in range(6):
                c1[colour, n, f] = parts[n]

    def update_1(colour, a, lo, hi):
        e, f = a + 4, a + 3
        here, at = slice(lo + 6, hi + 6), slice(lo + 16, hi + 16)
        first = {24: first_24, 16: first_16, 8: first_8}[hi - lo][colour]
        return relax(
            s1[colour, f, here], [c1[colour, n, f, here] for n in range(6)], v1[1 - colour, e, at],
            jnp.where(first, v1[1 - colour, e - 1, at], v1[1 - colour, e + 1, at]),
            v1[1 - colour, e, lo + 15:hi + 15], v1[1 - colour, e, lo + 17:hi + 17], 1,
        )

    def half_sweep_1(colour, start, stop, lo, hi):
        for a in range(start, stop):
            v1[colour, a + 4, lo + 16:hi + 16] = update_1(colour, a, lo, hi)

    hear(1)
    arrive(tree_y, 7)
    for copy in tree_z:
        copy.start()

    halo_wait([send_s1], position, arrived.at[3], dummy)
    for colour in (0, 1):
        for a in range(-3, 7):
            s1[colour, a + 3] = i1[colour, a + 3] * s1x[colour, a + 4, 10:34]
    for a in range(-2, 6):
        v1[0, a + 4, 12:28] = s1[0, a + 3, 2:18]
    half_sweep_1(1, -2, 6, -4, 12)
    half_sweep_1(0, -1, 5, -4, 12)
    half_sweep_1(1, -1, 5, -4, 12)
    pairs = []
    for a in range(4):
        left = [d1[n, a + 3, 6:14] * (update_1(n, a, 0, 8) - v1[n, a + 4, 16:24]) for n in (0, 1)]
        pairs.append(left[0] + left[1])
    level_2_share(1, pairs, sg)
    for copy in spread_s:
        copy.start()
    arrive(tree_z, 14)
    tree_core[0].start()
    vk1[4:8, 16:24] = v1[1, 4:8, 16:24]
    send_vk1 = halos(vk1, (4, 16), vk1, (4, 16), (4, 8), 5, (None, (3, 6), None))
    halo_start(send_vk1)

    arrive(tree_core, 8)
    def two_columns(size):
        return iota((size, 128), 1) < 64, (iota((size, 128), 0) & 1) == 1

    def beside_2(row_low, row_high, low, odd):
        turned = roll(jnp.where(low, row_high, row_low), 64)
        return jnp.where(odd, row_low, turned), jnp.where(odd, turned, row_high)

    lane = iota((32, 128), 1)
    place = lane & 63
    j_row = iota((32, 128), 0)
    low_32, odd_32 = two_columns(32)
    first_32 = first_of_pair(32, 0)
    w2 = 0.5 / 16.0
    wy_low = jnp.where((j_row == 0) & low_32, 0.0, w2).astype(F32)
    wy_high = jnp.where((j_row == 31) & (lane >= 64), 0.0, w2).astype(F32)
    wz_low = jnp.where(place == 0, 0.0, w2).astype(F32)
    wz_high = jnp.where(place == 63, 0.0, w2).astype(F32)

    def kg_rows(colour, a, at):
        return kg[colour, a // 4, a % 4, at]

    at = slice(8, 40)
    for colour in (0, 1):
        for a in range(16):
            other = kg_rows(1 - colour, a, at)
            before = kg_rows(1 - colour, max(a - 1, 0), at)
            after = kg_rows(1 - colour, min(a + 1, 15), at)
            w_cross = w2
            if a == 0:
                w_cross = jnp.where(first_32[colour], 0.0, w2).astype(F32)
            if a == 15:
                w_cross = jnp.where(first_32[colour], w2, 0.0).astype(F32)
            low, high = beside_2(
                kg_rows(1 - colour, a, slice(7, 39)), kg_rows(1 - colour, a, slice(9, 41)), low_32, odd_32
            )
            parts, total, inverse = couple(
                kg_rows(colour, a, at), other, jnp.where(first_32[colour], before, after), low, high, other,
                (w2, w_cross, wy_low, wy_high, wz_low, wz_high), 1,
            )
            d2[colour, a] = total
            i2[colour, a] = inverse
            for n in range(6):
                c2[colour, n, a] = parts[n]

    lane3 = iota((16, 128), 1)
    even_place = (lane3 & 1) == 0
    place3 = (lane3 & 63) >> 1
    row3 = iota((16, 128), 0)
    low3 = lane3 < 64
    odd3 = (((lane3 >> 6) + place3) & 1) == 1
    first3 = (jnp.logical_not(odd3), odd3)

    lower = even_place

    def level_3_share(p):
        rows = []
        for n in (2 * p, 2 * p + 1):
            both = []
            for a in (n, n + 8):
                row = t2[a, pl.ds(0, 16, stride=2)] + t2[a, pl.ds(1, 16, stride=2)]
                both.append(row + jnp.where(even_place, roll(row, -1), roll(row, 1)))
            rows.append(0.125 * jnp.where(lower, both[0], both[1]))
        return merge(rows[0], rows[1], odd3)

    w3 = 0.5 / 64.0
    wy_low = jnp.where((row3 == 0) & low3, 0.0, w3).astype(F32)
    wy_high = jnp.where((row3 == 15) & (lane3 >= 64), 0.0, w3).astype(F32)
    wz_low = jnp.where(place3 == 0, 0.0, w3).astype(F32)
    wz_high = jnp.where(place3 == 31, 0.0, w3).astype(F32)
    at3 = slice(8, 24)

    def around_3(ref, colour, p, first):
        here = ref[colour, p, at3]
        before = ref[colour, p - 1, at3] if p else roll(ref[colour, 3, at3], 1)
        after = ref[colour, p + 1, at3] if p < 3 else roll(ref[colour, 0, at3], -1)
        low = roll(jnp.where(low3, here, ref[colour, p, 7:23]), 64)
        high = roll(jnp.where(low3, ref[colour, p, 9:25], here), 64)
        return here, jnp.where(first, before, after), low, high

    for a in range(16):
        t2[a] = kg_rows(0, a, at) + kg_rows(1, a, at)
    for p in range(4):
        k3[0, p, at3], k3[1, p, at3] = level_3_share(p)
    for colour in (0, 1):
        for p in range(4):
            here, cross, low, high = around_3(k3, 1 - colour, p, first3[colour])
            w_cross = w3
            if p == 0:
                w_cross = jnp.where(first3[colour] & lower, 0.0, w3).astype(F32)
            if p == 3:
                w_cross = jnp.where(first3[colour] | lower, w3, 0.0).astype(F32)
            parts, _, inverse = couple(
                k3[colour, p, at3], here, cross, low, high, here, (w3, w_cross, wy_low, wy_high, wz_low, wz_high), 2
            )
            i3[colour, p] = inverse
            for n in range(6):
                c3[colour, n, p] = parts[n]

    halo_wait(
        [send_k, send_v, send_k1, send_s1, send_vk, send_vk1], position, sent.at[0], dummy,
        rows_of(tree_x + tree_y + tree_z + tree_core),
    )
    for x in (0, 1, 3, 2):
        arrive([copy for copy, chip in zip(spread_s, CHIPS) if chip[0] == x], 9 + x)
        share_s[x].start()
    arrive(share_s, 13)

    for colour in (0, 1):
        for a in range(16):
            source = i2[colour, a] * sg[colour, a // 4, a % 4, at]
            s2[colour, a] = source
            if colour == 0:
                v2[0, a + 2, at] = source

    def update_2(colour, a, rows, frame_rows, low, odd, first):
        before, here, after = frame_rows
        row_low, row_high = beside_2(v2[1 - colour, a + 2, before], v2[1 - colour, a + 2, after], low, odd)
        cross = jnp.where(first[colour], v2[1 - colour, a + 1, here], v2[1 - colour, a + 3, here])
        return relax(
            s2[colour, a, rows], [c2[colour, n, a, rows] for n in range(6)], v2[1 - colour, a + 2, here],
            cross, row_low, row_high, 1,
        )

    whole_2 = (slice(0, 32), (slice(7, 39), at, slice(9, 41)), low_32, odd_32, first_32)

    def half_sweep_2(colour):
        for a in range(16):
            v2[colour, a + 2, at] = update_2(colour, a, *whole_2)

    half_sweep_2(1)
    half_sweep_2(0)
    half_sweep_2(1)
    for a in range(16):
        left = [d2[n, a] * (update_2(n, a, *whole_2) - v2[n, a + 2, at]) for n in (0, 1)]
        t2[a] = left[0] + left[1]
    for p in range(4):
        sources = level_3_share(p)
        for colour in (0, 1):
            s3[colour, p] = i3[colour, p] * sources[colour]

    def half_sweep_3(colour):
        for p in range(4):
            here, cross, low, high = around_3(v3, 1 - colour, p, first3[colour])
            v3[colour, p, at3] = relax(
                s3[colour, p], [c3[colour, n, p] for n in range(6)], here, cross, low, high, 2
            )

    for p in range(4):
        v3[0, p, at3] = s3[0, p]
    half_sweep_3(1)
    for _ in range(COARSE_SWEEPS - 1):
        half_sweep_3(0)
        half_sweep_3(1)

    for p in range(4):
        cells = [v3[colour, p, at3] for colour in (0, 1)]
        firsts = [jnp.where(lower, c, roll(c, 1)) for c in cells]
        seconds = [jnp.where(lower, roll(c, -1), c) for c in cells]
        for pair, (red, black) in ((p, firsts), (p + 4, seconds)):
            for n, row in enumerate((jnp.where(odd3, black, red), jnp.where(odd3, red, black))):
                p2[2 * pair + n, pl.ds(0, 16, stride=2)] = row
                p2[2 * pair + n, pl.ds(1, 16, stride=2)] = row

    def within(value, top, span):
        value = value * ((value + span) // span)
        value = top - value
        return top - value * ((value + span) // span)

    a0 = 2 * within(gx - 2, 3, 8)
    r0 = 2 * within(gy - 2, 8, 16)
    strip = pl.ds(r0, 16)
    part_2 = (strip, (pl.ds(r0 + 7, 16), pl.ds(r0 + 8, 16), pl.ds(r0 + 9, 16)), *two_columns(16), first_16)
    for n in range(10):
        v2[1, a0 + n + 2, pl.ds(r0 + 8, 16)] = v2[1, a0 + n + 2, pl.ds(r0 + 8, 16)] + p2[a0 + n, strip]
    for colour in (0, 1, 0, 1):
        news = [update_2(colour, a0 + n, *part_2) for n in range(10)]
        for n, new in enumerate(news):
            v2[colour, a0 + n + 2, pl.ds(r0 + 8, 16)] = new

    spot = iota((8, 128), 1) >> 1
    for d in range(-3, 7):
        cells = (2 * gx + d // 2 + 2, pl.ds(2 * gy + 6, 8))
        coarse = jnp.where(odd_8 == (d % 2 == 1), v2[(0,) + cells], v2[(1,) + cells])
        q1[d + 3, 0] = jnp.take_along_axis(coarse, spot, axis=1)
        q1[d + 3, 1] = jnp.take_along_axis(coarse, spot + 64, axis=1)
    for d in range(10):
        for n in range(2):
            for m in range(2):
                column = q1[d, n, pl.ds(m, 4, stride=2)]
                p1[d, pl.ds(4 * n + 2 * m, 4, stride=8)] = column
                p1[d, pl.ds(4 * n + 2 * m + 1, 4, stride=8)] = column
    halo_wait([send_vk1], position, arrived.at[5], dummy)
    for a in range(-3, 7):
        v1[1, a + 4, 10:30] = vk1[a + 4, 10:30] + p1[a + 3, 2:22]
    half_sweep_1(0, -3, 7, -6, 18)
    half_sweep_1(1, -2, 6, -4, 12)
    half_sweep_1(0, -2, 6, -4, 12)
    half_sweep_1(1, -1, 5, -4, 12)

    odd_12 = (iota((12, 128), 0) + iota((12, 128), 1)) & 1
    for i in range(-2, 10):
        a = i // 2
        row = jnp.where(odd_12 == i % 2, v1[0, a + 4, 14:26], v1[1, a + 4, 14:26])
        p0[i + 2, pl.ds(0, 12, stride=2)] = row
        p0[i + 2, pl.ds(1, 12, stride=2)] = row
    halo_wait([send_vk], position, arrived.at[4], dummy)
    for i in range(-4, 20):
        vx[1, i + 5, 4:28] = vk[i + 5, 4:28] + p0[i // 2 + 2]
    half_sweep_0(0, -4, 20)
    half_sweep_0(1, -2, 18)
    half_sweep_0(0, -2, 18)
    for i in range(0, 16, 2):
        out[0, i:i + 2] = vx[0, i + 5:i + 7, 8:24]
        out[1, i:i + 2] = update_0(1, i, 0, 16, even_16)

    wait_rows(rows_of(spread_s + share_s), sent.at[1], dummy)


def join(cells, out, rows, sems):
    lane = iota((16, 128), 1)
    odd_row = iota((16, 128), 0) & 1
    low = lane < 64
    half = lane >> 1
    copies = []
    for i in range(16):
        red, turned = cells[0, i], roll(cells[1, i], 64)
        left, right = jnp.where(low, red, turned), jnp.where(low, turned, red)
        same = (lane & 1) == (odd_row ^ (i & 1))
        rows[i, :, :128] = jnp.take_along_axis(left, half + jnp.where(same, 0, 64), axis=1)
        rows[i, :, 128:] = jnp.take_along_axis(right, half + jnp.where(same, 64, 0), axis=1)
        if i % 4 == 3:
            part = pl.ds(i - 3, 4)
            copies.append(pltpu.make_async_copy(rows.at[part], out.at[part], sems.at[i // 4]))
            copies[-1].start()
    for copy in copies:
        copy.wait()


def v_cycle(image, conduct):
    def vmem(*shape):
        return pltpu.VMEM(shape, F32)

    frame0, frame1, gathered = (26, 32, 128), (12, 40, 128), (2, 4, 4, 48, 128)
    cells = pl.pallas_call(
        kernel,
        out_shape=jax.ShapeDtypeStruct((2, 16, 16, 128), F32),
        in_specs=[pl.BlockSpec(memory_space=pltpu.HBM)] * 2,
        out_specs=pl.BlockSpec(memory_space=pltpu.VMEM),
        scratch_shapes=[
            vmem(16, 16, 256), vmem(16, 16, 256),
            vmem(2, *frame0), vmem(2, *frame0), vmem(2, 16, 16, 128), vmem(*frame0), vmem(2, 6, 24, 24, 128),
            vmem(2, 24, 24, 128), vmem(2, 24, 24, 128), vmem(8, 16, 128), vmem(12, 24, 128),
            vmem(2, *frame1), vmem(2, *frame1), vmem(2, *frame1), vmem(*frame1), vmem(2, 6, 10, 24, 128),
            vmem(2, 10, 24, 128), vmem(2, 10, 24, 128), vmem(2, 10, 24, 128), vmem(4, 8, 128), vmem(10, 32, 128),
            vmem(10, 2, 8, 128), vmem(2, 2, 2, 2, 128), vmem(*gathered), vmem(*gathered), vmem(2, 20, 48, 128),
            vmem(2, 6, 16, 32, 128), vmem(2, 16, 32, 128), vmem(2, 16, 32, 128), vmem(2, 16, 32, 128), vmem(16, 32, 128),
            vmem(16, 32, 128),
            vmem(2, 4, 32, 128), vmem(2, 4, 32, 128), vmem(2, 6, 4, 16, 128), vmem(2, 4, 16, 128),
            vmem(2, 4, 16, 128), vmem(4096, 128),
            pltpu.SemaphoreType.DMA((2,)), pltpu.SemaphoreType.DMA((15,)), pltpu.SemaphoreType.DMA((2,)),
            pltpu.SemaphoreType.REGULAR((2,)),
        ],
        compiler_params=pltpu.CompilerParams(
            collective_id=0, has_side_effects=True, vmem_limit_bytes=48 * 2**20
        ),
        name="v_cycle",
    )(*(pltpu.with_memory_space_constraint(array, pltpu.HBM) for array in (image, conduct)))
    return pl.pallas_call(
        join,
        out_shape=jax.ShapeDtypeStruct((16, 16, 256), F32),
        in_specs=[pl.BlockSpec(memory_space=pltpu.VMEM)],
        out_specs=pl.BlockSpec(memory_space=pltpu.HBM),
        scratch_shapes=[vmem(16, 16, 256), pltpu.SemaphoreType.DMA((4,))],
        compiler_params=pltpu.CompilerParams(vmem_limit_bytes=8 * 2**20),
        name="join",
    )(cells)


def solution(mesh):
    return jax.shard_map(
        v_cycle,
        mesh=mesh,
        in_specs=(P("gx", "gy", None), P("gx", "gy", None)),
        out_specs=P("gx", "gy", None),
        check_vma=False,
    )
```

```python
import math

import jax
import jax.numpy as jnp
from jax import lax
from jax.experimental import pallas as pl
from jax.experimental.pallas import tpu as pltpu
from jax.sharding import PartitionSpec as P

COARSE_SWEEPS = 8
MESH = pl.DeviceIdType.MESH
F32 = jnp.float32
GX, GY = 8, 16
DIRECTIONS = [(-1, -1), (-1, 1), (1, -1), (1, 1), (0, -1), (0, 1), (-1, 0), (1, 0)]
CHIPS = sorted(
    [(x, y, z) for x in range(4) for y in range(4) for z in range(4) if (x, y, z) != (0, 0, 0)],
    key=lambda d: -sum(min(c, 4 - c) for c in d),
)


def nearness(offset):
    return max(min(offset[0], GX - offset[0]), min(offset[1], GY - offset[1]))


def iota(shape, dim):
    return lax.broadcasted_iota(jnp.int32, shape, dim)


def roll(values, shift):
    return pltpu.roll(values, shift % 128, values.ndim - 1)


def halo_copies(src, src_origin, dst, origin, extent, widths, sems, position, corners=None, colour=None):
    gx, gy = position
    lead = (slice(None),) * (len(dst.shape) - 3) if colour is None else (colour,)

    def piece(step, size, here, there, start, stop):
        if step == 0:
            return slice(here, here + size), slice(there, there + size)
        if step > 0:
            return slice(here + size - stop, here + size - start), slice(there - stop, there - start)
        return slice(here + start, here + stop), slice(there + size + start, there + size + stop)

    copies = []
    for dx, dy in DIRECTIONS:
        boxes = [((0, widths[0]), (0, widths[1]))]
        if dx and dy and corners is not None:
            boxes = [((start, stop), (0, width)) for start, stop, width in corners]
        group = []
        for box_x, box_y in boxes:
            src_x, dst_x = piece(dx, extent[0], src_origin[0], origin[0], *box_x)
            src_y, dst_y = piece(dy, extent[1], src_origin[1], origin[1], *box_y)
            group.append(
                pltpu.make_async_remote_copy(
                    src_ref=src.at[lead + (src_x, src_y)],
                    dst_ref=dst.at[lead + (dst_x, dst_y)],
                    send_sem=sems[0],
                    recv_sem=sems[1],
                    device_id=(lax.rem(gx + dx + GX, GX), lax.rem(gy + dy + GY, GY)),
                    device_id_type=MESH,
                )
            )
        copies.append((in_grid(gx + dx, gy + dy), group))
    return copies


def in_grid(x, y):
    return (x >= 0) & (x < GX) & (y >= 0) & (y < GY)


def halo_start(copies):
    for sends, group in copies:

        @pl.when(sends)
        def _():
            for copy in group:
                copy.start()


def rows_of(group):
    return sum(math.prod(copy.src_ref.shape[:-1]) for copy in group)


def wait_rows(rows, sem, room):
    pltpu.make_async_copy(room.at[0:rows], room.at[0:rows], sem).wait()


def halo_wait(exchanges, position, sem, room, more=0):
    edge_x = (position[0] == 0) | (position[0] == GX - 1)
    edge_y = (position[1] == 0) | (position[1] == GY - 1)
    rows = {direction: 0 for direction in DIRECTIONS}
    for copies in exchanges:
        for direction, (_, group) in zip(DIRECTIONS, copies):
            rows[direction] += rows_of(group)
    for at_x in (False, True):
        for at_y in (False, True):
            lost = [(dx, dy) for dx, dy in DIRECTIONS if (at_x and dx == 1) or (at_y and dy == 1)]
            total = more + sum(rows.values()) - sum(rows[direction] for direction in lost)

            @pl.when((edge_x == at_x) & (edge_y == at_y))
            def _():
                wait_rows(total, sem, room)


def couple(here, same, cross, low, high, other, weights, z_step):
    w, w_cross, w_low, w_high, w_below, w_above = weights
    parts = [
        (here + same) * w,
        (here + cross) * w_cross,
        (here + low) * w_low,
        (here + high) * w_high,
        (here + roll(other, z_step)) * w_below,
        (here + roll(other, -z_step)) * w_above,
    ]
    total = ((parts[0] + parts[1]) + (parts[2] + parts[3])) + ((parts[4] + parts[5]) + 1.0)
    inverse = 1.0 / total
    return [part * inverse for part in parts], total, inverse


def relax(source, couplings, same, cross, low, high, z_step):
    acc0 = source + couplings[0] * same
    acc1 = couplings[4] * roll(same, z_step) + couplings[5] * roll(same, -z_step)
    acc2 = couplings[2] * low + couplings[3] * high
    return (acc0 + acc2) + (acc1 + couplings[1] * cross)


def kernel(
    image, conduct, out,
    image_in, conduct_in, kx, vx, vs, vk, c0, s0, d0, t0, p0,
    k1, s1x, v1, vk1, c1, s1, i1, d1, t1, p1,
    q1, own2, kg, sg, v2, c2, s2, i2, d2, t2, p2,
    k3, v3, c3, s3, i3, dummy,
    sent, arrived, in_sems, known_sems,
):
    gx, gy = lax.axis_index("gx"), lax.axis_index("gy")
    chip_x, core = gx // 2, lax.rem(gx, 2)
    chip_z, chip_y = gy // 4, lax.rem(gy, 4)
    sibling = (chip_x * 2 + 1 - core, gy)
    chips = [
        (lax.rem(chip_x + x, 4) * 2 + core, lax.rem(chip_z + z, 4) * 4 + lax.rem(chip_y + y, 4))
        for x, y, z in CHIPS
    ]
    position = (gx, gy)

    barrier = pltpu.get_barrier_semaphore()

    fetch_k = pltpu.make_async_copy(conduct, conduct_in, in_sems.at[0])
    fetch_v = pltpu.make_async_copy(image, image_in, in_sems.at[1])
    fetch_k.start()
    fetch_v.start()

    def near(steps):
        offsets = sorted({(x % GX, y % GY) for x in steps for y in steps} - {(0, 0)}, key=nearness)
        return [(lax.rem(gx + x, GX), lax.rem(gy + y, GY)) for x, y in offsets]

    def tell(n):
        for peer in near((0, 2 << n, -2 << n)):
            pl.semaphore_signal(known_sems.at[n], inc=1, device_id=peer, device_id_type=MESH)

    def hear(n):
        pl.semaphore_wait(known_sems.at[n], len(near((0, 2 << n, -2 << n))))

    greeted = near(range(-2, 3)) + [(lax.rem(gx + 4, GX), gy)]
    for peer in greeted:
        pl.semaphore_signal(barrier, inc=1, device_id=peer, device_id_type=MESH)

    lane0 = iota((16, 128), 1)
    odd_row = iota((16, 128), 0) & 1
    low0 = lane0 < 64
    half_lane = (lane0 & 63) * 2

    def split(values, par):
        parity = odd_row ^ par
        first = half_lane + jnp.where(low0, parity, 1 - parity)
        second = half_lane + jnp.where(low0, 1 - parity, parity)
        left = jnp.take_along_axis(values[:, :128], first, axis=1)
        right = jnp.take_along_axis(values[:, 128:], second, axis=1)
        return jnp.where(low0, left, right), roll(jnp.where(low0, right, left), 64)

    nothing = jnp.zeros((2, 4, 4, 8, 128), F32)
    kg[:, :, :, 0:8], kg[:, :, :, 40:48] = nothing, nothing
    nothing = jnp.zeros((2, 20, 8, 128), F32)
    v2[:, :, 0:8], v2[:, :, 40:48] = nothing, nothing
    nothing = jnp.zeros((2, 2, 48, 128), F32)
    v2[:, 0:2], v2[:, 18:20] = nothing, nothing
    nothing = jnp.zeros((2, 4, 8, 128), F32)
    for ref in (k3, v3):
        ref[:, :, 0:8], ref[:, :, 24:32] = nothing, nothing

    def zero(ref, *at):
        at = (slice(None),) * (len(ref.shape) - 3) + at
        ref[at] = jnp.zeros(ref.at[at].shape, F32)

    for edge, rows0, rows1 in ((gx == 0, slice(0, 5), slice(0, 4)), (gx == GX - 1, slice(21, 26), slice(8, 12))):

        @pl.when(edge)
        def _():
            for ref in (kx, vx, vk):
                zero(ref, rows0)
            for ref in (k1, s1x, vk1):
                zero(ref, rows1)

    for edge, cols0, cols1 in ((gy == 0, slice(0, 8), slice(8, 16)), (gy == GY - 1, slice(24, 32), slice(24, 32))):

        @pl.when(edge)
        def _():
            for ref in (kx, vx, vk):
                zero(ref, slice(None), cols0)
            for ref in (k1, s1x, vk1):
                zero(ref, slice(None), cols1)

    for i in range(16):
        if i == 0:
            fetch_k.wait()
        kx[0, i + 5, 8:24], kx[1, i + 5, 8:24] = split(conduct_in[i], i & 1)

    pl.semaphore_wait(barrier, len(greeted))
    def halos(src, src_origin, dst, origin, extent, which, *cones):
        sems = (sent.at[0], arrived.at[which])
        each = [
            halo_copies(src, src_origin, dst, origin, extent, widths, sems, position, corners, colour)
            for colour, widths, corners in cones
        ]
        return [(ways[0][0], sum((group for _, group in ways), [])) for ways in zip(*each)]

    cones = (1, (5, 5), [(0, 2, 4), (2, 4, 2)]), (0, (4, 4), [(0, 3, 3)])
    send_k = halos(kx, (5, 8), kx, (5, 8), (16, 16), 0, *cones)
    send_v = halos(vs, (0, 0), vx, (5, 8), (16, 16), 1, *cones)
    tell(0)
    halo_start(send_k)
    fetch_v.wait()
    for i in range(16):
        red, black = split(image_in[i], i & 1)
        vx[0, i + 5, 8:24], vx[1, i + 5, 8:24] = red, black
        vs[0, i], vs[1, i] = red, black
    halo_start(send_v)

    def block_mean():
        return [0.125 * (t0[i, pl.ds(0, 8, stride=2)] + t0[i, pl.ds(1, 8, stride=2)]) for i in range(8)]

    odd_8 = ((iota((8, 128), 0) + iota((8, 128), 1)) & 1) == 1
    odd_2 = ((iota((2, 128), 0) + iota((2, 128), 1)) & 1) == 1
    low_2 = iota((2, 128), 1) < 64
    even_lane = (iota((8, 128), 1) & 63) * 2

    def merge(first, second, odd):
        return jnp.where(odd, second, first), jnp.where(odd, first, second)

    def level_2_share(kind, pairs, whole):
        rows = []
        for i in range(4):
            t1[i] = jnp.take_along_axis(pairs[i], even_lane, axis=1) + jnp.take_along_axis(pairs[i], even_lane + 1, axis=1)
        for i in range(4):
            first = t1[i, pl.ds(0, 2, stride=2)] + t1[i, pl.ds(1, 2, stride=2)]
            second = t1[i, pl.ds(4, 2, stride=2)] + t1[i, pl.ds(5, 2, stride=2)]
            rows.append(0.125 * jnp.where(low_2, first, second))
        for a in range(2):
            cells = merge(rows[2 * a], rows[2 * a + 1], odd_2)
            for colour in (0, 1):
                own2[kind, colour, a] = cells[colour]
                whole[colour, chip_x, 2 * core + a, pl.ds(8 + 2 * gy, 2)] = cells[colour]

    def remote(src, dst, which, device):
        return pltpu.make_async_remote_copy(
            src_ref=src, dst_ref=dst, send_sem=sent.at[int(9 <= which <= 13)], recv_sem=arrived.at[which], device_id=device, device_id_type=MESH
        )

    cores_rows = pl.ds(2 * core, 2)
    own_place = (slice(None), chip_x, cores_rows, pl.ds(8 + 2 * gy, 2))

    spread_s = [
        remote(own2.at[1], sg.at[own_place], 9 + x, chip) for chip, (x, _, _) in zip(chips, CHIPS)
    ]
    planes = [sg.at[:, lax.rem(chip_x + 4 - x, 4), cores_rows, 8:40] for x in range(4)]
    share_s = [remote(plane, plane, 13, sibling) for plane in planes]

    def arrive(copies, which):
        wait_rows(rows_of(copies), arrived.at[which], dummy)

    def chip_at(x, y, z):
        return (
            lax.rem(chip_x + x, 4) * 2 + core,
            lax.rem(chip_z + z, 4) * 4 + lax.rem(chip_y + y, 4),
        )

    row = kg.at[:, :, cores_rows, pl.ds(8 + 2 * gy, 2)]
    sheet = kg.at[:, :, cores_rows, pl.ds(8 + 8 * chip_z, 8)]
    half = kg.at[:, :, cores_rows, 8:40]
    tree_x = [remote(own2.at[0], kg.at[own_place], 6, chip_at(n, 0, 0)) for n in (2, 1, 3)]
    tree_y = [remote(row, row, 7, chip_at(0, n, 0)) for n in (2, 1, 3)]
    tree_z = [remote(sheet, sheet, 14, chip_at(0, 0, n)) for n in (2, 1, 3)]
    tree_core = [remote(half, half, 8, sibling)]

    for i in range(8):
        e = 2 * i + 5
        t0[i] = (kx[0, e, 8:24] + kx[1, e, 8:24]) + (kx[0, e + 1, 8:24] + kx[1, e + 1, 8:24])
    rows = block_mean()
    for a in range(4):
        k1[0, a + 4, 16:24], k1[1, a + 4, 16:24] = merge(rows[2 * a], rows[2 * a + 1], odd_8)
    level_2_share(0, [rows[2 * a] + rows[2 * a + 1] for a in range(4)], kg)
    send_k1 = halos(k1, (4, 16), k1, (4, 16), (4, 8), 2, (0, (3, 5), [(0, 1, 5), (1, 3, 3)]), (1, (3, 6), [(0, 1, 6), (1, 3, 4)]))
    halo_start(send_k1)

    shape = (2, 24, 128)
    sub, lanes = iota(shape, 1), iota(shape, 2)
    even_row = ((iota(shape, 0) + sub) & 1) == 0
    wy_low = jnp.where((sub == 4) & (gy == 0), 0.0, 0.5).astype(F32)
    wy_high = jnp.where((sub == 19) & (gy == GY - 1), 0.0, 0.5).astype(F32)
    wx_low = jnp.where(gx == 0, 0.0, 0.5).astype(F32)
    wx_high = jnp.where(gx == GX - 1, 0.0, 0.5).astype(F32)
    wz = [
        jnp.where(even_row, jnp.where(lanes == 0, 0.0, 0.5), jnp.where(lanes == 127, 0.0, 0.5)).astype(F32),
        jnp.where(even_row, jnp.where(lanes == 127, 0.0, 0.5), jnp.where(lanes == 0, 0.0, 0.5)).astype(F32),
    ]

    def beside(values, colour, even):
        step = 1 if colour == 0 else -1
        first = roll(jnp.where(even, values[0], values[1]), step)
        second = roll(jnp.where(even, values[1], values[0]), -step)
        return jnp.stack([jnp.where(even, first, second), jnp.where(even, second, first)])

    even_24 = (iota((24, 128), 0) & 1) == 0
    even_16 = (iota((16, 128), 0) & 1) == 0

    row_index = iota((2, 1, 1), 0)

    def couplings_0(colour, start, stop):
        for i in range(start, stop, 2):
            e = i + 5
            here, other = kx[colour, e:e + 2, 4:28], kx[1 - colour, e:e + 2, 4:28]
            wx_l = jnp.where(row_index == 0, wx_low, 0.5) if i == 0 else 0.5
            wx_h = jnp.where(row_index == 1, wx_high, 0.5) if i == 14 else 0.5
            parts = [
                (here + kx[1 - colour, e - 1:e + 1, 4:28]) * wx_l,
                (here + kx[1 - colour, e + 1:e + 3, 4:28]) * wx_h,
                (here + kx[1 - colour, e:e + 2, 3:27]) * wy_low,
                (here + kx[1 - colour, e:e + 2, 5:29]) * wy_high,
                (here + other) * 0.5,
                (here + beside(other, colour, even_24)) * wz[colour],
            ]
            total = ((parts[0] + parts[1]) + (parts[2] + parts[3])) + ((parts[4] + parts[5]) + 1.0)
            inverse = 1.0 / total
            d0[colour, i + 4:i + 6] = total
            s0[colour, i + 4:i + 6] = inverse
            for n in range(6):
                c0[colour, n, i + 4:i + 6] = parts[n] * inverse

    def update_0(colour, i, lo, hi, rows_even):
        e, f = i + 5, i + 4
        a, b = lo + 8, hi + 8
        here = slice(lo + 4, hi + 4)
        other = vx[1 - colour, e:e + 2, a:b]
        acc0 = s0[colour, f:f + 2, here] + c0[colour, 0, f:f + 2, here] * vx[1 - colour, e - 1:e + 1, a:b]
        acc1 = c0[colour, 1, f:f + 2, here] * vx[1 - colour, e + 1:e + 3, a:b]
        acc1 += c0[colour, 2, f:f + 2, here] * vx[1 - colour, e:e + 2, a - 1:b - 1]
        acc2 = c0[colour, 3, f:f + 2, here] * vx[1 - colour, e:e + 2, a + 1:b + 1]
        acc2 += c0[colour, 4, f:f + 2, here] * other
        acc3 = c0[colour, 5, f:f + 2, here] * beside(other, colour, rows_even)
        return (acc0 + acc1) + (acc2 + acc3)

    def half_sweep_0(colour, start, stop, lo=-4, hi=20):
        rows_even = even_24 if hi - lo == 24 else even_16
        for i in range(start, stop, 2):
            vx[colour, i + 5:i + 7, lo + 8:hi + 8] = update_0(colour, i, lo, hi, rows_even)

    for copy in tree_x:
        copy.start()
    halo_wait([send_k], position, arrived.at[0], dummy)
    couplings_0(0, -4, 20)
    couplings_0(1, -4, 20)
    hear(0)
    tell(1)
    arrive(tree_x, 6)
    for copy in tree_y:
        copy.start()
    halo_wait([send_v], position, arrived.at[1], dummy)
    for colour in (0, 1):
        for i in range(-4, 20, 2):
            s0[colour, i + 4:i + 6] = s0[colour, i + 4:i + 6] * vx[colour, i + 5:i + 7, 4:28]

    half_sweep_0(0, -4, 20)
    half_sweep_0(1, -4, 20)
    half_sweep_0(0, -2, 18)
    half_sweep_0(1, -2, 18)

    def residual_0(i):
        total = None
        for colour in (0, 1):
            left = update_0(colour, i, 0, 16, even_16) - vx[colour, i + 5:i + 7, 8:24]
            left = d0[colour, i + 4:i + 6, 4:20] * left
            total = left if total is None else total + left
        return total

    for i in range(8):
        both = residual_0(2 * i)
        t0[i] = both[0] + both[1]
    rows = block_mean()
    for a in range(4):
        s1x[0, a + 4, 16:24], s1x[1, a + 4, 16:24] = merge(rows[2 * a], rows[2 * a + 1], odd_8)
    send_s1 = halos(s1x, (4, 16), s1x, (4, 16), (4, 8), 3, (None, (3, 5), [(0, 1, 5), (1, 3, 3)]))
    halo_start(send_s1)


    shape = (24, 128)
    col, lanes = iota(shape, 0) - 6, iota(shape, 1)
    w1 = 0.5 / 4.0
    wy_low = jnp.where((col == 0) & (gy == 0), 0.0, w1).astype(F32)
    wy_high = jnp.where((col == 7) & (gy == GY - 1), 0.0, w1).astype(F32)
    wx_low = jnp.where(gx == 0, 0.0, w1).astype(F32)
    wx_high = jnp.where(gx == GX - 1, 0.0, w1).astype(F32)
    wz_low = jnp.where(lanes == 0, 0.0, w1).astype(F32)
    wz_high = jnp.where(lanes == 127, 0.0, w1).astype(F32)

    def first_of_pair(size, origin):
        odd = (iota((size, 128), 0) + iota((size, 128), 1) + origin) & 1
        return odd == 0, odd == 1

    first_24, first_16, first_8 = first_of_pair(24, 0), first_of_pair(16, 0), first_of_pair(8, 0)

    halo_wait([send_k1], position, arrived.at[2], dummy)
    for colour in (0, 1):
        for a in range(-3, 7):
            e, f = a + 4, a + 3
            other = k1[1 - colour, e, 10:34]
            first = first_24[colour]
            w_cross = w1
            if a in (0, 3):
                w_cross = jnp.where(first, wx_low if a == 0 else w1, wx_high if a == 3 else w1)
            parts, total, inverse = couple(
                k1[colour, e, 10:34], other, jnp.where(first, k1[1 - colour, e - 1, 10:34], k1[1 - colour, e + 1, 10:34]),
                k1[1 - colour, e, 9:33], k1[1 - colour, e, 11:35], other, (w1, w_cross, wy_low, wy_high, wz_low, wz_high), 1,
            )
            d1[colour, f] = total
            i1[colour, f] = inverse
            for n in range(6):
                c1[colour, n, f] = parts[n]

    def update_1(colour, a, lo, hi):
        e, f = a + 4, a + 3
        here, at = slice(lo + 6, hi + 6), slice(lo + 16, hi + 16)
        first = {24: first_24, 16: first_16, 8: first_8}[hi - lo][colour]
        return relax(
            s1[colour, f, here], [c1[colour, n, f, here] for n in range(6)], v1[1 - colour, e, at],
            jnp.where(first, v1[1 - colour, e - 1, at], v1[1 - colour, e + 1, at]),
            v1[1 - colour, e, lo + 15:hi + 15], v1[1 - colour, e, lo + 17:hi + 17], 1,
        )

    def half_sweep_1(colour, start, stop, lo, hi):
        for a in range(start, stop):
            v1[colour, a + 4, lo + 16:hi + 16] = update_1(colour, a, lo, hi)

    hear(1)
    arrive(tree_y, 7)
    for copy in tree_z:
        copy.start()

    vk[5:21, 8:24] = vx[1, 5:21, 8:24]
    send_vk = halos(vk, (5, 8), vk, (5, 8), (16, 16), 4, (None, (4, 4), None))
    halo_start(send_vk)
    halo_wait([send_s1], position, arrived.at[3], dummy)
    for colour in (0, 1):
        for a in range(-3, 7):
            s1[colour, a + 3] = i1[colour, a + 3] * s1x[colour, a + 4, 10:34]
    for a in range(-2, 6):
        v1[0, a + 4, 12:28] = s1[0, a + 3, 2:18]
    half_sweep_1(1, -2, 6, -4, 12)
    half_sweep_1(0, -1, 5, -4, 12)
    half_sweep_1(1, -1, 5, -4, 12)
    pairs = []
    for a in range(4):
        left = [d1[n, a + 3, 6:14] * (update_1(n, a, 0, 8) - v1[n, a + 4, 16:24]) for n in (0, 1)]
        pairs.append(left[0] + left[1])
    level_2_share(1, pairs, sg)
    for copy in spread_s:
        copy.start()
    arrive(tree_z, 14)
    tree_core[0].start()
    vk1[4:8, 16:24] = v1[1, 4:8, 16:24]
    send_vk1 = halos(vk1, (4, 16), vk1, (4, 16), (4, 8), 5, (None, (3, 6), None))
    halo_start(send_vk1)

    arrive(tree_core, 8)
    def two_columns(size):
        return iota((size, 128), 1) < 64, (iota((size, 128), 0) & 1) == 1

    def beside_2(row_low, row_high, low, odd):
        turned = roll(jnp.where(low, row_high, row_low), 64)
        return jnp.where(odd, row_low, turned), jnp.where(odd, turned, row_high)

    lane = iota((32, 128), 1)
    place = lane & 63
    j_row = iota((32, 128), 0)
    low_32, odd_32 = two_columns(32)
    first_32 = first_of_pair(32, 0)
    w2 = 0.5 / 16.0
    wy_low = jnp.where((j_row == 0) & low_32, 0.0, w2).astype(F32)
    wy_high = jnp.where((j_row == 31) & (lane >= 64), 0.0, w2).astype(F32)
    wz_low = jnp.where(place == 0, 0.0, w2).astype(F32)
    wz_high = jnp.where(place == 63, 0.0, w2).astype(F32)

    def kg_rows(colour, a, at):
        return kg[colour, a // 4, a % 4, at]

    at = slice(8, 40)
    for colour in (0, 1):
        for a in range(16):
            other = kg_rows(1 - colour, a, at)
            before = kg_rows(1 - colour, max(a - 1, 0), at)
            after = kg_rows(1 - colour, min(a + 1, 15), at)
            w_cross = w2
            if a == 0:
                w_cross = jnp.where(first_32[colour], 0.0, w2).astype(F32)
            if a == 15:
                w_cross = jnp.where(first_32[colour], w2, 0.0).astype(F32)
            low, high = beside_2(
                kg_rows(1 - colour, a, slice(7, 39)), kg_rows(1 - colour, a, slice(9, 41)), low_32, odd_32
            )
            parts, total, inverse = couple(
                kg_rows(colour, a, at), other, jnp.where(first_32[colour], before, after), low, high, other,
                (w2, w_cross, wy_low, wy_high, wz_low, wz_high), 1,
            )
            d2[colour, a] = total
            i2[colour, a] = inverse
            for n in range(6):
                c2[colour, n, a] = parts[n]

    lane3 = iota((16, 128), 1)
    even_place = (lane3 & 1) == 0
    place3 = (lane3 & 63) >> 1
    row3 = iota((16, 128), 0)
    low3 = lane3 < 64
    odd3 = (((lane3 >> 6) + place3) & 1) == 1
    first3 = (jnp.logical_not(odd3), odd3)

    lower = even_place

    def level_3_share(p):
        rows = []
        for n in (2 * p, 2 * p + 1):
            both = []
            for a in (n, n + 8):
                row = t2[a, pl.ds(0, 16, stride=2)] + t2[a, pl.ds(1, 16, stride=2)]
                both.append(row + jnp.where(even_place, roll(row, -1), roll(row, 1)))
            rows.append(0.125 * jnp.where(lower, both[0], both[1]))
        return merge(rows[0], rows[1], odd3)

    w3 = 0.5 / 64.0
    wy_low = jnp.where((row3 == 0) & low3, 0.0, w3).astype(F32)
    wy_high = jnp.where((row3 == 15) & (lane3 >= 64), 0.0, w3).astype(F32)
    wz_low = jnp.where(place3 == 0, 0.0, w3).astype(F32)
    wz_high = jnp.where(place3 == 31, 0.0, w3).astype(F32)
    at3 = slice(8, 24)

    def around_3(ref, colour, p, first):
        here = ref[colour, p, at3]
        before = ref[colour, p - 1, at3] if p else roll(ref[colour, 3, at3], 1)
        after = ref[colour, p + 1, at3] if p < 3 else roll(ref[colour, 0, at3], -1)
        low = roll(jnp.where(low3, here, ref[colour, p, 7:23]), 64)
        high = roll(jnp.where(low3, ref[colour, p, 9:25], here), 64)
        return here, jnp.where(first, before, after), low, high

    for a in range(16):
        t2[a] = kg_rows(0, a, at) + kg_rows(1, a, at)
    for p in range(4):
        k3[0, p, at3], k3[1, p, at3] = level_3_share(p)
    for colour in (0, 1):
        for p in range(4):
            here, cross, low, high = around_3(k3, 1 - colour, p, first3[colour])
            w_cross = w3
            if p == 0:
                w_cross = jnp.where(first3[colour] & lower, 0.0, w3).astype(F32)
            if p == 3:
                w_cross = jnp.where(first3[colour] | lower, w3, 0.0).astype(F32)
            parts, _, inverse = couple(
                k3[colour, p, at3], here, cross, low, high, here, (w3, w_cross, wy_low, wy_high, wz_low, wz_high), 2
            )
            i3[colour, p] = inverse
            for n in range(6):
                c3[colour, n, p] = parts[n]

    for x in (0, 1, 3, 2):
        arrive([copy for copy, chip in zip(spread_s, CHIPS) if chip[0] == x], 9 + x)
        share_s[x].start()
    arrive(share_s, 13)

    for colour in (0, 1):
        for a in range(16):
            source = i2[colour, a] * sg[colour, a // 4, a % 4, at]
            s2[colour, a] = source
            if colour == 0:
                v2[0, a + 2, at] = source

    def update_2(colour, a, rows, frame_rows, low, odd, first):
        before, here, after = frame_rows
        row_low, row_high = beside_2(v2[1 - colour, a + 2, before], v2[1 - colour, a + 2, after], low, odd)
        cross = jnp.where(first[colour], v2[1 - colour, a + 1, here], v2[1 - colour, a + 3, here])
        return relax(
            s2[colour, a, rows], [c2[colour, n, a, rows] for n in range(6)], v2[1 - colour, a + 2, here],
            cross, row_low, row_high, 1,
        )

    whole_2 = (slice(0, 32), (slice(7, 39), at, slice(9, 41)), low_32, odd_32, first_32)

    def half_sweep_2(colour):
        for a in range(16):
            v2[colour, a + 2, at] = update_2(colour, a, *whole_2)

    half_sweep_2(1)
    half_sweep_2(0)
    half_sweep_2(1)
    for a in range(16):
        left = [d2[n, a] * (update_2(n, a, *whole_2) - v2[n, a + 2, at]) for n in (0, 1)]
        t2[a] = left[0] + left[1]
    for p in range(4):
        sources = level_3_share(p)
        for colour in (0, 1):
            s3[colour, p] = i3[colour, p] * sources[colour]

    def half_sweep_3(colour):
        for p in range(4):
            here, cross, low, high = around_3(v3, 1 - colour, p, first3[colour])
            v3[colour, p, at3] = relax(
                s3[colour, p], [c3[colour, n, p] for n in range(6)], here, cross, low, high, 2
            )

    for p in range(4):
        v3[0, p, at3] = s3[0, p]
    half_sweep_3(1)
    for _ in range(COARSE_SWEEPS - 1):
        half_sweep_3(0)
        half_sweep_3(1)

    for p in range(4):
        cells = [v3[colour, p, at3] for colour in (0, 1)]
        firsts = [jnp.where(lower, c, roll(c, 1)) for c in cells]
        seconds = [jnp.where(lower, roll(c, -1), c) for c in cells]
        for pair, (red, black) in ((p, firsts), (p + 4, seconds)):
            for n, row in enumerate((jnp.where(odd3, black, red), jnp.where(odd3, red, black))):
                p2[2 * pair + n, pl.ds(0, 16, stride=2)] = row
                p2[2 * pair + n, pl.ds(1, 16, stride=2)] = row

    def within(value, top, span):
        value = value * ((value + span) // span)
        value = top - value
        return top - value * ((value + span) // span)

    a0 = 2 * within(gx - 2, 3, 8)
    r0 = 2 * within(gy - 2, 8, 16)
    strip = pl.ds(r0, 16)
    part_2 = (strip, (pl.ds(r0 + 7, 16), pl.ds(r0 + 8, 16), pl.ds(r0 + 9, 16)), *two_columns(16), first_16)
    for n in range(10):
        v2[1, a0 + n + 2, pl.ds(r0 + 8, 16)] = v2[1, a0 + n + 2, pl.ds(r0 + 8, 16)] + p2[a0 + n, strip]
    for colour in (0, 1, 0, 1):
        news = [update_2(colour, a0 + n, *part_2) for n in range(10)]
        for n, new in enumerate(news):
            v2[colour, a0 + n + 2, pl.ds(r0 + 8, 16)] = new

    spot = iota((8, 128), 1) >> 1
    for d in range(-3, 7):
        cells = (2 * gx + d // 2 + 2, pl.ds(2 * gy + 6, 8))
        coarse = jnp.where(odd_8 == (d % 2 == 1), v2[(0,) + cells], v2[(1,) + cells])
        q1[d + 3, 0] = jnp.take_along_axis(coarse, spot, axis=1)
        q1[d + 3, 1] = jnp.take_along_axis(coarse, spot + 64, axis=1)
    for d in range(10):
        for n in range(2):
            for m in range(2):
                column = q1[d, n, pl.ds(m, 4, stride=2)]
                p1[d, pl.ds(4 * n + 2 * m, 4, stride=8)] = column
                p1[d, pl.ds(4 * n + 2 * m + 1, 4, stride=8)] = column
    halo_wait([send_vk1], position, arrived.at[5], dummy)
    for a in range(-3, 7):
        v1[1, a + 4, 10:30] = vk1[a + 4, 10:30] + p1[a + 3, 2:22]
    half_sweep_1(0, -3, 7, -6, 18)
    half_sweep_1(1, -2, 6, -4, 12)
    half_sweep_1(0, -2, 6, -4, 12)
    half_sweep_1(1, -1, 5, -4, 12)

    odd_12 = (iota((12, 128), 0) + iota((12, 128), 1)) & 1
    for i in range(-2, 10):
        a = i // 2
        row = jnp.where(odd_12 == i % 2, v1[0, a + 4, 14:26], v1[1, a + 4, 14:26])
        p0[i + 2, pl.ds(0, 12, stride=2)] = row
        p0[i + 2, pl.ds(1, 12, stride=2)] = row
    halo_wait([send_vk], position, arrived.at[4], dummy)
    for i in range(-4, 20):
        vx[1, i + 5, 4:28] = vk[i + 5, 4:28] + p0[i // 2 + 2]
    half_sweep_0(0, -4, 20)
    half_sweep_0(1, -2, 18)
    half_sweep_0(0, -2, 18)
    for i in range(0, 16, 2):
        out[0, i:i + 2] = vx[0, i + 5:i + 7, 8:24]
        out[1, i:i + 2] = update_0(1, i, 0, 16, even_16)

    halo_wait(
        [send_k, send_v, send_k1, send_s1, send_vk, send_vk1], position, sent.at[0], dummy,
        rows_of(tree_x + tree_y + tree_z + tree_core),
    )
    wait_rows(rows_of(spread_s + share_s), sent.at[1], dummy)


def join(cells, out, rows, sems):
    lane = iota((16, 128), 1)
    odd_row = iota((16, 128), 0) & 1
    low = lane < 64
    half = lane >> 1
    copies = []
    for i in range(16):
        red, turned = cells[0, i], roll(cells[1, i], 64)
        left, right = jnp.where(low, red, turned), jnp.where(low, turned, red)
        same = (lane & 1) == (odd_row ^ (i & 1))
        rows[i, :, :128] = jnp.take_along_axis(left, half + jnp.where(same, 0, 64), axis=1)
        rows[i, :, 128:] = jnp.take_along_axis(right, half + jnp.where(same, 64, 0), axis=1)
        if i % 4 == 3:
            part = pl.ds(i - 3, 4)
            copies.append(pltpu.make_async_copy(rows.at[part], out.at[part], sems.at[i // 4]))
            copies[-1].start()
    for copy in copies:
        copy.wait()


def v_cycle(image, conduct):
    def vmem(*shape):
        return pltpu.VMEM(shape, F32)

    frame0, frame1, gathered = (26, 32, 128), (12, 40, 128), (2, 4, 4, 48, 128)
    cells = pl.pallas_call(
        kernel,
        out_shape=jax.ShapeDtypeStruct((2, 16, 16, 128), F32),
        in_specs=[pl.BlockSpec(memory_space=pltpu.HBM)] * 2,
        out_specs=pl.BlockSpec(memory_space=pltpu.VMEM),
        scratch_shapes=[
            vmem(16, 16, 256), vmem(16, 16, 256),
            vmem(2, *frame0), vmem(2, *frame0), vmem(2, 16, 16, 128), vmem(*frame0), vmem(2, 6, 24, 24, 128),
            vmem(2, 24, 24, 128), vmem(2, 24, 24, 128), vmem(8, 16, 128), vmem(12, 24, 128),
            vmem(2, *frame1), vmem(2, *frame1), vmem(2, *frame1), vmem(*frame1), vmem(2, 6, 10, 24, 128),
            vmem(2, 10, 24, 128), vmem(2, 10, 24, 128), vmem(2, 10, 24, 128), vmem(4, 8, 128), vmem(10, 32, 128),
            vmem(10, 2, 8, 128), vmem(2, 2, 2, 2, 128), vmem(*gathered), vmem(*gathered), vmem(2, 20, 48, 128),
            vmem(2, 6, 16, 32, 128), vmem(2, 16, 32, 128), vmem(2, 16, 32, 128), vmem(2, 16, 32, 128), vmem(16, 32, 128),
            vmem(16, 32, 128),
            vmem(2, 4, 32, 128), vmem(2, 4, 32, 128), vmem(2, 6, 4, 16, 128), vmem(2, 4, 16, 128),
            vmem(2, 4, 16, 128), vmem(4096, 128),
            pltpu.SemaphoreType.DMA((2,)), pltpu.SemaphoreType.DMA((15,)), pltpu.SemaphoreType.DMA((2,)),
            pltpu.SemaphoreType.REGULAR((2,)),
        ],
        compiler_params=pltpu.CompilerParams(
            collective_id=0, has_side_effects=True, vmem_limit_bytes=48 * 2**20
        ),
        name="v_cycle",
    )(*(pltpu.with_memory_space_constraint(array, pltpu.HBM) for array in (image, conduct)))
    return pl.pallas_call(
        join,
        out_shape=jax.ShapeDtypeStruct((16, 16, 256), F32),
        in_specs=[pl.BlockSpec(memory_space=pltpu.VMEM)],
        out_specs=pl.BlockSpec(memory_space=pltpu.HBM),
        scratch_shapes=[vmem(16, 16, 256), pltpu.SemaphoreType.DMA((4,))],
        compiler_params=pltpu.CompilerParams(vmem_limit_bytes=8 * 2**20),
        name="join",
    )(cells)


def solution(mesh):
    return jax.shard_map(
        v_cycle,
        mesh=mesh,
        in_specs=(P("gx", "gy", None), P("gx", "gy", None)),
        out_specs=P("gx", "gy", None),
        check_vma=False,
    )
```

```python
import math

import jax
import jax.numpy as jnp
from jax import lax
from jax.experimental import pallas as pl
from jax.experimental.pallas import tpu as pltpu
from jax.sharding import PartitionSpec as P

COARSE_SWEEPS = 8
MESH = pl.DeviceIdType.MESH
F32 = jnp.float32
GX, GY = 8, 16
DIRECTIONS = [(-1, -1), (-1, 1), (1, -1), (1, 1), (0, -1), (0, 1), (-1, 0), (1, 0)]
CHIPS = sorted(
    [(x, y, z) for x in range(4) for y in range(4) for z in range(4) if (x, y, z) != (0, 0, 0)],
    key=lambda d: -sum(min(c, 4 - c) for c in d),
)


def nearness(offset):
    return max(min(offset[0], GX - offset[0]), min(offset[1], GY - offset[1]))


def iota(shape, dim):
    return lax.broadcasted_iota(jnp.int32, shape, dim)


def roll(values, shift):
    return pltpu.roll(values, shift % 128, values.ndim - 1)


def halo_copies(src, src_origin, dst, origin, extent, widths, sems, position, corners=None, colour=None):
    gx, gy = position
    lead = (slice(None),) * (len(dst.shape) - 3) if colour is None else (colour,)

    def piece(step, size, here, there, start, stop):
        if step == 0:
            return slice(here, here + size), slice(there, there + size)
        if step > 0:
            return slice(here + size - stop, here + size - start), slice(there - stop, there - start)
        return slice(here + start, here + stop), slice(there + size + start, there + size + stop)

    copies = []
    for dx, dy in DIRECTIONS:
        boxes = [((0, widths[0]), (0, widths[1]))]
        if dx and dy and corners is not None:
            boxes = [((start, stop), (0, width)) for start, stop, width in corners]
        group = []
        for box_x, box_y in boxes:
            src_x, dst_x = piece(dx, extent[0], src_origin[0], origin[0], *box_x)
            src_y, dst_y = piece(dy, extent[1], src_origin[1], origin[1], *box_y)
            group.append(
                pltpu.make_async_remote_copy(
                    src_ref=src.at[lead + (src_x, src_y)],
                    dst_ref=dst.at[lead + (dst_x, dst_y)],
                    send_sem=sems[0],
                    recv_sem=sems[1],
                    device_id=(lax.rem(gx + dx + GX, GX), lax.rem(gy + dy + GY, GY)),
                    device_id_type=MESH,
                )
            )
        copies.append((in_grid(gx + dx, gy + dy), group))
    return copies


def in_grid(x, y):
    return (x >= 0) & (x < GX) & (y >= 0) & (y < GY)


def halo_start(copies):
    for sends, group in copies:

        @pl.when(sends)
        def _():
            for copy in group:
                copy.start()


def rows_of(group):
    return sum(math.prod(copy.src_ref.shape[:-1]) for copy in group)


def wait_rows(rows, sem, room):
    pltpu.make_async_copy(room.at[0:rows], room.at[0:rows], sem).wait()


def halo_wait(exchanges, position, sem, room, more=0):
    edge_x = (position[0] == 0) | (position[0] == GX - 1)
    edge_y = (position[1] == 0) | (position[1] == GY - 1)
    rows = {direction: 0 for direction in DIRECTIONS}
    for copies in exchanges:
        for direction, (_, group) in zip(DIRECTIONS, copies):
            rows[direction] += rows_of(group)
    for at_x in (False, True):
        for at_y in (False, True):
            lost = [(dx, dy) for dx, dy in DIRECTIONS if (at_x and dx == 1) or (at_y and dy == 1)]
            total = more + sum(rows.values()) - sum(rows[direction] for direction in lost)

            @pl.when((edge_x == at_x) & (edge_y == at_y))
            def _():
                wait_rows(total, sem, room)


def couple(here, same, cross, low, high, other, weights, z_step):
    w, w_cross, w_low, w_high, w_below, w_above = weights
    parts = [
        (here + same) * w,
        (here + cross) * w_cross,
        (here + low) * w_low,
        (here + high) * w_high,
        (here + roll(other, z_step)) * w_below,
        (here + roll(other, -z_step)) * w_above,
    ]
    total = ((parts[0] + parts[1]) + (parts[2] + parts[3])) + ((parts[4] + parts[5]) + 1.0)
    inverse = 1.0 / total
    return [part * inverse for part in parts], total, inverse


def relax(source, couplings, same, cross, low, high, z_step):
    acc0 = source + couplings[0] * same
    acc1 = couplings[4] * roll(same, z_step) + couplings[5] * roll(same, -z_step)
    acc2 = couplings[2] * low + couplings[3] * high
    return (acc0 + acc2) + (acc1 + couplings[1] * cross)


def kernel(
    image, conduct, out,
    image_in, conduct_in, kx, vx, vs, vk, c0, s0, d0, t0, p0,
    k1, s1x, v1, vk1, c1, s1, i1, d1, t1, p1,
    q1, own2, kg, sg, v2, c2, s2, i2, d2, t2, p2,
    k3, v3, c3, s3, i3, dummy,
    sent, arrived, in_sems, known_sems,
):
    gx, gy = lax.axis_index("gx"), lax.axis_index("gy")
    chip_x, core = gx // 2, lax.rem(gx, 2)
    chip_z, chip_y = gy // 4, lax.rem(gy, 4)
    sibling = (chip_x * 2 + 1 - core, gy)
    chips = [
        (lax.rem(chip_x + x, 4) * 2 + core, lax.rem(chip_z + z, 4) * 4 + lax.rem(chip_y + y, 4))
        for x, y, z in CHIPS
    ]
    position = (gx, gy)

    barrier = pltpu.get_barrier_semaphore()

    fetch_k = pltpu.make_async_copy(conduct, conduct_in, in_sems.at[0])
    fetch_v = pltpu.make_async_copy(image, image_in, in_sems.at[1])
    fetch_k.start()
    fetch_v.start()

    def near(steps):
        offsets = sorted({(x % GX, y % GY) for x in steps for y in steps} - {(0, 0)}, key=nearness)
        return [(lax.rem(gx + x, GX), lax.rem(gy + y, GY)) for x, y in offsets]

    def tell(n):
        for peer in near((0, 2 << n, -2 << n)):
            pl.semaphore_signal(known_sems.at[n], inc=1, device_id=peer, device_id_type=MESH)

    def hear(n):
        pl.semaphore_wait(known_sems.at[n], len(near((0, 2 << n, -2 << n))))

    greeted = near(range(-2, 3)) + [(lax.rem(gx + 4, GX), gy)]
    for peer in greeted:
        pl.semaphore_signal(barrier, inc=1, device_id=peer, device_id_type=MESH)

    lane0 = iota((16, 128), 1)
    odd_row = iota((16, 128), 0) & 1
    low0 = lane0 < 64
    half_lane = (lane0 & 63) * 2

    def split(values, par):
        parity = odd_row ^ par
        first = half_lane + jnp.where(low0, parity, 1 - parity)
        second = half_lane + jnp.where(low0, 1 - parity, parity)
        left = jnp.take_along_axis(values[:, :128], first, axis=1)
        right = jnp.take_along_axis(values[:, 128:], second, axis=1)
        return jnp.where(low0, left, right), roll(jnp.where(low0, right, left), 64)

    nothing = jnp.zeros((2, 4, 4, 8, 128), F32)
    kg[:, :, :, 0:8], kg[:, :, :, 40:48] = nothing, nothing
    nothing = jnp.zeros((2, 20, 8, 128), F32)
    v2[:, :, 0:8], v2[:, :, 40:48] = nothing, nothing
    nothing = jnp.zeros((2, 2, 48, 128), F32)
    v2[:, 0:2], v2[:, 18:20] = nothing, nothing
    nothing = jnp.zeros((2, 4, 8, 128), F32)
    for ref in (k3, v3):
        ref[:, :, 0:8], ref[:, :, 24:32] = nothing, nothing

    def zero(ref, *at):
        at = (slice(None),) * (len(ref.shape) - 3) + at
        ref[at] = jnp.zeros(ref.at[at].shape, F32)

    for edge, rows0, rows1 in ((gx == 0, slice(0, 5), slice(0, 4)), (gx == GX - 1, slice(21, 26), slice(8, 12))):

        @pl.when(edge)
        def _():
            for ref in (kx, vx, vk):
                zero(ref, rows0)
            for ref in (k1, s1x, vk1):
                zero(ref, rows1)

    for edge, cols0, cols1 in ((gy == 0, slice(0, 8), slice(8, 16)), (gy == GY - 1, slice(24, 32), slice(24, 32))):

        @pl.when(edge)
        def _():
            for ref in (kx, vx, vk):
                zero(ref, slice(None), cols0)
            for ref in (k1, s1x, vk1):
                zero(ref, slice(None), cols1)

    for i in range(16):
        if i == 0:
            fetch_k.wait()
        kx[0, i + 5, 8:24], kx[1, i + 5, 8:24] = split(conduct_in[i], i & 1)

    pl.semaphore_wait(barrier, len(greeted))
    def halos(src, src_origin, dst, origin, extent, which, *cones):
        sems = (sent.at[0], arrived.at[which])
        each = [
            halo_copies(src, src_origin, dst, origin, extent, widths, sems, position, corners, colour)
            for colour, widths, corners in cones
        ]
        return [(ways[0][0], sum((group for _, group in ways), [])) for ways in zip(*each)]

    cones = (1, (5, 5), [(0, 2, 4), (2, 4, 2)]), (0, (4, 4), [(0, 1, 3), (1, 3, 2)])
    send_k = halos(kx, (5, 8), kx, (5, 8), (16, 16), 0, *cones)
    send_v = halos(vs, (0, 0), vx, (5, 8), (16, 16), 1, *cones)
    tell(0)
    halo_start(send_k)
    fetch_v.wait()
    for i in range(16):
        red, black = split(image_in[i], i & 1)
        vx[0, i + 5, 8:24], vx[1, i + 5, 8:24] = red, black
        vs[0, i], vs[1, i] = red, black
    halo_start(send_v)

    def block_mean():
        return [0.125 * (t0[i, pl.ds(0, 8, stride=2)] + t0[i, pl.ds(1, 8, stride=2)]) for i in range(8)]

    odd_8 = ((iota((8, 128), 0) + iota((8, 128), 1)) & 1) == 1
    odd_2 = ((iota((2, 128), 0) + iota((2, 128), 1)) & 1) == 1
    low_2 = iota((2, 128), 1) < 64
    even_lane = (iota((8, 128), 1) & 63) * 2

    def merge(first, second, odd):
        return jnp.where(odd, second, first), jnp.where(odd, first, second)

    def level_2_share(kind, pairs, whole):
        rows = []
        for i in range(4):
            t1[i] = jnp.take_along_axis(pairs[i], even_lane, axis=1) + jnp.take_along_axis(pairs[i], even_lane + 1, axis=1)
        for i in range(4):
            first = t1[i, pl.ds(0, 2, stride=2)] + t1[i, pl.ds(1, 2, stride=2)]
            second = t1[i, pl.ds(4, 2, stride=2)] + t1[i, pl.ds(5, 2, stride=2)]
            rows.append(0.125 * jnp.where(low_2, first, second))
        for a in range(2):
            cells = merge(rows[2 * a], rows[2 * a + 1], odd_2)
            for colour in (0, 1):
                own2[kind, colour, a] = cells[colour]
                whole[colour, chip_x, 2 * core + a, pl.ds(8 + 2 * gy, 2)] = cells[colour]

    def remote(src, dst, which, device):
        return pltpu.make_async_remote_copy(
            src_ref=src, dst_ref=dst, send_sem=sent.at[int(9 <= which <= 13)], recv_sem=arrived.at[which], device_id=device, device_id_type=MESH
        )

    cores_rows = pl.ds(2 * core, 2)
    own_place = (slice(None), chip_x, cores_rows, pl.ds(8 + 2 * gy, 2))

    spread_s = [
        remote(own2.at[1], sg.at[own_place], 9 + x, chip) for chip, (x, _, _) in zip(chips, CHIPS)
    ]
    planes = [sg.at[:, lax.rem(chip_x + 4 - x, 4), cores_rows, 8:40] for x in range(4)]
    share_s = [remote(plane, plane, 13, sibling) for plane in planes]

    def arrive(copies, which):
        wait_rows(rows_of(copies), arrived.at[which], dummy)

    def chip_at(x, y, z):
        return (
            lax.rem(chip_x + x, 4) * 2 + core,
            lax.rem(chip_z + z, 4) * 4 + lax.rem(chip_y + y, 4),
        )

    row = kg.at[:, :, cores_rows, pl.ds(8 + 2 * gy, 2)]
    sheet = kg.at[:, :, cores_rows, pl.ds(8 + 8 * chip_z, 8)]
    half = kg.at[:, :, cores_rows, 8:40]
    tree_x = [remote(own2.at[0], kg.at[own_place], 6, chip_at(n, 0, 0)) for n in (2, 1, 3)]
    tree_y = [remote(row, row, 7, chip_at(0, n, 0)) for n in (2, 1, 3)]
    tree_z = [remote(sheet, sheet, 14, chip_at(0, 0, n)) for n in (2, 1, 3)]
    tree_core = [remote(half, half, 8, sibling)]

    for i in range(8):
        e = 2 * i + 5
        t0[i] = (kx[0, e, 8:24] + kx[1, e, 8:24]) + (kx[0, e + 1, 8:24] + kx[1, e + 1, 8:24])
    rows = block_mean()
    for a in range(4):
        k1[0, a + 4, 16:24], k1[1, a + 4, 16:24] = merge(rows[2 * a], rows[2 * a + 1], odd_8)
    level_2_share(0, [rows[2 * a] + rows[2 * a + 1] for a in range(4)], kg)
    send_k1 = halos(k1, (4, 16), k1, (4, 16), (4, 8), 2, (0, (3, 5), [(0, 1, 5), (1, 3, 3)]), (1, (3, 6), [(0, 1, 6), (1, 3, 4)]))
    halo_start(send_k1)

    shape = (2, 24, 128)
    sub, lanes = iota(shape, 1), iota(shape, 2)
    even_row = ((iota(shape, 0) + sub) & 1) == 0
    wy_low = jnp.where((sub == 4) & (gy == 0), 0.0, 0.5).astype(F32)
    wy_high = jnp.where((sub == 19) & (gy == GY - 1), 0.0, 0.5).astype(F32)
    wx_low = jnp.where(gx == 0, 0.0, 0.5).astype(F32)
    wx_high = jnp.where(gx == GX - 1, 0.0, 0.5).astype(F32)
    wz = [
        jnp.where(even_row, jnp.where(lanes == 0, 0.0, 0.5), jnp.where(lanes == 127, 0.0, 0.5)).astype(F32),
        jnp.where(even_row, jnp.where(lanes == 127, 0.0, 0.5), jnp.where(lanes == 0, 0.0, 0.5)).astype(F32),
    ]

    def beside(values, colour, even):
        step = 1 if colour == 0 else -1
        first = roll(jnp.where(even, values[0], values[1]), step)
        second = roll(jnp.where(even, values[1], values[0]), -step)
        return jnp.stack([jnp.where(even, first, second), jnp.where(even, second, first)])

    even_24 = (iota((24, 128), 0) & 1) == 0
    even_16 = (iota((16, 128), 0) & 1) == 0

    row_index = iota((2, 1, 1), 0)

    def couplings_0(colour, start, stop):
        for i in range(start, stop, 2):
            e = i + 5
            here, other = kx[colour, e:e + 2, 4:28], kx[1 - colour, e:e + 2, 4:28]
            wx_l = jnp.where(row_index == 0, wx_low, 0.5) if i == 0 else 0.5
            wx_h = jnp.where(row_index == 1, wx_high, 0.5) if i == 14 else 0.5
            parts = [
                (here + kx[1 - colour, e - 1:e + 1, 4:28]) * wx_l,
                (here + kx[1 - colour, e + 1:e + 3, 4:28]) * wx_h,
                (here + kx[1 - colour, e:e + 2, 3:27]) * wy_low,
                (here + kx[1 - colour, e:e + 2, 5:29]) * wy_high,
                (here + other) * 0.5,
                (here + beside(other, colour, even_24)) * wz[colour],
            ]
            total = ((parts[0] + parts[1]) + (parts[2] + parts[3])) + ((parts[4] + parts[5]) + 1.0)
            inverse = 1.0 / total
            d0[colour, i + 4:i + 6] = total
            s0[colour, i + 4:i + 6] = inverse
            for n in range(6):
                c0[colour, n, i + 4:i + 6] = parts[n] * inverse

    def update_0(colour, i, lo, hi, rows_even):
        e, f = i + 5, i + 4
        a, b = lo + 8, hi + 8
        here = slice(lo + 4, hi + 4)
        other = vx[1 - colour, e:e + 2, a:b]
        acc0 = s0[colour, f:f + 2, here] + c0[colour, 0, f:f + 2, here] * vx[1 - colour, e - 1:e + 1, a:b]
        acc1 = c0[colour, 1, f:f + 2, here] * vx[1 - colour, e + 1:e + 3, a:b]
        acc1 += c0[colour, 2, f:f + 2, here] * vx[1 - colour, e:e + 2, a - 1:b - 1]
        acc2 = c0[colour, 3, f:f + 2, here] * vx[1 - colour, e:e + 2, a + 1:b + 1]
        acc2 += c0[colour, 4, f:f + 2, here] * other
        acc3 = c0[colour, 5, f:f + 2, here] * beside(other, colour, rows_even)
        return (acc0 + acc1) + (acc2 + acc3)

    def half_sweep_0(colour, start, stop, lo=-4, hi=20):
        rows_even = even_24 if hi - lo == 24 else even_16
        for i in range(start, stop, 2):
            vx[colour, i + 5:i + 7, lo + 8:hi + 8] = update_0(colour, i, lo, hi, rows_even)

    for copy in tree_x:
        copy.start()
    halo_wait([send_k], position, arrived.at[0], dummy)
    couplings_0(0, -4, 20)
    couplings_0(1, -4, 20)
    hear(0)
    tell(1)
    arrive(tree_x, 6)
    for copy in tree_y:
        copy.start()
    halo_wait([send_v], position, arrived.at[1], dummy)
    for colour in (0, 1):
        for i in range(-4, 20, 2):
            s0[colour, i + 4:i + 6] = s0[colour, i + 4:i + 6] * vx[colour, i + 5:i + 7, 4:28]

    half_sweep_0(0, -4, 20)
    half_sweep_0(1, -4, 20)
    half_sweep_0(0, -2, 18)
    half_sweep_0(1, -2, 18)

    def residual_0(i):
        total = None
        for colour in (0, 1):
            left = update_0(colour, i, 0, 16, even_16) - vx[colour, i + 5:i + 7, 8:24]
            left = d0[colour, i + 4:i + 6, 4:20] * left
            total = left if total is None else total + left
        return total

    for i in range(8):
        both = residual_0(2 * i)
        t0[i] = both[0] + both[1]
    rows = block_mean()
    for a in range(4):
        s1x[0, a + 4, 16:24], s1x[1, a + 4, 16:24] = merge(rows[2 * a], rows[2 * a + 1], odd_8)
    send_s1 = halos(s1x, (4, 16), s1x, (4, 16), (4, 8), 3, (0, (3, 5), None), (1, (2, 4), None))
    halo_start(send_s1)


    shape = (24, 128)
    col, lanes = iota(shape, 0) - 6, iota(shape, 1)
    w1 = 0.5 / 4.0
    wy_low = jnp.where((col == 0) & (gy == 0), 0.0, w1).astype(F32)
    wy_high = jnp.where((col == 7) & (gy == GY - 1), 0.0, w1).astype(F32)
    wx_low = jnp.where(gx == 0, 0.0, w1).astype(F32)
    wx_high = jnp.where(gx == GX - 1, 0.0, w1).astype(F32)
    wz_low = jnp.where(lanes == 0, 0.0, w1).astype(F32)
    wz_high = jnp.where(lanes == 127, 0.0, w1).astype(F32)

    def first_of_pair(size, origin):
        odd = (iota((size, 128), 0) + iota((size, 128), 1) + origin) & 1
        return odd == 0, odd == 1

    first_24, first_16, first_8 = first_of_pair(24, 0), first_of_pair(16, 0), first_of_pair(8, 0)

    halo_wait([send_k1], position, arrived.at[2], dummy)
    for colour in (0, 1):
        for a in range(-3, 7):
            e, f = a + 4, a + 3
            other = k1[1 - colour, e, 10:34]
            first = first_24[colour]
            w_cross = w1
            if a in (0, 3):
                w_cross = jnp.where(first, wx_low if a == 0 else w1, wx_high if a == 3 else w1)
            parts, total, inverse = couple(
                k1[colour, e, 10:34], other, jnp.where(first, k1[1 - colour, e - 1, 10:34], k1[1 - colour, e + 1, 10:34]),
                k1[1 - colour, e, 9:33], k1[1 - colour, e, 11:35], other, (w1, w_cross, wy_low, wy_high, wz_low, wz_high), 1,
            )
            d1[colour, f] = total
            i1[colour, f] = inverse
            for n in range(6):
                c1[colour, n, f] = parts[n]

    def update_1(colour, a, lo, hi):
        e, f = a + 4, a + 3
        here, at = slice(lo + 6, hi + 6), slice(lo + 16, hi + 16)
        first = {24: first_24, 16: first_16, 8: first_8}[hi - lo][colour]
        return relax(
            s1[colour, f, here], [c1[colour, n, f, here] for n in range(6)], v1[1 - colour, e, at],
            jnp.where(first, v1[1 - colour, e - 1, at], v1[1 - colour, e + 1, at]),
            v1[1 - colour, e, lo + 15:hi + 15], v1[1 - colour, e, lo + 17:hi + 17], 1,
        )

    def half_sweep_1(colour, start, stop, lo, hi):
        for a in range(start, stop):
            v1[colour, a + 4, lo + 16:hi + 16] = update_1(colour, a, lo, hi)

    hear(1)
    arrive(tree_y, 7)
    for copy in tree_z:
        copy.start()

    vk[5:21, 8:24] = vx[1, 5:21, 8:24]
    send_vk = halos(vk, (5, 8), vk, (5, 8), (16, 16), 4, (None, (4, 4), None))
    halo_start(send_vk)
    halo_wait([send_s1], position, arrived.at[3], dummy)
    for colour in (0, 1):
        for a in range(-3, 7):
            s1[colour, a + 3] = i1[colour, a + 3] * s1x[colour, a + 4, 10:34]
    for a in range(-2, 6):
        v1[0, a + 4, 12:28] = s1[0, a + 3, 2:18]
    half_sweep_1(1, -2, 6, -4, 12)
    half_sweep_1(0, -1, 5, -4, 12)
    half_sweep_1(1, -1, 5, -4, 12)
    pairs = []
    for a in range(4):
        left = [d1[n, a + 3, 6:14] * (update_1(n, a, 0, 8) - v1[n, a + 4, 16:24]) for n in (0, 1)]
        pairs.append(left[0] + left[1])
    level_2_share(1, pairs, sg)
    for copy in spread_s:
        copy.start()
    arrive(tree_z, 14)
    tree_core[0].start()
    vk1[4:8, 16:24] = v1[1, 4:8, 16:24]
    send_vk1 = halos(vk1, (4, 16), vk1, (4, 16), (4, 8), 5, (None, (3, 6), None))
    halo_start(send_vk1)

    arrive(tree_core, 8)
    def two_columns(size):
        return iota((size, 128), 1) < 64, (iota((size, 128), 0) & 1) == 1

    def beside_2(row_low, row_high, low, odd):
        turned = roll(jnp.where(low, row_high, row_low), 64)
        return jnp.where(odd, row_low, turned), jnp.where(odd, turned, row_high)

    lane = iota((32, 128), 1)
    place = lane & 63
    j_row = iota((32, 128), 0)
    low_32, odd_32 = two_columns(32)
    first_32 = first_of_pair(32, 0)
    w2 = 0.5 / 16.0
    wy_low = jnp.where((j_row == 0) & low_32, 0.0, w2).astype(F32)
    wy_high = jnp.where((j_row == 31) & (lane >= 64), 0.0, w2).astype(F32)
    wz_low = jnp.where(place == 0, 0.0, w2).astype(F32)
    wz_high = jnp.where(place == 63, 0.0, w2).astype(F32)

    def kg_rows(colour, a, at):
        return kg[colour, a // 4, a % 4, at]

    at = slice(8, 40)
    for colour in (0, 1):
        for a in range(16):
            other = kg_rows(1 - colour, a, at)
            before = kg_rows(1 - colour, max(a - 1, 0), at)
            after = kg_rows(1 - colour, min(a + 1, 15), at)
            w_cross = w2
            if a == 0:
                w_cross = jnp.where(first_32[colour], 0.0, w2).astype(F32)
            if a == 15:
                w_cross = jnp.where(first_32[colour], w2, 0.0).astype(F32)
            low, high = beside_2(
                kg_rows(1 - colour, a, slice(7, 39)), kg_rows(1 - colour, a, slice(9, 41)), low_32, odd_32
            )
            parts, total, inverse = couple(
                kg_rows(colour, a, at), other, jnp.where(first_32[colour], before, after), low, high, other,
                (w2, w_cross, wy_low, wy_high, wz_low, wz_high), 1,
            )
            d2[colour, a] = total
            i2[colour, a] = inverse
            for n in range(6):
                c2[colour, n, a] = parts[n]

    lane3 = iota((16, 128), 1)
    even_place = (lane3 & 1) == 0
    place3 = (lane3 & 63) >> 1
    row3 = iota((16, 128), 0)
    low3 = lane3 < 64
    odd3 = (((lane3 >> 6) + place3) & 1) == 1
    first3 = (jnp.logical_not(odd3), odd3)

    lower = even_place

    def level_3_share(p):
        rows = []
        for n in (2 * p, 2 * p + 1):
            both = []
            for a in (n, n + 8):
                row = t2[a, pl.ds(0, 16, stride=2)] + t2[a, pl.ds(1, 16, stride=2)]
                both.append(row + jnp.where(even_place, roll(row, -1), roll(row, 1)))
            rows.append(0.125 * jnp.where(lower, both[0], both[1]))
        return merge(rows[0], rows[1], odd3)

    w3 = 0.5 / 64.0
    wy_low = jnp.where((row3 == 0) & low3, 0.0, w3).astype(F32)
    wy_high = jnp.where((row3 == 15) & (lane3 >= 64), 0.0, w3).astype(F32)
    wz_low = jnp.where(place3 == 0, 0.0, w3).astype(F32)
    wz_high = jnp.where(place3 == 31, 0.0, w3).astype(F32)
    at3 = slice(8, 24)

    def around_3(ref, colour, p, first):
        here = ref[colour, p, at3]
        before = ref[colour, p - 1, at3] if p else roll(ref[colour, 3, at3], 1)
        after = ref[colour, p + 1, at3] if p < 3 else roll(ref[colour, 0, at3], -1)
        low = roll(jnp.where(low3, here, ref[colour, p, 7:23]), 64)
        high = roll(jnp.where(low3, ref[colour, p, 9:25], here), 64)
        return here, jnp.where(first, before, after), low, high

    for a in range(16):
        t2[a] = kg_rows(0, a, at) + kg_rows(1, a, at)
    for p in range(4):
        k3[0, p, at3], k3[1, p, at3] = level_3_share(p)
    for colour in (0, 1):
        for p in range(4):
            here, cross, low, high = around_3(k3, 1 - colour, p, first3[colour])
            w_cross = w3
            if p == 0:
                w_cross = jnp.where(first3[colour] & lower, 0.0, w3).astype(F32)
            if p == 3:
                w_cross = jnp.where(first3[colour] | lower, w3, 0.0).astype(F32)
            parts, _, inverse = couple(
                k3[colour, p, at3], here, cross, low, high, here, (w3, w_cross, wy_low, wy_high, wz_low, wz_high), 2
            )
            i3[colour, p] = inverse
            for n in range(6):
                c3[colour, n, p] = parts[n]

    for x in (0, 1, 3, 2):
        arrive([copy for copy, chip in zip(spread_s, CHIPS) if chip[0] == x], 9 + x)
        share_s[x].start()
    arrive(share_s, 13)

    for colour in (0, 1):
        for a in range(16):
            source = i2[colour, a] * sg[colour, a // 4, a % 4, at]
            s2[colour, a] = source
            if colour == 0:
                v2[0, a + 2, at] = source

    def update_2(colour, a, rows, frame_rows, low, odd, first):
        before, here, after = frame_rows
        row_low, row_high = beside_2(v2[1 - colour, a + 2, before], v2[1 - colour, a + 2, after], low, odd)
        cross = jnp.where(first[colour], v2[1 - colour, a + 1, here], v2[1 - colour, a + 3, here])
        return relax(
            s2[colour, a, rows], [c2[colour, n, a, rows] for n in range(6)], v2[1 - colour, a + 2, here],
            cross, row_low, row_high, 1,
        )

    whole_2 = (slice(0, 32), (slice(7, 39), at, slice(9, 41)), low_32, odd_32, first_32)

    def half_sweep_2(colour):
        for a in range(16):
            v2[colour, a + 2, at] = update_2(colour, a, *whole_2)

    half_sweep_2(1)
    half_sweep_2(0)
    half_sweep_2(1)
    for a in range(16):
        left = [d2[n, a] * (update_2(n, a, *whole_2) - v2[n, a + 2, at]) for n in (0, 1)]
        t2[a] = left[0] + left[1]
    for p in range(4):
        sources = level_3_share(p)
        for colour in (0, 1):
            s3[colour, p] = i3[colour, p] * sources[colour]

    def half_sweep_3(colour):
        for p in range(4):
            here, cross, low, high = around_3(v3, 1 - colour, p, first3[colour])
            v3[colour, p, at3] = relax(
                s3[colour, p], [c3[colour, n, p] for n in range(6)], here, cross, low, high, 2
            )

    for p in range(4):
        v3[0, p, at3] = s3[0, p]
    half_sweep_3(1)
    for _ in range(COARSE_SWEEPS - 1):
        half_sweep_3(0)
        half_sweep_3(1)

    for p in range(4):
        cells = [v3[colour, p, at3] for colour in (0, 1)]
        firsts = [jnp.where(lower, c, roll(c, 1)) for c in cells]
        seconds = [jnp.where(lower, roll(c, -1), c) for c in cells]
        for pair, (red, black) in ((p, firsts), (p + 4, seconds)):
            for n, row in enumerate((jnp.where(odd3, black, red), jnp.where(odd3, red, black))):
                p2[2 * pair + n, pl.ds(0, 16, stride=2)] = row
                p2[2 * pair + n, pl.ds(1, 16, stride=2)] = row

    def within(value, top, span):
        value = value * ((value + span) // span)
        value = top - value
        return top - value * ((value + span) // span)

    a0 = 2 * within(gx - 2, 3, 8)
    r0 = 2 * within(gy - 2, 8, 16)
    strip = pl.ds(r0, 16)
    part_2 = (strip, (pl.ds(r0 + 7, 16), pl.ds(r0 + 8, 16), pl.ds(r0 + 9, 16)), *two_columns(16), first_16)
    for n in range(10):
        v2[1, a0 + n + 2, pl.ds(r0 + 8, 16)] = v2[1, a0 + n + 2, pl.ds(r0 + 8, 16)] + p2[a0 + n, strip]
    for colour in (0, 1, 0, 1):
        news = [update_2(colour, a0 + n, *part_2) for n in range(10)]
        for n, new in enumerate(news):
            v2[colour, a0 + n + 2, pl.ds(r0 + 8, 16)] = new

    spot = iota((8, 128), 1) >> 1
    for d in range(-3, 7):
        cells = (2 * gx + d // 2 + 2, pl.ds(2 * gy + 6, 8))
        coarse = jnp.where(odd_8 == (d % 2 == 1), v2[(0,) + cells], v2[(1,) + cells])
        q1[d + 3, 0] = jnp.take_along_axis(coarse, spot, axis=1)
        q1[d + 3, 1] = jnp.take_along_axis(coarse, spot + 64, axis=1)
    for d in range(10):
        for n in range(2):
            for m in range(2):
                column = q1[d, n, pl.ds(m, 4, stride=2)]
                p1[d, pl.ds(4 * n + 2 * m, 4, stride=8)] = column
                p1[d, pl.ds(4 * n + 2 * m + 1, 4, stride=8)] = column
    halo_wait([send_vk1], position, arrived.at[5], dummy)
    for a in range(-3, 7):
        v1[1, a + 4, 10:30] = vk1[a + 4, 10:30] + p1[a + 3, 2:22]
    half_sweep_1(0, -3, 7, -6, 18)
    half_sweep_1(1, -2, 6, -4, 12)
    half_sweep_1(0, -2, 6, -4, 12)
    half_sweep_1(1, -1, 5, -4, 12)

    odd_12 = (iota((12, 128), 0) + iota((12, 128), 1)) & 1
    for i in range(-2, 10):
        a = i // 2
        row = jnp.where(odd_12 == i % 2, v1[0, a + 4, 14:26], v1[1, a + 4, 14:26])
        p0[i + 2, pl.ds(0, 12, stride=2)] = row
        p0[i + 2, pl.ds(1, 12, stride=2)] = row
    halo_wait([send_vk], position, arrived.at[4], dummy)
    for i in range(-4, 20):
        vx[1, i + 5, 4:28] = vk[i + 5, 4:28] + p0[i // 2 + 2]
    half_sweep_0(0, -4, 20)
    half_sweep_0(1, -2, 18)
    half_sweep_0(0, -2, 18)
    for i in range(0, 16, 2):
        out[0, i:i + 2] = vx[0, i + 5:i + 7, 8:24]
        out[1, i:i + 2] = update_0(1, i, 0, 16, even_16)

    halo_wait(
        [send_k, send_v, send_k1, send_s1, send_vk, send_vk1], position, sent.at[0], dummy,
        rows_of(tree_x + tree_y + tree_z + tree_core),
    )
    wait_rows(rows_of(spread_s + share_s), sent.at[1], dummy)


def join(cells, out, rows, sems):
    lane = iota((16, 128), 1)
    odd_row = iota((16, 128), 0) & 1
    low = lane < 64
    half = lane >> 1
    copies = []
    for i in range(16):
        red, turned = cells[0, i], roll(cells[1, i], 64)
        left, right = jnp.where(low, red, turned), jnp.where(low, turned, red)
        same = (lane & 1) == (odd_row ^ (i & 1))
        rows[i, :, :128] = jnp.take_along_axis(left, half + jnp.where(same, 0, 64), axis=1)
        rows[i, :, 128:] = jnp.take_along_axis(right, half + jnp.where(same, 64, 0), axis=1)
        if i % 4 == 3:
            part = pl.ds(i - 3, 4)
            copies.append(pltpu.make_async_copy(rows.at[part], out.at[part], sems.at[i // 4]))
            copies[-1].start()
    for copy in copies:
        copy.wait()


def v_cycle(image, conduct):
    def vmem(*shape):
        return pltpu.VMEM(shape, F32)

    frame0, frame1, gathered = (26, 32, 128), (12, 40, 128), (2, 4, 4, 48, 128)
    cells = pl.pallas_call(
        kernel,
        out_shape=jax.ShapeDtypeStruct((2, 16, 16, 128), F32),
        in_specs=[pl.BlockSpec(memory_space=pltpu.HBM)] * 2,
        out_specs=pl.BlockSpec(memory_space=pltpu.VMEM),
        scratch_shapes=[
            vmem(16, 16, 256), vmem(16, 16, 256),
            vmem(2, *frame0), vmem(2, *frame0), vmem(2, 16, 16, 128), vmem(*frame0), vmem(2, 6, 24, 24, 128),
            vmem(2, 24, 24, 128), vmem(2, 24, 24, 128), vmem(8, 16, 128), vmem(12, 24, 128),
            vmem(2, *frame1), vmem(2, *frame1), vmem(2, *frame1), vmem(*frame1), vmem(2, 6, 10, 24, 128),
            vmem(2, 10, 24, 128), vmem(2, 10, 24, 128), vmem(2, 10, 24, 128), vmem(4, 8, 128), vmem(10, 32, 128),
            vmem(10, 2, 8, 128), vmem(2, 2, 2, 2, 128), vmem(*gathered), vmem(*gathered), vmem(2, 20, 48, 128),
            vmem(2, 6, 16, 32, 128), vmem(2, 16, 32, 128), vmem(2, 16, 32, 128), vmem(2, 16, 32, 128), vmem(16, 32, 128),
            vmem(16, 32, 128),
            vmem(2, 4, 32, 128), vmem(2, 4, 32, 128), vmem(2, 6, 4, 16, 128), vmem(2, 4, 16, 128),
            vmem(2, 4, 16, 128), vmem(4096, 128),
            pltpu.SemaphoreType.DMA((2,)), pltpu.SemaphoreType.DMA((15,)), pltpu.SemaphoreType.DMA((2,)),
            pltpu.SemaphoreType.REGULAR((2,)),
        ],
        compiler_params=pltpu.CompilerParams(
            collective_id=0, has_side_effects=True, vmem_limit_bytes=48 * 2**20
        ),
        name="v_cycle",
    )(*(pltpu.with_memory_space_constraint(array, pltpu.HBM) for array in (image, conduct)))
    return pl.pallas_call(
        join,
        out_shape=jax.ShapeDtypeStruct((16, 16, 256), F32),
        in_specs=[pl.BlockSpec(memory_space=pltpu.VMEM)],
        out_specs=pl.BlockSpec(memory_space=pltpu.HBM),
        scratch_shapes=[vmem(16, 16, 256), pltpu.SemaphoreType.DMA((4,))],
        compiler_params=pltpu.CompilerParams(vmem_limit_bytes=8 * 2**20),
        name="join",
    )(cells)


def solution(mesh):
    return jax.shard_map(
        v_cycle,
        mesh=mesh,
        in_specs=(P("gx", "gy", None), P("gx", "gy", None)),
        out_specs=P("gx", "gy", None),
        check_vma=False,
    )
```
